512 devices in a mesh: crop: 8 (over x, core), dap: 64 (over y, z).
Axes of the slice: x: 4, y: 4, z: 16, core: 2. Of those that a mesh axis runs over, the one named last changes fastest.
Arguments:
- sequence_stack: bfloat16 [8, 64, 256, 256], P('crop', None, 'dap'), may hold values from -65 to 65
- upstream_derivative: bfloat16 [8, 64, 256, 256], P('crop', None, 'dap'), may hold values from -6 to 6
- coupling_logits: bfloat16 [8, 8, 256, 256], P('crop', None, 'dap'), may hold values from -6 to 300
- piece_extents: int32 [8], P('crop'), may hold values from 64 to 256, as said below
- projection_matrices: bfloat16 [4, 256, 256], replicated, may hold values from -0.375 to 0.375
- final_projection_matrix: bfloat16 [256, 256], replicated, may hold values from -0.375 to 0.375
- norm_multiplier: float32 [256], replicated, may hold values from 0.1 to 1.9
Outputs:
- sequence_stack_derivative: bfloat16 [8, 64, 256, 256], P('crop', None, 'dap')
- coupling_logit_derivative: float32 [8, 8, 256, 256], P('crop', None, 'dap')
- d_w_in: float32 [4, 256, 256], replicated
- d_w_out: float32 [256, 256], replicated
- d_gain: float32 [256], replicated
The draws below stay inside these ranges and needn't reach their ends.
Inputs may be any that keep to these rules, and one draw needn't show every extreme that they name: `piece_extents`: in every draw one crop has 256 residues; every crop has 64 or more.
All inputs are finite; a program needn't handle non-finite values.
Results may differ from the reference program's by a relative error of at most 0.01.
Values may be sent and summed in bfloat16 or wider, within the bound.
A program may use at most 64 MiB of HBM per device.

```python
import math
import jax
import jax.numpy as jnp
from jax import lax

FEATURE_DEPTH = 256
H = 8
POSITION_SLOTS = 256
SEQUENCE_NUMBER = 64
HD = 256
PROTEIN_PIECES = 8


def draw_piece_extents(key, part):
    key = jax.random.fold_in(key, 11)
    first_key, random_seed_two = jax.random.split(key)
    base = jax.random.randint(first_key, (PROTEIN_PIECES,), POSITION_SLOTS // 4, POSITION_SLOTS + 1)
    full_place = jax.random.randint(random_seed_two, (), 0, PROTEIN_PIECES)
    places = jnp.arange(PROTEIN_PIECES)
    base = jnp.where(places == full_place, POSITION_SLOTS, base)
    return base.astype(jnp.int32)


def draw_coupling_logits(key, part):
    key = jax.random.fold_in(key, 23)
    tensor_dimensions = (PROTEIN_PIECES, H, POSITION_SLOTS, POSITION_SLOTS)
    base = jnp.clip(jax.random.normal(key, tensor_dimensions, jnp.float32), -6.0, 6.0)
    return base.astype(jnp.bfloat16)


def draw_sequence_stack(key, part):
    key = jax.random.fold_in(key, 37)
    first_key, random_seed_two, random_seed_three = jax.random.split(key, 3)
    tensor_dimensions = (PROTEIN_PIECES, SEQUENCE_NUMBER, POSITION_SLOTS, FEATURE_DEPTH)
    multipliers = jnp.exp(jax.random.uniform(random_seed_two, (PROTEIN_PIECES, SEQUENCE_NUMBER, POSITION_SLOTS, 1), jnp.float32, 0.0, math.log(10.0)))
    displacements = jnp.clip(jax.random.normal(random_seed_three, (PROTEIN_PIECES, SEQUENCE_NUMBER, POSITION_SLOTS, 1), jnp.float32), -3.0, 3.0) * 0.5
    noise = jnp.clip(jax.random.normal(first_key, tensor_dimensions, jnp.float32), -5.0, 5.0)
    value_floats = (noise + displacements) * multipliers
    return value_floats.astype(jnp.bfloat16)


def block_levels(own_key, dims, pieces, least, high):
    level, own = 1.0, jax.random.fold_in(own_key, 6)
    for dim, shards_of in pieces:
        draws = jnp.exp(jax.random.uniform(jax.random.fold_in(own, dim), (shards_of,), jnp.float32, least / len(pieces), high / len(pieces)))
        level = level * jnp.repeat(draws, dims[dim] // shards_of).reshape([-1 if axis == dim else 1 for axis in range(len(dims))])
    return level


def normal_values(key, extent, deviation, most, cuts=(), kind=jnp.bfloat16):
    array = deviation * jax.random.normal(key, extent, jnp.float32)
    if cuts:
        array = array * block_levels(key, extent, cuts, -0.22, 0.18)
    return jnp.clip(array, -most, most).astype(kind)


def setup_inputs(seed: int = 0) -> dict:
    splits = jax.random.split(jax.random.key(seed), 8)
    sequence_stack = draw_sequence_stack(jax.random.fold_in(splits[7], 71), 0)
    upstream_derivative = normal_values(splits[1], (PROTEIN_PIECES, SEQUENCE_NUMBER, POSITION_SLOTS, FEATURE_DEPTH), 1.0, 6.0, ((0, 8), (2, 64)))
    coupling_logits = draw_coupling_logits(jax.random.fold_in(splits[7], 71), 0)
    piece_extents = draw_piece_extents(jax.random.fold_in(splits[7], 71), 0)
    projection_matrices = normal_values(splits[4], (4, FEATURE_DEPTH, HD), FEATURE_DEPTH ** -0.5, 0.375)
    final_projection_matrix = normal_values(splits[5], (HD, FEATURE_DEPTH), HD ** -0.5, 0.375)
    norm_multiplier = jnp.clip(1.0 + 0.18 * jax.random.normal(splits[6], (FEATURE_DEPTH,), jnp.float32), 0.1, 1.9)
    return dict(sequence_stack=sequence_stack, upstream_derivative=upstream_derivative, coupling_logits=coupling_logits, piece_extents=piece_extents, projection_matrices=projection_matrices, final_projection_matrix=final_projection_matrix, norm_multiplier=norm_multiplier)


EPSILON = 1e-05
MASKED = -1000000000.0

def product(form, left, right):
    return jnp.einsum(form, left.astype(jnp.float32), right.astype(jnp.float32), precision=lax.Precision.HIGHEST)

def crop_gradient_list(alignment_rows, gradient_row_list, head_bias, crop_length, projection_matrices, final_projection_matrix, norm_multiplier):
    heads = head_bias.shape[0]
    residue_count = alignment_rows.shape[1]
    channel_width = alignment_rows.shape[2]
    hidden = projection_matrices.shape[2]
    head_size = hidden // heads
    multiplier_amount = 1.0 / math.sqrt(head_size)
    valid = jnp.arange(residue_count, dtype=jnp.int32) < crop_length.astype(jnp.int32)
    valid_rows = valid.astype(jnp.bfloat16)[:, None]
    bias_float = head_bias.astype(jnp.float32)

    def single_row(carry, input_arrays):
        bias_sum, in_sum, out_sum, gain_sum = carry
        alignment_row, gradient_row = input_arrays
        value_floats = alignment_row.astype(jnp.float32)
        centred = value_floats - lax.optimization_barrier(jnp.mean(value_floats, axis=-1, keepdims=True))
        inv_std = lax.rsqrt(lax.optimization_barrier(jnp.mean(centred * centred, axis=-1, keepdims=True)) + EPSILON)
        normal_x = centred * inv_std
        normed = (normal_x * norm_multiplier).astype(jnp.bfloat16)
        projected = [jnp.dot(normed, projection_matrices[proj_index], preferred_element_type=jnp.float32).astype(jnp.bfloat16) for proj_index in range(4)]
        queries = projected[0].reshape(residue_count, heads, head_size)
        keys_h = projected[1].reshape(residue_count, heads, head_size)
        vals_h = projected[2].reshape(residue_count, heads, head_size)
        scores = product('ihd,jhd->hij', queries, keys_h) * multiplier_amount + bias_float
        scores = jnp.where(valid[None, None, :], scores, MASKED)
        highest = lax.optimization_barrier(jnp.max(scores, axis=-1, keepdims=True))
        expo = jnp.exp(scores - highest)
        probs = expo / lax.optimization_barrier(jnp.sum(expo, axis=-1, keepdims=True))
        probs_b = probs.astype(jnp.bfloat16)
        attended = product('hij,jhd->ihd', probs_b, vals_h).reshape(residue_count, hidden)
        gate_f = jax.nn.sigmoid(projected[3].astype(jnp.float32))
        gated = (attended * gate_f).astype(jnp.bfloat16)
        masked_grad = gradient_row * valid_rows
        d_gated = jnp.dot(masked_grad, final_projection_matrix.T, preferred_element_type=jnp.float32)
        d_att = (d_gated * gate_f).astype(jnp.bfloat16)
        d_gate = (d_gated * attended * gate_f * (1.0 - gate_f)).astype(jnp.bfloat16)
        d_att_h = d_att.reshape(residue_count, heads, head_size)
        d_probs = product('ihd,jhd->hij', d_att_h, vals_h)
        d_vals = product('hij,ihd->jhd', probs_b, d_att_h).astype(jnp.bfloat16)
        row_total = lax.optimization_barrier(jnp.sum(probs * d_probs, axis=-1, keepdims=True))
        d_scores = probs * (d_probs - row_total)
        d_scores_b = d_scores.astype(jnp.bfloat16)
        d_queries = (product('hij,jhd->ihd', d_scores_b, keys_h) * multiplier_amount).astype(jnp.bfloat16)
        d_keys = (product('hij,ihd->jhd', d_scores_b, queries) * multiplier_amount).astype(jnp.bfloat16)
        grads = [d_queries.reshape(residue_count, hidden), d_keys.reshape(residue_count, hidden), d_vals.reshape(residue_count, hidden), d_gate]
        d_normed = jnp.zeros((residue_count, channel_width), jnp.float32)
        in_terms = []
        for proj_index in range(4):
            d_normed = d_normed + jnp.dot(grads[proj_index], projection_matrices[proj_index].T, preferred_element_type=jnp.float32)
            in_terms.append(jnp.dot(normed.T, grads[proj_index], preferred_element_type=jnp.float32))
        out_term = jnp.dot(gated.T, masked_grad, preferred_element_type=jnp.float32)
        scaled = d_normed * norm_multiplier
        d_row = inv_std * (scaled - lax.optimization_barrier(jnp.mean(scaled, axis=-1, keepdims=True)) - normal_x * lax.optimization_barrier(jnp.mean(scaled * normal_x, axis=-1, keepdims=True)))
        new_carry = (bias_sum + d_scores, in_sum + jnp.stack(in_terms), out_sum + out_term, gain_sum + lax.optimization_barrier(jnp.sum(d_normed * normal_x, axis=0)))
        return (new_carry, d_row.astype(jnp.bfloat16))
    crop_offset = (jnp.zeros(head_bias.shape, jnp.float32), jnp.zeros(projection_matrices.shape, jnp.float32), jnp.zeros(final_projection_matrix.shape, jnp.float32), jnp.zeros((channel_width,), jnp.float32))
    gradient_totals, row_gradients = lax.scan(single_row, crop_offset, (alignment_rows, gradient_row_list))
    return (row_gradients, gradient_totals[0], gradient_totals[1], gradient_totals[2], gradient_totals[3])

def reference(sequence_stack, upstream_derivative, coupling_logits, piece_extents, projection_matrices, final_projection_matrix, norm_multiplier):

    def piece_outcomes(items):
        return crop_gradient_list(items[0], items[1], items[2], items[3], projection_matrices, final_projection_matrix, norm_multiplier)
    sequence_stack_derivative, coupling_logit_derivative, projection_matrices_accumulated, final_projection_accumulated, sigmoid_matrix_accumulated = lax.map(piece_outcomes, (sequence_stack, upstream_derivative, coupling_logits, piece_extents))
    multiplier_amount = 1.0 / (PROTEIN_PIECES * SEQUENCE_NUMBER)
    return (sequence_stack_derivative, coupling_logit_derivative, lax.optimization_barrier(jnp.sum(projection_matrices_accumulated, axis=0)) * multiplier_amount, lax.optimization_barrier(jnp.sum(final_projection_accumulated, axis=0)) * multiplier_amount, lax.optimization_barrier(jnp.sum(sigmoid_matrix_accumulated, axis=0)) * multiplier_amount)
```

```python
import functools
import math

import jax
import jax.numpy as jnp
from jax import lax
from jax.experimental import pallas as pl
from jax.experimental.pallas import tpu as pltpu
from jax.sharding import PartitionSpec as P

EPSILON = 1e-05
MASKED = -1000000000.0
LANES = 128
BF = jnp.bfloat16
F32 = jnp.float32
VMEM = pl.BlockSpec(memory_space=pltpu.VMEM)
SMEM = pl.BlockSpec(memory_space=pltpu.SMEM)
LIMIT = 28 * 1024 * 1024


class Plan:
    def __init__(self, mesh, residues, channels, heads):
        self.nc = mesh.shape["crop"]
        dap = mesh.shape["dap"]
        self.ny = 4 if dap >= 16 else 2
        self.nz = dap // self.ny
        self.qb = 4 if self.nz >= 16 else 2
        self.qa = self.nz // self.qb
        self.dap = dap
        self.n = residues
        self.c = channels
        self.heads = heads
        self.own = residues // dap
        self.msg = self.ny * self.own
        self.blk = self.nz * self.own
        self.chunks = heads // self.ny
        self.tile = self.ny * self.nz * self.own
        self.flat = 5 * channels * channels // LANES
        self.share = self.flat // self.nc
        self.quarter = self.share // self.ny
        self.extra = 16


def nn(a, b):
    return lax.dot_general(a, b, (((1,), (0,)), ((), ())), preferred_element_type=F32)


def nt(a, b):
    return lax.dot_general(a, b, (((1,), (1,)), ((), ())), preferred_element_type=F32)


def tn(a, b):
    return lax.dot_general(a, b, (((0,), (0,)), ((), ())), preferred_element_type=F32)


def swap_matrix(plan, to_z):
    size = (plan.tile, plan.tile)
    row = lax.broadcasted_iota(jnp.int32, size, 0)
    col = lax.broadcasted_iota(jnp.int32, size, 1)
    za, az = (row, col) if to_z else (col, row)
    z, a, k = za // plan.msg, (za % plan.msg) // plan.own, za % plan.own
    return jnp.where(az == a * plan.blk + z * plan.own + k, 1.0, 0.0).astype(BF)


def place(plan):
    me = lax.axis_index("dap")
    return me // plan.nz, me % plan.nz


def signal(peer):
    pl.semaphore_signal(
        pltpu.get_barrier_semaphore(), inc=1, device_id=peer, device_id_type=pl.DeviceIdType.MESH
    )


def remote(src, dst, send, recv, peer):
    return pltpu.make_async_remote_copy(
        src_ref=src,
        dst_ref=dst,
        send_sem=send,
        recv_sem=recv,
        device_id=peer,
        device_id_type=pl.DeviceIdType.MESH,
    )


def loop(count, body):
    lax.fori_loop(0, count, lambda i, c: (body(i), c)[1], 0)


def gather_kernel(
    plan, x_ref, g_ref, b_ref, xg_out, bias_out, xg_z, xg_y, b_z,
    xs, xr, gs, gr, bs, br, ys, yr, cs, cr,
):
    y, z = place(plan)
    ny, nz, blk = plan.ny, plan.nz, plan.blk

    def zpeer(i):
        zp = lax.rem(z + i + 1, nz)
        return zp, {"dap": y * nz + zp}

    def ypeer(i):
        yp = lax.rem(y + i + 1, ny)
        return yp, {"dap": yp * nz + z}

    loop(nz - 1, lambda i: signal(zpeer(i)[1]))
    loop(ny - 1, lambda i: signal(ypeer(i)[1]))
    pl.semaphore_wait(pltpu.get_barrier_semaphore(), nz + ny - 2)

    def b_copy(i):
        return remote(b_ref, b_z.at[:, z], bs.at[i], br.at[i], zpeer(i)[1])

    def x_copy(i):
        zp, peer = zpeer(i)
        return remote(x_ref.at[zp], xg_z.at[0, z], xs.at[i], xr.at[i], peer)

    def g_copy(i):
        zp, peer = zpeer(i)
        return remote(g_ref.at[zp], xg_z.at[1, z], gs.at[i], gr.at[i], peer)

    loop(nz - 1, lambda i: b_copy(i).start())
    loop(nz - 1, lambda i: x_copy(i).start())
    loop(nz - 1, lambda i: g_copy(i).start())
    b_z[:, z] = b_ref[...]
    xg_z[0, z] = x_ref[z]
    xg_z[1, z] = g_ref[z]
    swap = swap_matrix(plan, False)

    mine = pl.ds(pl.multiple_of(y * blk, blk), blk)

    def c_copy(c, i):
        part = bias_out.at[pl.ds(c * ny, ny), mine]
        return remote(part, part, cs.at[c, i], cr.at[c, i], ypeer(i)[1])

    loop(nz - 1, lambda i: b_copy(i).wait_recv())
    for c in range(plan.chunks):
        rows = nn(swap, b_z[c].reshape(plan.tile, plan.n)).astype(BF)
        bias_out[pl.ds(c * ny, ny), mine] = rows.reshape(ny, blk, plan.n)
        for i in range(ny - 1):
            c_copy(c, i).start()

    def y_copy(i):
        yp, peer = ypeer(i)
        return remote(xg_y.at[:, yp], xg_out.at[:, y], ys.at[i], yr.at[i], peer)

    loop(nz - 1, lambda i: x_copy(i).wait_recv())
    loop(nz - 1, lambda i: g_copy(i).wait_recv())
    for t in range(2):
        rows = nn(swap, xg_z[t].reshape(plan.tile, plan.c)).astype(BF)
        xg_y[t] = rows.reshape(ny, blk, plan.c)
    for i in range(ny - 1):
        y_copy(i).start()
    xg_out[:, y] = xg_y[:, y]

    for i in range(ny - 1):
        y_copy(i).wait_recv()
    for c in range(plan.chunks):
        for i in range(ny - 1):
            c_copy(c, i).wait_recv()
            c_copy(c, i).wait_send()
    for i in range(ny - 1):
        y_copy(i).wait_send()
    loop(nz - 1, lambda i: b_copy(i).wait_send())
    loop(nz - 1, lambda i: x_copy(i).wait_send())
    loop(nz - 1, lambda i: g_copy(i).wait_send())


def compute_kernel(
    plan, ext_ref, xg_ref, bias_ref, win_ref, wout_ref, gain_ref, dr_ref, ds_ref, wg_ref
):
    n, ch = plan.n, plan.c
    size = ch // plan.heads
    mult = 1.0 / math.sqrt(size)
    extent = ext_ref[0]
    gain = gain_ref[...]
    value = xg_ref[0].astype(F32)
    centred = value - jnp.mean(value, axis=-1, keepdims=True)
    inv_std = lax.rsqrt(jnp.mean(centred * centred, axis=-1, keepdims=True) + EPSILON)
    normal = centred * inv_std
    normed = (normal * gain).astype(BF)
    q, k, v, gl = [nn(normed, win_ref[p]).astype(BF) for p in range(4)]
    gate = jax.nn.sigmoid(gl.astype(F32))
    row_valid = lax.broadcasted_iota(jnp.int32, (n, ch), 0) < extent
    mg = jnp.where(row_valid, xg_ref[1].astype(F32), 0.0).astype(BF)
    d_gated = nt(mg, wout_ref[...])
    da = (d_gated * gate).astype(BF)
    col_valid = lax.broadcasted_iota(jnp.int32, (n, n), 1) < extent
    head_of = lax.broadcasted_iota(jnp.int32, (1, ch), 1) // size
    att = dv = dq = dk = jnp.zeros((n, ch), F32)
    for h in range(plan.heads):
        own = jnp.where(head_of == h, 1.0, 0.0).astype(BF)
        qh, kh, vh, dah = q * own, k * own, v * own, da * own
        scores = nt(qh, k) * mult + bias_ref[h].astype(F32)
        scores = jnp.where(col_valid, scores, MASKED)
        expo = jnp.exp(scores - jnp.max(scores, axis=-1, keepdims=True))
        probs = expo * (1.0 / jnp.sum(expo, axis=-1, keepdims=True))
        pb = probs.astype(BF)
        d_probs = nt(dah, v)
        total = jnp.sum(probs * d_probs, axis=-1, keepdims=True)
        dsb = (probs * (d_probs - total)).astype(BF)
        ds_ref[h] = dsb
        att += nn(pb, vh)
        dv += tn(pb, dah)
        dq += nn(dsb, kh)
        dk += tn(dsb, qh)
    gated = (att * gate).astype(BF)
    grads = [
        (dq * mult).astype(BF),
        (dk * mult).astype(BF),
        dv.astype(BF),
        (d_gated * att * gate * (1.0 - gate)).astype(BF),
    ]
    d_normed = jnp.zeros((n, ch), F32)
    for p in range(4):
        d_normed += nt(grads[p], win_ref[p])
    scaled = d_normed * gain
    d_row = inv_std * (
        scaled
        - jnp.mean(scaled, axis=-1, keepdims=True)
        - normal * jnp.mean(scaled * normal, axis=-1, keepdims=True)
    )
    dr_ref[...] = d_row.astype(BF)

    share = plan.share

    def keep(start, part):
        at = start
        while at < start + ch:
            c = at // share
            end = min(start + ch, (c + 1) * share)
            wg_ref[c, at - c * share : end - c * share] = part[at - start : end - start]
            at = end

    for t in range(5):
        term = tn(normed, grads[t]) if t < 4 else tn(gated, mg)
        for half in range(2):
            part = term[:, half * LANES : (half + 1) * LANES].astype(BF)
            keep((2 * t + half) * ch, part)
    d_gain = jnp.sum(d_normed * normal, axis=0, keepdims=True)
    line = lax.broadcasted_iota(jnp.int32, (plan.extra, LANES), 0)
    lo = jnp.broadcast_to(d_gain[:, :LANES], (plan.extra, LANES))
    hi = jnp.broadcast_to(d_gain[:, LANES:], (plan.extra, LANES))
    block = jnp.where(line == 0, lo, jnp.where(line == 1, hi, 0.0)).astype(BF)
    for c in range(plan.nc):
        wg_ref[c, share : share + plan.extra] = block


def scatter_kernel(
    plan, dr_ref, ds_ref, wg_ref, dr_out, db_out, w_out, gain_out,
    dr_y, dr_z, ds_y, ds_z, ds_in, w_c, w_y, w_yin, w_a, w_b, w_q, w_s,
    dys, dyr, dzs, dzr, sys_, syr, szs, szr, wcs, wcr, wys, wyr, was, war, wbs, wbr,
    gys, gyr, gcs, gcr,
):
    y, z = place(plan)
    crop = lax.axis_index("crop")
    ny, nz, nc, blk, qa, qb = plan.ny, plan.nz, plan.nc, plan.blk, plan.qa, plan.qb
    za, zb = z // qb, z % qb
    share, quarter = plan.share, plan.quarter

    def zpeer(i):
        zp = lax.rem(z + i + 1, nz)
        return zp, {"dap": y * nz + zp}

    def ypeer(i):
        yp = lax.rem(y + i + 1, ny)
        return yp, {"dap": yp * nz + z}

    def cpeer(i):
        cp = lax.rem(crop + i + 1, nc)
        return cp, {"crop": cp}

    loop(nz - 1, lambda i: signal(zpeer(i)[1]))
    loop(ny - 1, lambda i: signal(ypeer(i)[1]))
    loop(nc - 1, lambda i: signal(cpeer(i)[1]))
    pl.semaphore_wait(pltpu.get_barrier_semaphore(), nz + ny + nc - 3)

    def dr_ycopy(i):
        yp, peer = ypeer(i)
        return remote(dr_ref.at[yp], dr_y.at[y], dys.at[i], dyr.at[i], peer)

    def dr_zcopy(i):
        zp, peer = zpeer(i)
        return remote(dr_z.at[zp], dr_out.at[z], dzs.at[i], dzr.at[i], peer)

    def ds_ycopy(c, i):
        yp, peer = ypeer(i)
        part = ds_ref.at[pl.ds(c * ny, ny), yp]
        return remote(part, ds_y.at[c, i], sys_.at[c, i], syr.at[c, i], peer)

    def ds_zcopy(c, i):
        zp, peer = zpeer(i)
        return remote(ds_z.at[c, zp], ds_in.at[c, z], szs.at[c, i], szr.at[c, i], peer)

    def w_ccopy(i):
        cp, peer = cpeer(i)
        return remote(wg_ref.at[cp], w_c.at[crop], wcs.at[i], wcr.at[i], peer)

    def w_ycopy(i):
        yp, peer = ypeer(i)
        return remote(w_y.at[yp], w_yin.at[y], wys.at[i], wyr.at[i], peer)

    def w_acopy(i):
        peer = {"dap": y * nz + za * qb + lax.rem(zb + i + 1, qb)}
        return remote(w_a.at[zb], w_a.at[zb], was.at[i], war.at[i], peer)

    def w_bcopy(i):
        peer = {"dap": y * nz + lax.rem(za + i + 1, qa) * qb + zb}
        return remote(w_b.at[za], w_b.at[za], wbs.at[i], wbr.at[i], peer)

    def g_ycopy(i):
        part = w_q.at[y]
        return remote(part, part, gys.at[i], gyr.at[i], ypeer(i)[1])

    def g_ccopy(i):
        part = w_out.at[crop]
        return remote(w_s, part, gcs.at[i], gcr.at[i], cpeer(i)[1])

    for i in range(ny - 1):
        dr_ycopy(i).start()
    loop(nc - 1, lambda i: w_ccopy(i).start())
    for c in range(plan.chunks):
        for i in range(ny - 1):
            ds_ycopy(c, i).start()
    dr_y[y] = dr_ref[y]
    w_c[crop] = wg_ref[crop]
    swap = swap_matrix(plan, True)

    for i in range(ny - 1):
        dr_ycopy(i).wait_recv()
    rows = nn(swap, dr_y[...].reshape(plan.tile, plan.c)).astype(BF)
    dr_z[...] = rows.reshape(nz, plan.msg, plan.c)
    loop(nz - 1, lambda i: dr_zcopy(i).start())
    dr_out[z] = dr_z[z]

    def fold(c):
        for i in range(ny - 1):
            ds_ycopy(c, i).wait_recv()
        total = ds_ref[pl.ds(c * ny, ny), y].astype(F32)
        for i in range(ny - 1):
            total += ds_y[c, i].astype(F32)
        rows = nn(swap, total.astype(BF).reshape(plan.tile, plan.n)).astype(BF)
        ds_z[c] = rows.reshape(nz, plan.msg, plan.n)
        loop(nz - 1, lambda i: ds_zcopy(c, i).start())
        ds_in[c, z] = ds_z[c, z]

    half = (plan.chunks + 1) // 2
    for c in range(half):
        fold(c)

    loop(nc - 1, lambda i: w_ccopy(i).wait_recv())
    total = w_c[0].astype(F32)
    for i in range(1, nc):
        total += w_c[i].astype(F32)
    total = total.astype(BF)
    for i in range(ny):
        w_y[i, :quarter] = total[i * quarter : (i + 1) * quarter]
        w_y[i, quarter:] = total[share:]
    for i in range(ny - 1):
        w_ycopy(i).start()
    w_yin[y] = w_y[y]

    for c in range(half, plan.chunks):
        fold(c)

    def summed(ref, count):
        out = ref[0].astype(F32)
        for i in range(1, count):
            out += ref[i].astype(F32)
        return out

    for i in range(ny - 1):
        w_ycopy(i).wait_recv()
    w_a[zb] = summed(w_yin, ny).astype(BF)
    for i in range(qb - 1):
        w_acopy(i).start()
    for i in range(qb - 1):
        w_acopy(i).wait_recv()
    w_b[za] = summed(w_a, qb).astype(BF)
    for i in range(qa - 1):
        w_bcopy(i).start()
    for i in range(qa - 1):
        w_bcopy(i).wait_recv()
    total = summed(w_b, qa)
    gain_out[...] = total[quarter:]
    w_q[y] = total[:quarter].astype(BF)
    for i in range(ny - 1):
        g_ycopy(i).start()
    for i in range(ny - 1):
        g_ycopy(i).wait_recv()
    for i in range(ny):
        w_s[pl.ds(i * quarter, quarter)] = w_q[i]
    loop(nc - 1, lambda i: g_ccopy(i).start())
    w_out[crop] = w_s[...]

    for c in range(plan.chunks):
        loop(nz - 1, lambda i: ds_zcopy(c, i).wait_recv())
        db_out[c] = summed(ds_in.at[c], nz)
    loop(nz - 1, lambda i: dr_zcopy(i).wait_recv())
    loop(nc - 1, lambda i: g_ccopy(i).wait_recv())

    for i in range(ny - 1):
        dr_ycopy(i).wait_send()
        w_ycopy(i).wait_send()
        g_ycopy(i).wait_send()
        for c in range(plan.chunks):
            ds_ycopy(c, i).wait_send()
    for i in range(qb - 1):
        w_acopy(i).wait_send()
    for i in range(qa - 1):
        w_bcopy(i).wait_send()
    loop(nc - 1, lambda i: w_ccopy(i).wait_send())
    loop(nc - 1, lambda i: g_ccopy(i).wait_send())
    loop(nz - 1, lambda i: dr_zcopy(i).wait_send())
    for c in range(plan.chunks):
        loop(nz - 1, lambda i: ds_zcopy(c, i).wait_send())


def dma(*shape):
    return pltpu.SemaphoreType.DMA(shape)


def on_device(plan, x, upstream, bias, extents, w_in, w_final, gain):
    ny, nz, nc, n, ch = plan.ny, plan.nz, plan.nc, plan.n, plan.c
    msg, blk, chunks = plan.msg, plan.blk, plan.chunks
    xg, full = pl.pallas_call(
        functools.partial(gather_kernel, plan),
        out_shape=(
            jax.ShapeDtypeStruct((2, ny, blk, ch), BF),
            jax.ShapeDtypeStruct((plan.heads, n, n), BF),
        ),
        in_specs=[VMEM] * 3,
        out_specs=(VMEM, VMEM),
        scratch_shapes=[
            pltpu.VMEM((2, nz, msg, ch), BF),
            pltpu.VMEM((2, ny, blk, ch), BF),
            pltpu.VMEM((chunks, nz, msg, n), BF),
            *[dma(nz - 1)] * 6,
            *[dma(ny - 1)] * 2,
            *[dma(chunks, ny - 1)] * 2,
        ],
        compiler_params=pltpu.CompilerParams(
            collective_id=0, has_side_effects=True, vmem_limit_bytes=LIMIT
        ),
        name="gather_rows",
    )(
        x.reshape(nz, msg, ch),
        upstream.reshape(nz, msg, ch),
        bias.reshape(chunks, msg, n),
    )
    total = plan.share + plan.extra
    dr, ds, wg = pl.pallas_call(
        functools.partial(compute_kernel, plan),
        out_shape=(
            jax.ShapeDtypeStruct((n, ch), BF),
            jax.ShapeDtypeStruct((plan.heads, n, n), BF),
            jax.ShapeDtypeStruct((nc, total, LANES), BF),
        ),
        in_specs=[SMEM] + [VMEM] * 5,
        out_specs=(VMEM, VMEM, VMEM),
        compiler_params=pltpu.CompilerParams(vmem_limit_bytes=LIMIT),
        name="row_gradients",
    )(extents, xg.reshape(2, n, ch), full, w_in, w_final, gain.reshape(1, ch))
    part = plan.quarter + plan.extra
    d_rows, d_bias, w_sum, gain_sum = pl.pallas_call(
        functools.partial(scatter_kernel, plan),
        out_shape=(
            jax.ShapeDtypeStruct((nz, msg, ch), BF),
            jax.ShapeDtypeStruct((chunks, msg, n), F32),
            jax.ShapeDtypeStruct((nc, plan.share, LANES), BF),
            jax.ShapeDtypeStruct((plan.extra, LANES), F32),
        ),
        in_specs=[VMEM] * 3,
        out_specs=(VMEM,) * 4,
        scratch_shapes=[
            pltpu.VMEM((ny, blk, ch), BF),
            pltpu.VMEM((nz, msg, ch), BF),
            pltpu.VMEM((chunks, ny - 1, ny, blk, n), BF),
            pltpu.VMEM((chunks, nz, msg, n), BF),
            pltpu.VMEM((chunks, nz, msg, n), BF),
            pltpu.VMEM((nc, total, LANES), BF),
            pltpu.VMEM((ny, part, LANES), BF),
            pltpu.VMEM((ny, part, LANES), BF),
            pltpu.VMEM((plan.qb, part, LANES), BF),
            pltpu.VMEM((plan.qa, part, LANES), BF),
            pltpu.VMEM((ny, plan.quarter, LANES), BF),
            pltpu.VMEM((plan.share, LANES), BF),
            *[dma(ny - 1)] * 2,
            *[dma(nz - 1)] * 2,
            *[dma(chunks, ny - 1)] * 2,
            *[dma(chunks, nz - 1)] * 2,
            *[dma(nc - 1)] * 2,
            *[dma(ny - 1)] * 2,
            *[dma(plan.qb - 1)] * 2,
            *[dma(plan.qa - 1)] * 2,
            *[dma(ny - 1)] * 2,
            *[dma(nc - 1)] * 2,
        ],
        compiler_params=pltpu.CompilerParams(
            collective_id=1, has_side_effects=True, vmem_limit_bytes=LIMIT
        ),
        name="scatter_gradients",
    )(
        dr.reshape(ny, blk, ch),
        ds.reshape(plan.heads, ny, blk, n),
        wg,
    )
    scale = 1.0 / (nc * plan.dap)
    w_sum = w_sum.reshape(5, 2, ch, LANES).transpose(0, 2, 1, 3).reshape(5, ch, ch)
    w_sum = w_sum.astype(F32) * scale
    return (
        d_rows.reshape(x.shape),
        d_bias.reshape(bias.shape),
        w_sum[:4],
        w_sum[4],
        gain_sum[:2].reshape(ch) * scale,
    )


def solution(mesh):
    split = P("crop", None, "dap", None)

    def whole(*arrays):
        plan = Plan(mesh, arrays[0].shape[2], arrays[0].shape[3], arrays[2].shape[1])
        return jax.shard_map(
            functools.partial(on_device, plan),
            mesh=mesh,
            in_specs=(split, split, split, P("crop"), P(), P(), P()),
            out_specs=(split, split, P(), P(), P()),
            check_vma=False,
        )(*arrays)

    return whole
```

```python
import functools
import math

import jax
import jax.numpy as jnp
from jax import lax
from jax.experimental import pallas as pl
from jax.experimental.pallas import tpu as pltpu
from jax.sharding import PartitionSpec as P

EPSILON = 1e-05
MASKED = -1000000000.0
LANES = 128
BF = jnp.bfloat16
F32 = jnp.float32
ANY = pl.BlockSpec(memory_space=pl.ANY)
VMEM = pl.BlockSpec(memory_space=pltpu.VMEM)
SMEM = pl.BlockSpec(memory_space=pltpu.SMEM)
LIMIT = 44 * 1024 * 1024


class Plan:
    def __init__(self, mesh, residues, channels, heads):
        self.nc = mesh.shape["crop"]
        self.nx = self.nc // 2
        dap = mesh.shape["dap"]
        self.ny = 4 if dap >= 16 else 2
        self.nz = dap // self.ny
        self.qb = 4 if self.nz >= 16 else 2
        self.qa = self.nz // self.qb
        self.dap = dap
        self.n = residues
        self.c = channels
        self.heads = heads
        self.own = residues // dap
        self.msg = self.ny * self.own
        self.blk = self.nz * self.own
        self.chunks = heads // self.ny
        self.tile = self.ny * self.nz * self.own
        self.flat = 5 * channels * channels // LANES
        self.share = self.flat // self.nc
        self.quarter = self.share // self.ny
        self.extra = 16


def nn(a, b):
    return lax.dot_general(a, b, (((1,), (0,)), ((), ())), preferred_element_type=F32)


def nt(a, b):
    return lax.dot_general(a, b, (((1,), (1,)), ((), ())), preferred_element_type=F32)


def tn(a, b):
    return lax.dot_general(a, b, (((0,), (0,)), ((), ())), preferred_element_type=F32)


def swap_matrix(plan, to_z):
    size = (plan.tile, plan.tile)
    row = lax.broadcasted_iota(jnp.int32, size, 0)
    col = lax.broadcasted_iota(jnp.int32, size, 1)
    za, az = (row, col) if to_z else (col, row)
    z, a, k = za // plan.msg, (za % plan.msg) // plan.own, za % plan.own
    return jnp.where(az == a * plan.blk + z * plan.own + k, 1.0, 0.0).astype(BF)


def place(plan):
    me = lax.axis_index("dap")
    return me // plan.nz, me % plan.nz


def signal(peer):
    pl.semaphore_signal(
        pltpu.get_barrier_semaphore(), inc=1, device_id=peer, device_id_type=pl.DeviceIdType.MESH
    )


def remote(src, dst, send, recv, peer):
    return pltpu.make_async_remote_copy(
        src_ref=src,
        dst_ref=dst,
        send_sem=send,
        recv_sem=recv,
        device_id=peer,
        device_id_type=pl.DeviceIdType.MESH,
    )


def loop(count, body):
    lax.fori_loop(0, count, lambda i, c: (body(i), c)[1], 0)


def keep(plan, put):
    for t in range(5):
        for half in range(2):
            start = (2 * t + half) * plan.c
            at = start
            while at < start + plan.c:
                s = at // plan.share
                end = min(start + plan.c, (s + 1) * plan.share)
                low = s * plan.share
                put(t, half, slice(at - start, end - start), s, slice(at - low, end - low))
                at = end


def summed(ref, count):
    out = ref[0].astype(F32)
    for i in range(1, count):
        out += ref[i].astype(F32)
    return out


def whole_kernel(
    plan, ext_ref, x_hbm, g_hbm, b_hbm, win_hbm, wout_hbm, gain_hbm,
    dr_out, db_out, win_out, wout_out, gain_out,
    x_in, g_in, b_in, win_ref, wout_ref, gain_ref,
    xg_s, xg_y, xg_zs, xg_z, b_z, bias_ref, ds_ref, ds_y, ds_zs, ds_z,
    dr_s, dr_y, dr_zs, dr_z, wg, w_cin, w_x, w_xin, w_y, w_yin, w_a, w_b, w_all,
    lsem, xy, xz, bf, bn, by, dy, dz, ry, rz, wc, wx, wy, wa, wb, gy, gx, gc,
):
    y, z = place(plan)
    crop = lax.axis_index("crop")
    cx, core = crop // 2, crop % 2
    ny, nz, nx, blk, qa, qb = plan.ny, plan.nz, plan.nx, plan.blk, plan.qa, plan.qb
    za, zb = z // qb, z % qb
    n, ch, msg = plan.n, plan.c, plan.msg
    share, quarter, extra = plan.share, plan.quarter, plan.extra

    def zpeer(i):
        step = (i + 1) // 2
        zp = lax.rem(z + nz // 2 + step * (1 - 2 * (i % 2)), nz)
        return zp, {"dap": y * nz + zp}

    def ypeer(i):
        yp = lax.rem(y + i + 1, ny)
        return yp, {"dap": yp * nz + z}

    def xpeer(i):
        xp = lax.rem(cx + i + 1, nx)
        return xp, {"crop": xp * 2 + core}

    def apeer(i):
        return {"dap": y * nz + lax.rem(za + i + 1, qa) * qb + zb}

    def bpeer(i):
        return {"dap": y * nz + za * qb + lax.rem(zb + i + 1, qb)}

    other = {"crop": cx * 2 + 1 - core}

    local = [
        pltpu.make_async_copy(s, d, lsem.at[i])
        for i, (s, d) in enumerate(
            [
                (b_hbm, b_in), (x_hbm, x_in), (g_hbm, g_in),
                (win_hbm, win_ref), (wout_hbm, wout_ref), (gain_hbm, gain_ref),
            ]
        )
    ]
    for c in local:
        c.start()
    loop(nz - 1, lambda i: signal(zpeer(i)[1]))
    for i in range(ny - 1):
        signal(ypeer(i)[1])
    for i in range(nx - 1):
        signal(xpeer(i)[1])
    signal(other)
    for c in local[:3]:
        c.wait()
    b_z[:, za, zb] = b_in[...].reshape(plan.chunks, msg, n)
    xg_s[0] = x_in[...].reshape(ny, blk, ch)
    xg_s[1] = g_in[...].reshape(ny, blk, ch)
    to_y = swap_matrix(plan, False)
    to_z = swap_matrix(plan, True)
    pl.semaphore_wait(pltpu.get_barrier_semaphore(), nz + ny + nx - 2)

    def b_far(i):
        part = b_z.at[:, za, zb]
        return remote(part, part, bf.at[0, i], bf.at[1, i], apeer(i))

    def b_near(i):
        part = b_z.at[:, :, zb]
        return remote(part, part, bn.at[0, i], bn.at[1, i], bpeer(i))

    mine = pl.ds(pl.multiple_of(y * blk, blk), blk)

    def b_y(c, i):
        part = bias_ref.at[pl.ds(c * ny, ny), mine]
        return remote(part, part, by.at[0, c, i], by.at[1, c, i], ypeer(i)[1])

    def x_y(i):
        yp, peer = ypeer(i)
        return remote(xg_s.at[:, yp], xg_y.at[:, y], xy.at[0, i], xy.at[1, i], peer)

    def x_z(i):
        zp, peer = zpeer(i)
        return remote(xg_zs.at[:, zp], xg_z.at[:, z], xz.at[0, i], xz.at[1, i], peer)

    for i in range(qa - 1):
        b_far(i).start()
    for i in range(ny - 1):
        x_y(i).start()
    xg_y[:, y] = xg_s[:, y]
    for i in range(qa - 1):
        b_far(i).wait_recv()
    for i in range(qb - 1):
        b_near(i).start()
    for i in range(ny - 1):
        x_y(i).wait_recv()
    for t in range(2):
        rows = nn(to_z, xg_y[t].reshape(plan.tile, ch)).astype(BF)
        xg_zs[t] = rows.reshape(nz, msg, ch)
    loop(nz - 1, lambda i: x_z(i).start())
    xg_z[:, z] = xg_zs[:, z]
    for i in range(qb - 1):
        b_near(i).wait_recv()
    for c in range(plan.chunks):
        rows = nn(to_y, b_z[c].reshape(plan.tile, n)).astype(BF)
        bias_ref[pl.ds(c * ny, ny), mine] = rows.reshape(ny, blk, n)
        for i in range(ny - 1):
            b_y(c, i).start()
    for c in local[3:]:
        c.wait()
    loop(nz - 1, lambda i: x_z(i).wait_recv())

    size = ch // plan.heads
    mult = 1.0 / math.sqrt(size)
    extent = ext_ref[0]
    gain = gain_ref[...]
    value = nn(to_y, xg_z[0].reshape(plan.tile, ch))
    upstream = nn(to_y, xg_z[1].reshape(plan.tile, ch))
    centred = value - jnp.mean(value, axis=-1, keepdims=True)
    inv_std = lax.rsqrt(jnp.mean(centred * centred, axis=-1, keepdims=True) + EPSILON)
    normal = centred * inv_std
    normed = (normal * gain).astype(BF)
    q, k, v, gl = [nn(normed, win_ref[p]).astype(BF) for p in range(4)]
    gate = jax.nn.sigmoid(gl.astype(F32))
    row_valid = lax.broadcasted_iota(jnp.int32, (n, ch), 0) < extent
    mg = jnp.where(row_valid, upstream, 0.0).astype(BF)
    d_gated = nt(mg, wout_ref[...])
    da = (d_gated * gate).astype(BF)
    col_valid = lax.broadcasted_iota(jnp.int32, (n, n), 1) < extent
    head_of = lax.broadcasted_iota(jnp.int32, (1, ch), 1) // size
    att = dv = dq = dk = jnp.zeros((n, ch), F32)

    def ds_ycopy(c, i):
        yp, peer = ypeer(i)
        part = ds_ref.at[pl.ds(c * ny, ny), yp]
        return remote(part, ds_y.at[c, i], dy.at[0, c, i], dy.at[1, c, i], peer)

    for h in range(plan.heads):
        if h % ny == 0:
            for i in range(ny - 1):
                b_y(h // ny, i).wait_recv()
        own = jnp.where(head_of == h, 1.0, 0.0).astype(BF)
        qh, kh, vh, dah = q * own, k * own, v * own, da * own
        scores = nt(qh, k) * mult + bias_ref[h].astype(F32)
        scores = jnp.where(col_valid, scores, MASKED)
        expo = jnp.exp(scores - jnp.max(scores, axis=-1, keepdims=True))
        probs = expo * (1.0 / jnp.sum(expo, axis=-1, keepdims=True))
        pb = probs.astype(BF)
        d_probs = nt(dah, v)
        total = jnp.sum(probs * d_probs, axis=-1, keepdims=True)
        dsb = (probs * (d_probs - total)).astype(BF)
        ds_ref[h] = dsb.reshape(ny, blk, n)
        att += nn(pb, vh)
        dv += tn(pb, dah)
        dq += nn(dsb, kh)
        dk += tn(dsb, qh)
        if h % ny == ny - 1:
            for i in range(ny - 1):
                ds_ycopy(h // ny, i).start()
    gated = (att * gate).astype(BF)
    grads = [
        (dq * mult).astype(BF),
        (dk * mult).astype(BF),
        dv.astype(BF),
        (d_gated * att * gate * (1.0 - gate)).astype(BF),
    ]
    d_normed = jnp.zeros((n, ch), F32)
    for p in range(4):
        d_normed += nt(grads[p], win_ref[p])
    terms = [tn(normed, grads[p]).astype(BF) for p in range(4)] + [tn(gated, mg).astype(BF)]

    def put(t, half, rows, s, at):
        wg[s // nx, s % nx, at] = terms[t][rows, half * LANES : (half + 1) * LANES]

    keep(plan, put)
    d_gain = jnp.sum(d_normed * normal, axis=0, keepdims=True)
    line = lax.broadcasted_iota(jnp.int32, (extra, LANES), 0)
    lo = jnp.broadcast_to(d_gain[:, :LANES], (extra, LANES))
    hi = jnp.broadcast_to(d_gain[:, LANES:], (extra, LANES))
    block = jnp.where(line == 0, lo, jnp.where(line == 1, hi, 0.0)).astype(BF)
    for c in range(plan.nc):
        wg[c // nx, c % nx, share:] = block

    def w_core():
        return remote(wg.at[1 - core], w_cin, wc.at[0], wc.at[1], other)

    def w_xcopy(i):
        xp, peer = xpeer(i)
        return remote(w_x.at[xp], w_xin.at[cx], wx.at[0, i], wx.at[1, i], peer)

    def w_ycopy(i):
        yp, peer = ypeer(i)
        return remote(w_y.at[yp], w_yin.at[y], wy.at[0, i], wy.at[1, i], peer)

    def w_acopy(i):
        return remote(w_a.at[zb], w_a.at[zb], wa.at[0, i], wa.at[1, i], bpeer(i))

    def w_bcopy(i):
        return remote(w_b.at[za], w_b.at[za], wb.at[0, i], wb.at[1, i], apeer(i))

    fourth = pl.ds(pl.multiple_of(y * quarter, 16), quarter)

    def g_y(i):
        part = w_all.at[core, cx, fourth]
        return remote(part, part, gy.at[0, i], gy.at[1, i], ypeer(i)[1])

    def g_x(i):
        part = w_all.at[core, cx]
        return remote(part, part, gx.at[0, i], gx.at[1, i], xpeer(i)[1])

    def g_core():
        part = w_all.at[core]
        return remote(part, part, gc.at[0], gc.at[1], other)

    def dr_ycopy(i):
        yp, peer = ypeer(i)
        return remote(dr_s.at[yp], dr_y.at[y], ry.at[0, i], ry.at[1, i], peer)

    def dr_zcopy(i):
        zp, peer = zpeer(i)
        return remote(dr_zs.at[zp], dr_z.at[z], rz.at[0, i], rz.at[1, i], peer)

    def ds_zcopy(c, i):
        zp, peer = zpeer(i)
        return remote(ds_zs.at[c, zp], ds_z.at[c, z], dz.at[0, c, i], dz.at[1, c, i], peer)

    def fold(c):
        for i in range(ny - 1):
            ds_ycopy(c, i).wait_recv()
        total = ds_ref[pl.ds(c * ny, ny), y].astype(F32)
        for i in range(ny - 1):
            total += ds_y[c, i].astype(F32)
        rows = nn(to_z, total.astype(BF).reshape(plan.tile, n)).astype(BF)
        ds_zs[c] = rows.reshape(nz, msg, n)
        loop(nz - 1, lambda i: ds_zcopy(c, i).start())
        ds_z[c, z] = ds_zs[c, z]

    w_core().start()
    scaled = d_normed * gain
    d_row = inv_std * (
        scaled
        - jnp.mean(scaled, axis=-1, keepdims=True)
        - normal * jnp.mean(scaled * normal, axis=-1, keepdims=True)
    )
    dr_s[...] = d_row.astype(BF).reshape(ny, blk, ch)
    for i in range(ny - 1):
        dr_ycopy(i).start()
    dr_y[y] = dr_s[y]

    w_core().wait_recv()
    w_x[...] = (wg[core].astype(F32) + w_cin[...].astype(F32)).astype(BF)
    for i in range(nx - 1):
        w_xcopy(i).start()
    w_xin[cx] = w_x[cx]

    half = (plan.chunks + 1) // 2
    for c in range(half):
        fold(c)
    for i in range(ny - 1):
        dr_ycopy(i).wait_recv()
    rows = nn(to_z, dr_y[...].reshape(plan.tile, ch)).astype(BF)
    dr_zs[...] = rows.reshape(nz, msg, ch)
    loop(nz - 1, lambda i: dr_zcopy(i).start())
    dr_z[z] = dr_zs[z]

    for i in range(nx - 1):
        w_xcopy(i).wait_recv()
    total = summed(w_xin, nx).astype(BF)
    for i in range(ny):
        w_y[i, :quarter] = total[i * quarter : (i + 1) * quarter]
        w_y[i, quarter:] = total[share:]
    for i in range(ny - 1):
        w_ycopy(i).start()
    w_yin[y] = w_y[y]

    for c in range(half, plan.chunks):
        fold(c)

    for i in range(ny - 1):
        w_ycopy(i).wait_recv()
    w_a[zb] = summed(w_yin, ny).astype(BF)
    for i in range(qb - 1):
        w_acopy(i).start()
    for i in range(qb - 1):
        w_acopy(i).wait_recv()
    w_b[za] = summed(w_a, qb).astype(BF)
    for i in range(qa - 1):
        w_bcopy(i).start()
    for i in range(qa - 1):
        w_bcopy(i).wait_recv()
    scale = 1.0 / (plan.nc * plan.dap)
    total = summed(w_b, qa)
    gain_out[...] = total[quarter:] * scale
    w_all[core, cx, fourth] = total[:quarter].astype(BF)
    for i in range(ny - 1):
        g_y(i).start()
    for c in range(half):
        loop(nz - 1, lambda i: ds_zcopy(c, i).wait_recv())
        db_out[pl.ds(c * ny, ny)] = summed(ds_z.at[c], nz).reshape(ny, plan.own, n)
    for i in range(ny - 1):
        g_y(i).wait_recv()
    for i in range(nx - 1):
        g_x(i).start()
    loop(nz - 1, lambda i: dr_zcopy(i).wait_recv())
    rows = nn(to_y, dr_z[...].reshape(plan.tile, ch)).astype(BF)
    dr_out[...] = rows.reshape(plan.dap, plan.own, ch)
    for c in range(half, plan.chunks):
        loop(nz - 1, lambda i: ds_zcopy(c, i).wait_recv())
        db_out[pl.ds(c * ny, ny)] = summed(ds_z.at[c], nz).reshape(ny, plan.own, n)
    for i in range(nx - 1):
        g_x(i).wait_recv()
    g_core().start()

    def take(t, half, rows, s, at):
        part = w_all[s // nx, s % nx, at].astype(F32) * scale
        cols = slice(half * LANES, (half + 1) * LANES)
        if t < 4:
            win_out[t, rows, cols] = part
        else:
            wout_out[rows, cols] = part

    for i in range(qa - 1):
        b_far(i).wait_send()
        w_bcopy(i).wait_send()
    for i in range(qb - 1):
        b_near(i).wait_send()
        w_acopy(i).wait_send()
    for i in range(ny - 1):
        x_y(i).wait_send()
        dr_ycopy(i).wait_send()
        w_ycopy(i).wait_send()
        g_y(i).wait_send()
        for c in range(plan.chunks):
            b_y(c, i).wait_send()
            ds_ycopy(c, i).wait_send()
    for i in range(nx - 1):
        w_xcopy(i).wait_send()
        g_x(i).wait_send()
    w_core().wait_send()
    loop(nz - 1, lambda i: x_z(i).wait_send())
    loop(nz - 1, lambda i: dr_zcopy(i).wait_send())
    for c in range(plan.chunks):
        loop(nz - 1, lambda i: ds_zcopy(c, i).wait_send())
    g_core().wait_recv()
    g_core().wait_send()
    keep(plan, take)


def dma(*shape):
    return pltpu.SemaphoreType.DMA(shape)


def on_device(plan, x, upstream, bias, extents, w_in, w_final, gain):
    ny, nz, nx, n, ch = plan.ny, plan.nz, plan.nx, plan.n, plan.c
    msg, blk, chunks, heads = plan.msg, plan.blk, plan.chunks, plan.heads
    total, part = plan.share + plan.extra, plan.quarter + plan.extra

    def buf(*shape, kind=BF):
        return pltpu.VMEM(shape, kind)

    d_rows, d_bias, d_in, d_out, gain_sum = pl.pallas_call(
        functools.partial(whole_kernel, plan),
        out_shape=(
            jax.ShapeDtypeStruct((plan.dap, plan.own, ch), BF),
            jax.ShapeDtypeStruct((heads, plan.own, n), F32),
            jax.ShapeDtypeStruct((4, ch, ch), F32),
            jax.ShapeDtypeStruct((ch, ch), F32),
            jax.ShapeDtypeStruct((plan.extra, LANES), F32),
        ),
        in_specs=[SMEM] + [ANY] * 6,
        out_specs=(VMEM,) * 5,
        scratch_shapes=[
            buf(plan.dap, plan.own, ch),
            buf(plan.dap, plan.own, ch),
            buf(heads, plan.own, n),
            buf(4, ch, ch),
            buf(ch, ch),
            buf(1, ch, kind=F32),
            buf(2, ny, blk, ch),
            buf(2, ny, blk, ch),
            buf(2, nz, msg, ch),
            buf(2, nz, msg, ch),
            buf(chunks, plan.qa, plan.qb, msg, n),
            buf(heads, n, n),
            buf(heads, ny, blk, n),
            buf(chunks, ny - 1, ny, blk, n),
            buf(chunks, nz, msg, n),
            buf(chunks, nz, msg, n),
            buf(ny, blk, ch),
            buf(ny, blk, ch),
            buf(nz, msg, ch),
            buf(nz, msg, ch),
            buf(2, nx, total, LANES),
            buf(nx, total, LANES),
            buf(nx, total, LANES),
            buf(nx, total, LANES),
            buf(ny, part, LANES),
            buf(ny, part, LANES),
            buf(plan.qb, part, LANES),
            buf(plan.qa, part, LANES),
            buf(2, nx, plan.share, LANES),
            dma(6),
            dma(2, ny - 1),
            dma(2, nz - 1),
            dma(2, plan.qa - 1),
            dma(2, plan.qb - 1),
            dma(2, chunks, ny - 1),
            dma(2, chunks, ny - 1),
            dma(2, chunks, nz - 1),
            dma(2, ny - 1),
            dma(2, nz - 1),
            dma(2),
            dma(2, nx - 1),
            dma(2, ny - 1),
            dma(2, plan.qb - 1),
            dma(2, plan.qa - 1),
            dma(2, ny - 1),
            dma(2, nx - 1),
            dma(2),
        ],
        compiler_params=pltpu.CompilerParams(
            collective_id=0, has_side_effects=True, vmem_limit_bytes=LIMIT
        ),
        name="row_attention_gradients",
    )(
        extents, x[0], upstream[0], bias[0], w_in, w_final, gain.reshape(1, ch)
    )
    return (
        d_rows[None],
        d_bias[None],
        d_in,
        d_out,
        gain_sum[:2].reshape(ch),
    )


def solution(mesh):
    split = P("crop", None, "dap", None)

    def whole(*arrays):
        plan = Plan(mesh, arrays[0].shape[2], arrays[0].shape[3], arrays[2].shape[1])
        return jax.shard_map(
            functools.partial(on_device, plan),
            mesh=mesh,
            in_specs=(split, split, split, P("crop"), P(), P(), P()),
            out_specs=(split, split, P(), P(), P()),
            check_vma=False,
        )(*arrays)

    return whole
```

```python
import functools
import math

import jax
import jax.numpy as jnp
from jax import lax
from jax.experimental import pallas as pl
from jax.experimental.pallas import tpu as pltpu
from jax.sharding import PartitionSpec as P

EPSILON = 1e-05
MASKED = -1000000000.0
LANES = 128
BF = jnp.bfloat16
F32 = jnp.float32
ANY = pl.BlockSpec(memory_space=pl.ANY)
VMEM = pl.BlockSpec(memory_space=pltpu.VMEM)
SMEM = pl.BlockSpec(memory_space=pltpu.SMEM)
LIMIT = 60 * 1024 * 1024


class Plan:
    def __init__(self, mesh, residues, channels, heads):
        self.nc = mesh.shape["crop"]
        self.nx = self.nc // 2
        dap = mesh.shape["dap"]
        self.ny = 4 if dap >= 16 else 2
        self.nz = dap // self.ny
        self.qb = 4 if self.nz >= 16 else 2
        self.qa = self.nz // self.qb
        self.dap = dap
        self.n = residues
        self.c = channels
        self.heads = heads
        self.own = residues // dap
        self.msg = self.ny * self.own
        self.blk = self.nz * self.own
        self.chunks = heads // self.ny
        self.tile = self.ny * self.nz * self.own
        self.flat = 5 * channels * channels // LANES
        self.plane = self.nx * self.ny
        self.share = self.flat // (2 * self.plane)
        self.extra = 16


def nn(a, b):
    return lax.dot_general(a, b, (((1,), (0,)), ((), ())), preferred_element_type=F32)


def nt(a, b):
    return lax.dot_general(a, b, (((1,), (1,)), ((), ())), preferred_element_type=F32)


def tn(a, b):
    return lax.dot_general(a, b, (((0,), (0,)), ((), ())), preferred_element_type=F32)


def swap_matrix(plan, to_z):
    size = (plan.tile, plan.tile)
    row = lax.broadcasted_iota(jnp.int32, size, 0)
    col = lax.broadcasted_iota(jnp.int32, size, 1)
    za, az = (row, col) if to_z else (col, row)
    z, a, k = za // plan.msg, (za % plan.msg) // plan.own, za % plan.own
    return jnp.where(az == a * plan.blk + z * plan.own + k, 1.0, 0.0).astype(BF)


def place(plan):
    me = lax.axis_index("dap")
    return me // plan.nz, me % plan.nz


def signal(peer):
    pl.semaphore_signal(
        pltpu.get_barrier_semaphore(), inc=1, device_id=peer, device_id_type=pl.DeviceIdType.MESH
    )


def remote(src, dst, send, recv, peer):
    return pltpu.make_async_remote_copy(
        src_ref=src,
        dst_ref=dst,
        send_sem=send,
        recv_sem=recv,
        device_id=peer,
        device_id_type=pl.DeviceIdType.MESH,
    )


def loop(count, body):
    lax.fori_loop(0, count, lambda i, c: (body(i), c)[1], 0)


def keep(plan, put):
    for t in range(5):
        for half in range(2):
            start = (2 * t + half) * plan.c
            at = start
            while at < start + plan.c:
                s = at // plan.share
                end = min(start + plan.c, (s + 1) * plan.share)
                low = s * plan.share
                put(t, half, slice(at - start, end - start), s, slice(at - low, end - low))
                at = end


def summed(ref, count):
    out = ref[0].astype(F32)
    for i in range(1, count):
        out += ref[i].astype(F32)
    return out


def whole_kernel(
    plan, ext_ref, x_hbm, g_hbm, b_hbm, win_hbm, wout_hbm, gain_hbm,
    dr_out, db_out, win_out, wout_out, gain_out,
    x_in, g_in, b_in, win_ref, wout_ref, gain_ref,
    xg_s, xg_y, xg_zs, xg_z, b_z, bias_ref, ds_ref, ds_y, ds_n, ds_nin, ds_f, ds_fin,
    dr_s, dr_y, dr_zs, dr_z, wg, w_cin, w_p, w_pin, w_a, w_b, w_all,
    lsem, xy, xz, bf, bn, by, dy, dn, df, ry, rz, wc, wp, wa, wb, gp, gc,
):
    y, z = place(plan)
    crop = lax.axis_index("crop")
    cx, core = crop // 2, crop % 2
    ny, nz, nx, blk, qa, qb = plan.ny, plan.nz, plan.nx, plan.blk, plan.qa, plan.qb
    za, zb = z // qb, z % qb
    n, ch, msg = plan.n, plan.c, plan.msg
    share, extra, plane = plan.share, plan.extra, plan.plane
    spot = cx * ny + y

    def zpeer(i):
        step = (i + 1) // 2
        zp = lax.rem(z + nz // 2 + step * (1 - 2 * (i % 2)), nz)
        return zp, {"dap": y * nz + zp}

    def ypeer(i):
        yp = lax.rem(y + i + 1, ny)
        return yp, {"dap": yp * nz + z}

    def ppeer(i):
        to = lax.rem(spot + i + 1, plane)
        return to, {"crop": (to // ny) * 2 + core, "dap": (to % ny) * nz + z}

    def apeer(i):
        return {"dap": y * nz + lax.rem(za + i + 1, qa) * qb + zb}

    def bpeer(i):
        return {"dap": y * nz + za * qb + lax.rem(zb + i + 1, qb)}

    def xpeer(i):
        xp = lax.rem(cx + i // ny + 1, nx)
        return {"crop": xp * 2 + core, "dap": (i % ny) * nz + z}

    other = {"crop": cx * 2 + 1 - core}

    local = [
        pltpu.make_async_copy(s, d, lsem.at[i])
        for i, (s, d) in enumerate(
            [
                (b_hbm, b_in), (x_hbm, x_in), (g_hbm, g_in),
                (win_hbm, win_ref), (wout_hbm, wout_ref), (gain_hbm, gain_ref),
            ]
        )
    ]
    for c in local:
        c.start()
    loop(nz - 1, lambda i: signal(zpeer(i)[1]))
    for i in range(ny - 1):
        signal(ypeer(i)[1])
    loop(plane - ny, lambda i: signal(xpeer(i)))
    signal(other)
    for c in local[:3]:
        c.wait()
    b_z[:, za, zb] = b_in[...].reshape(plan.chunks, msg, n)
    xg_s[0] = x_in[...].reshape(ny, blk, ch)
    xg_s[1] = g_in[...].reshape(ny, blk, ch)
    to_y = swap_matrix(plan, False)
    to_z = swap_matrix(plan, True)
    pl.semaphore_wait(pltpu.get_barrier_semaphore(), nz + plane - 1)

    def b_far(i):
        part = b_z.at[:, za, zb]
        return remote(part, part, bf.at[0, i], bf.at[1, i], apeer(i))

    def b_near(i):
        part = b_z.at[:, :, zb]
        return remote(part, part, bn.at[0, i], bn.at[1, i], bpeer(i))

    mine = pl.ds(pl.multiple_of(y * blk, blk), blk)

    def b_y(c, i):
        part = bias_ref.at[pl.ds(c * ny, ny), mine]
        return remote(part, part, by.at[0, c, i], by.at[1, c, i], ypeer(i)[1])

    def x_y(i):
        yp, peer = ypeer(i)
        return remote(xg_s.at[:, yp], xg_y.at[:, y], xy.at[0, i], xy.at[1, i], peer)

    def x_z(i):
        zp, peer = zpeer(i)
        return remote(xg_zs.at[:, zp], xg_z.at[:, z], xz.at[0, i], xz.at[1, i], peer)

    for i in range(qa - 1):
        b_far(i).start()
    for i in range(ny - 1):
        x_y(i).start()
    xg_y[:, y] = xg_s[:, y]
    for i in range(ny - 1):
        x_y(i).wait_recv()
    for t in range(2):
        rows = nn(to_z, xg_y[t].reshape(plan.tile, ch)).astype(BF)
        xg_zs[t] = rows.reshape(nz, msg, ch)
    loop(nz - 1, lambda i: x_z(i).start())
    for i in range(qa - 1):
        b_far(i).wait_recv()
    for i in range(qb - 1):
        b_near(i).start()
    xg_z[:, z] = xg_zs[:, z]
    for i in range(qb - 1):
        b_near(i).wait_recv()
    for c in range(plan.chunks):
        rows = nn(to_y, b_z[c].reshape(plan.tile, n)).astype(BF)
        bias_ref[pl.ds(c * ny, ny), mine] = rows.reshape(ny, blk, n)
        for i in range(ny - 1):
            b_y(c, i).start()
    for c in local[3:]:
        c.wait()
    loop(nz - 1, lambda i: x_z(i).wait_recv())

    size = ch // plan.heads
    mult = 1.0 / math.sqrt(size)
    extent = ext_ref[0]
    gain = gain_ref[...]
    value = nn(to_y, xg_z[0].reshape(plan.tile, ch))
    upstream = nn(to_y, xg_z[1].reshape(plan.tile, ch))
    centred = value - jnp.mean(value, axis=-1, keepdims=True)
    inv_std = lax.rsqrt(jnp.mean(centred * centred, axis=-1, keepdims=True) + EPSILON)
    normal = centred * inv_std
    normed = (normal * gain).astype(BF)
    q, k, v, gl = [nn(normed, win_ref[p]).astype(BF) for p in range(4)]
    gate = jax.nn.sigmoid(gl.astype(F32))
    row_valid = lax.broadcasted_iota(jnp.int32, (n, ch), 0) < extent
    mg = jnp.where(row_valid, upstream, 0.0).astype(BF)
    d_gated = nt(mg, wout_ref[...])
    da = (d_gated * gate).astype(BF)
    col_valid = lax.broadcasted_iota(jnp.int32, (n, n), 1) < extent
    head_of = lax.broadcasted_iota(jnp.int32, (1, ch), 1) // size
    att = dv = dq = dk = jnp.zeros((n, ch), F32)

    def ds_ycopy(c, i):
        yp, peer = ypeer(i)
        part = ds_ref.at[pl.ds(c * ny, ny), yp]
        return remote(part, ds_y.at[c, i], dy.at[0, c, i], dy.at[1, c, i], peer)

    for h in range(plan.heads):
        if h % ny == 0:
            for i in range(ny - 1):
                b_y(h // ny, i).wait_recv()
        own = jnp.where(head_of == h, 1.0, 0.0).astype(BF)
        qh, kh, vh, dah = q * own, k * own, v * own, da * own
        scores = nt(qh, k) * mult + bias_ref[h].astype(F32)
        scores = jnp.where(col_valid, scores, MASKED)
        expo = jnp.exp(scores - jnp.max(scores, axis=-1, keepdims=True))
        probs = expo * (1.0 / jnp.sum(expo, axis=-1, keepdims=True))
        pb = probs.astype(BF)
        d_probs = nt(dah, v)
        total = jnp.sum(probs * d_probs, axis=-1, keepdims=True)
        dsb = (probs * (d_probs - total)).astype(BF)
        ds_ref[h] = dsb.reshape(ny, blk, n)
        att += nn(pb, vh)
        dv += tn(pb, dah)
        dq += nn(dsb, kh)
        dk += tn(dsb, qh)
        if h % ny == ny - 1:
            for i in range(ny - 1):
                ds_ycopy(h // ny, i).start()
    gated = (att * gate).astype(BF)
    grads = [
        (dq * mult).astype(BF),
        (dk * mult).astype(BF),
        dv.astype(BF),
        (d_gated * att * gate * (1.0 - gate)).astype(BF),
    ]
    d_normed = jnp.zeros((n, ch), F32)
    for p in range(4):
        d_normed += nt(grads[p], win_ref[p])
    terms = [tn(normed, grads[p]).astype(BF) for p in range(4)] + [tn(gated, mg).astype(BF)]

    def put(t, half, rows, s, at):
        wg[s // plane, s % plane, at] = terms[t][rows, half * LANES : (half + 1) * LANES]

    keep(plan, put)
    d_gain = jnp.sum(d_normed * normal, axis=0, keepdims=True)
    line = lax.broadcasted_iota(jnp.int32, (extra, LANES), 0)
    lo = jnp.broadcast_to(d_gain[:, :LANES], (extra, LANES))
    hi = jnp.broadcast_to(d_gain[:, LANES:], (extra, LANES))
    block = jnp.where(line == 0, lo, jnp.where(line == 1, hi, 0.0)).astype(BF)
    for core_of in range(2):
        wg[core_of, :, share:] = jnp.broadcast_to(block[None], (plane, extra, LANES))

    def w_core():
        return remote(wg.at[1 - core], w_cin, wc.at[0], wc.at[1], other)

    def w_pcopy(i):
        to, peer = ppeer(i)
        return remote(w_p.at[to], w_pin.at[spot], wp.at[0, i], wp.at[1, i], peer)

    def w_acopy(i):
        return remote(w_a.at[zb], w_a.at[zb], wa.at[0, i], wa.at[1, i], bpeer(i))

    def w_bcopy(i):
        return remote(w_b.at[za], w_b.at[za], wb.at[0, i], wb.at[1, i], apeer(i))

    def g_p(i):
        part = w_all.at[core, spot]
        return remote(part, part, gp.at[0, i], gp.at[1, i], ppeer(i)[1])

    def g_core():
        part = w_all.at[core]
        return remote(part, part, gc.at[0], gc.at[1], other)

    def dr_ycopy(i):
        yp, peer = ypeer(i)
        return remote(dr_s.at[yp], dr_y.at[y], ry.at[0, i], ry.at[1, i], peer)

    def dr_zcopy(i):
        zp, peer = zpeer(i)
        return remote(dr_zs.at[zp], dr_z.at[z], rz.at[0, i], rz.at[1, i], peer)

    def ds_near(c, i):
        bp = lax.rem(zb + i + 1, qb)
        part = ds_n.at[c, :, bp]
        return remote(part, ds_nin.at[c, i], dn.at[0, c, i], dn.at[1, c, i], bpeer(i))

    def ds_far(i):
        ap = lax.rem(za + i + 1, qa)
        return remote(ds_f.at[:, ap], ds_fin.at[:, i], df.at[0, i], df.at[1, i], apeer(i))

    def fold(c):
        for i in range(ny - 1):
            ds_ycopy(c, i).wait_recv()
        total = ds_ref[pl.ds(c * ny, ny), y].astype(F32)
        for i in range(ny - 1):
            total += ds_y[c, i].astype(F32)
        rows = nn(to_z, total.astype(BF).reshape(plan.tile, n)).astype(BF)
        ds_n[c] = rows.reshape(qa, qb, msg, n)
        for i in range(qb - 1):
            ds_near(c, i).start()

    w_core().start()
    scaled = d_normed * gain
    d_row = inv_std * (
        scaled
        - jnp.mean(scaled, axis=-1, keepdims=True)
        - normal * jnp.mean(scaled * normal, axis=-1, keepdims=True)
    )
    dr_s[...] = d_row.astype(BF).reshape(ny, blk, ch)
    for i in range(ny - 1):
        dr_ycopy(i).start()
    dr_y[y] = dr_s[y]

    w_core().wait_recv()
    w_p[...] = (wg[core].astype(F32) + w_cin[...].astype(F32)).astype(BF)
    loop(plane - 1, lambda i: w_pcopy(i).start())
    w_pin[spot] = w_p[spot]

    half = (plan.chunks + 1) // 2
    for c in range(half):
        fold(c)
    for i in range(ny - 1):
        dr_ycopy(i).wait_recv()
    rows = nn(to_z, dr_y[...].reshape(plan.tile, ch)).astype(BF)
    dr_zs[...] = rows.reshape(nz, msg, ch)
    loop(nz - 1, lambda i: dr_zcopy(i).start())
    dr_z[z] = dr_zs[z]
    for c in range(half, plan.chunks):
        fold(c)

    loop(plane - 1, lambda i: w_pcopy(i).wait_recv())
    w_a[zb] = summed(w_pin, plane).astype(BF)
    for i in range(qb - 1):
        w_acopy(i).start()
    for c in range(plan.chunks):
        for i in range(qb - 1):
            ds_near(c, i).wait_recv()
        total = ds_n[c, :, zb].astype(F32)
        for i in range(qb - 1):
            total += ds_nin[c, i].astype(F32)
        ds_f[c] = total.astype(BF)
    for i in range(qa - 1):
        ds_far(i).start()
    for i in range(qb - 1):
        w_acopy(i).wait_recv()
    w_b[za] = summed(w_a, qb).astype(BF)
    for i in range(qa - 1):
        w_bcopy(i).start()
    for i in range(qa - 1):
        w_bcopy(i).wait_recv()
    scale = 1.0 / (plan.nc * plan.dap)
    total = summed(w_b, qa)
    w_all[core, spot] = total[:share].astype(BF)
    loop(plane - 1, lambda i: g_p(i).start())
    gain_out[...] = total[share:] * scale
    loop(nz - 1, lambda i: dr_zcopy(i).wait_recv())
    rows = nn(to_y, dr_z[...].reshape(plan.tile, ch)).astype(BF)
    dr_out[...] = rows.reshape(plan.dap, plan.own, ch)
    for i in range(qa - 1):
        ds_far(i).wait_recv()
    total = ds_f[:, za].astype(F32)
    for i in range(qa - 1):
        total += ds_fin[:, i].astype(F32)
    db_out[...] = total.reshape(plan.heads, plan.own, n)
    loop(plane - 1, lambda i: g_p(i).wait_recv())
    g_core().start()

    def take(t, half, rows, s, at):
        part = w_all[s // plane, s % plane, at].astype(F32) * scale
        cols = slice(half * LANES, (half + 1) * LANES)
        if t < 4:
            win_out[t, rows, cols] = part
        else:
            wout_out[rows, cols] = part

    for i in range(qa - 1):
        b_far(i).wait_send()
        w_bcopy(i).wait_send()
        ds_far(i).wait_send()
    for i in range(qb - 1):
        b_near(i).wait_send()
        w_acopy(i).wait_send()
        for c in range(plan.chunks):
            ds_near(c, i).wait_send()
    for i in range(ny - 1):
        x_y(i).wait_send()
        dr_ycopy(i).wait_send()
        for c in range(plan.chunks):
            b_y(c, i).wait_send()
            ds_ycopy(c, i).wait_send()
    loop(plane - 1, lambda i: w_pcopy(i).wait_send())
    loop(plane - 1, lambda i: g_p(i).wait_send())
    w_core().wait_send()
    loop(nz - 1, lambda i: x_z(i).wait_send())
    loop(nz - 1, lambda i: dr_zcopy(i).wait_send())
    g_core().wait_recv()
    g_core().wait_send()
    keep(plan, take)


def dma(*shape):
    return pltpu.SemaphoreType.DMA(shape)


def on_device(plan, x, upstream, bias, extents, w_in, w_final, gain):
    ny, nz, n, ch = plan.ny, plan.nz, plan.n, plan.c
    msg, blk, chunks, heads = plan.msg, plan.blk, plan.chunks, plan.heads
    total, plane = plan.share + plan.extra, plan.plane

    def buf(*shape, kind=BF):
        return pltpu.VMEM(shape, kind)

    d_rows, d_bias, d_in, d_out, gain_sum = pl.pallas_call(
        functools.partial(whole_kernel, plan),
        out_shape=(
            jax.ShapeDtypeStruct((plan.dap, plan.own, ch), BF),
            jax.ShapeDtypeStruct((heads, plan.own, n), F32),
            jax.ShapeDtypeStruct((4, ch, ch), F32),
            jax.ShapeDtypeStruct((ch, ch), F32),
            jax.ShapeDtypeStruct((plan.extra, LANES), F32),
        ),
        in_specs=[SMEM] + [ANY] * 6,
        out_specs=(VMEM,) * 5,
        scratch_shapes=[
            buf(plan.dap, plan.own, ch),
            buf(plan.dap, plan.own, ch),
            buf(heads, plan.own, n),
            buf(4, ch, ch),
            buf(ch, ch),
            buf(1, ch, kind=F32),
            buf(2, ny, blk, ch),
            buf(2, ny, blk, ch),
            buf(2, nz, msg, ch),
            buf(2, nz, msg, ch),
            buf(chunks, plan.qa, plan.qb, msg, n),
            buf(heads, n, n),
            buf(heads, ny, blk, n),
            buf(chunks, ny - 1, ny, blk, n),
            buf(chunks, plan.qa, plan.qb, msg, n),
            buf(chunks, plan.qb - 1, plan.qa, msg, n),
            buf(chunks, plan.qa, msg, n),
            buf(chunks, plan.qa - 1, msg, n),
            buf(ny, blk, ch),
            buf(ny, blk, ch),
            buf(nz, msg, ch),
            buf(nz, msg, ch),
            buf(2, plane, total, LANES),
            buf(plane, total, LANES),
            buf(plane, total, LANES),
            buf(plane, total, LANES),
            buf(plan.qb, total, LANES),
            buf(plan.qa, total, LANES),
            buf(2, plane, plan.share, LANES),
            dma(6),
            dma(2, ny - 1),
            dma(2, nz - 1),
            dma(2, plan.qa - 1),
            dma(2, plan.qb - 1),
            dma(2, chunks, ny - 1),
            dma(2, chunks, ny - 1),
            dma(2, chunks, plan.qb - 1),
            dma(2, plan.qa - 1),
            dma(2, ny - 1),
            dma(2, nz - 1),
            dma(2),
            dma(2, plane - 1),
            dma(2, plan.qb - 1),
            dma(2, plan.qa - 1),
            dma(2, plane - 1),
            dma(2),
        ],
        compiler_params=pltpu.CompilerParams(
            collective_id=0, has_side_effects=True, vmem_limit_bytes=LIMIT
        ),
        name="row_attention_gradients",
    )(
        extents, x[0], upstream[0], bias[0], w_in, w_final, gain.reshape(1, ch)
    )
    return (
        d_rows[None],
        d_bias[None],
        d_in,
        d_out,
        gain_sum[:2].reshape(ch),
    )


def solution(mesh):
    split = P("crop", None, "dap", None)

    def whole(*arrays):
        plan = Plan(mesh, arrays[0].shape[2], arrays[0].shape[3], arrays[2].shape[1])
        return jax.shard_map(
            functools.partial(on_device, plan),
            mesh=mesh,
            in_specs=(split, split, split, P("crop"), P(), P(), P()),
            out_specs=(split, split, P(), P(), P()),
            check_vma=False,
        )(*arrays)

    return whole
```

```python
import functools
import math

import jax
import jax.numpy as jnp
from jax import lax
from jax.experimental import pallas as pl
from jax.experimental.pallas import tpu as pltpu
from jax.sharding import PartitionSpec as P

EPSILON = 1e-05
MASKED = -1000000000.0
LANES = 128
BF = jnp.bfloat16
F32 = jnp.float32
ANY = pl.BlockSpec(memory_space=pl.ANY)
VMEM = pl.BlockSpec(memory_space=pltpu.VMEM)
SMEM = pl.BlockSpec(memory_space=pltpu.SMEM)
LIMIT = 60 * 1024 * 1024
EARLY = 5


class Plan:
    def __init__(self, mesh, residues, channels, heads):
        self.nc = mesh.shape["crop"]
        self.nx = self.nc // 2
        dap = mesh.shape["dap"]
        self.ny = 4 if dap >= 16 else 2
        self.nz = dap // self.ny
        self.qb = 4 if self.nz >= 16 else 2
        self.qa = self.nz // self.qb
        self.dap = dap
        self.n = residues
        self.c = channels
        self.heads = heads
        self.own = residues // dap
        self.msg = self.ny * self.own
        self.blk = self.nz * self.own
        self.chunks = heads // self.ny
        self.tile = self.ny * self.nz * self.own
        self.flat = 5 * channels * channels // LANES
        self.plane = self.nx * self.ny
        self.share = self.flat // (2 * self.plane)
        self.extra = 16


def nn(a, b):
    return lax.dot_general(a, b, (((1,), (0,)), ((), ())), preferred_element_type=F32)


def nt(a, b):
    return lax.dot_general(a, b, (((1,), (1,)), ((), ())), preferred_element_type=F32)


def tn(a, b):
    return lax.dot_general(a, b, (((0,), (0,)), ((), ())), preferred_element_type=F32)


def swap_matrix(plan, to_z):
    size = (plan.tile, plan.tile)
    row = lax.broadcasted_iota(jnp.int32, size, 0)
    col = lax.broadcasted_iota(jnp.int32, size, 1)
    za, az = (row, col) if to_z else (col, row)
    z, a, k = za // plan.msg, (za % plan.msg) // plan.own, za % plan.own
    return jnp.where(az == a * plan.blk + z * plan.own + k, 1.0, 0.0).astype(BF)


def place(plan):
    me = lax.axis_index("dap")
    return me // plan.nz, me % plan.nz


def signal(peer):
    pl.semaphore_signal(
        pltpu.get_barrier_semaphore(), inc=1, device_id=peer, device_id_type=pl.DeviceIdType.MESH
    )


def remote(src, dst, send, recv, peer):
    return pltpu.make_async_remote_copy(
        src_ref=src,
        dst_ref=dst,
        send_sem=send,
        recv_sem=recv,
        device_id=peer,
        device_id_type=pl.DeviceIdType.MESH,
    )


class Exchange:
    def __init__(self, make, count, like, sems):
        self.make, self.count, self.like, self.sems = make, count, like, sems

    def start(self, low=0, high=None):
        for i in range(low, self.count if high is None else high):
            src, dst, peer = self.make(i)
            remote(src, dst, self.sems.at[0], self.sems.at[1], peer).start()

    def received(self):
        pltpu.make_async_copy(self.like, self.like, self.sems.at[1]).wait()

    def sent(self):
        pltpu.make_async_copy(self.like, self.like, self.sems.at[0]).wait()


def keep(plan, put):
    for t in range(5):
        for half in range(2):
            start = (2 * t + half) * plan.c
            at = start
            while at < start + plan.c:
                s = at // plan.share
                end = min(start + plan.c, (s + 1) * plan.share)
                low = s * plan.share
                put(t, half, slice(at - start, end - start), s, slice(at - low, end - low))
                at = end


def summed(ref, count):
    out = ref[0].astype(F32)
    for i in range(1, count):
        out += ref[i].astype(F32)
    return out


def whole_kernel(
    plan, ext_ref, x_hbm, g_hbm, b_hbm, win_hbm, wout_hbm, gain_hbm,
    dr_out, db_out, w_all, gain_out,
    x_in, g_in, b_in, win_ref, wout_ref, gain_ref,
    xg_s, xg_y, xg_zs, xg_z, b_z, bias_ref, ds_ref, ds_y, z_out, z_in,
    dr_s, dr_y, wg, w_cin, w_p, w_pin, w_a, w_b,
    lsem, xy, xz, bf, bn, by, dy, z1, z2, ry, wc, wp, wa, wb, gp, gc,
):
    y, z = place(plan)
    crop = lax.axis_index("crop")
    cx, core = crop // 2, crop % 2
    ny, nz, nx, blk, qa, qb = plan.ny, plan.nz, plan.nx, plan.blk, plan.qa, plan.qb
    za, zb = z // qb, z % qb
    n, ch, msg = plan.n, plan.c, plan.msg
    share, extra, plane = plan.share, plan.extra, plan.plane
    spot = cx * ny + y

    def zpeer(i):
        step = (i + 1) // 2
        zp = lax.rem(z + nz // 2 + step * (1 - 2 * (i % 2)), nz)
        return zp, {"dap": y * nz + zp}

    def ypeer(i):
        yp = lax.rem(y + i + 1, ny)
        return yp, {"dap": yp * nz + z}

    def ppeer(i):
        to = lax.rem(spot + i + 1, plane)
        return to, {"crop": (to // ny) * 2 + core, "dap": (to % ny) * nz + z}

    def apeer(i):
        return {"dap": y * nz + lax.rem(za + i + 1, qa) * qb + zb}

    def bpeer(i):
        return {"dap": y * nz + za * qb + lax.rem(zb + i + 1, qb)}

    def xpeer(i):
        xp = lax.rem(cx + i // ny + 1, nx)
        return {"crop": xp * 2 + core, "dap": (i % ny) * nz + z}

    other = {"crop": cx * 2 + 1 - core}

    local = [
        pltpu.make_async_copy(s, d, lsem.at[i])
        for i, (s, d) in enumerate(
            [
                (b_hbm, b_in), (x_hbm, x_in), (g_hbm, g_in),
                (win_hbm, win_ref), (wout_hbm, wout_ref), (gain_hbm, gain_ref),
            ]
        )
    ]
    for c in local:
        c.start()
    for i in range(nz - 1):
        signal(zpeer(i)[1])
    for i in range(ny - 1):
        signal(ypeer(i)[1])
    for i in range(plane - ny):
        signal(xpeer(i))
    signal(other)
    for c in local[:3]:
        c.wait()
    b_z[:, za, zb] = b_in[...].reshape(plan.chunks, msg, n)
    xg_s[0] = x_in[...].reshape(ny, blk, ch)
    xg_s[1] = g_in[...].reshape(ny, blk, ch)
    to_y = swap_matrix(plan, False)
    to_z = swap_matrix(plan, True)
    pl.semaphore_wait(pltpu.get_barrier_semaphore(), nz + plane - 1)

    def b_far(i):
        part = b_z.at[:, za, zb]
        return part, part, apeer(i)

    def b_near(i):
        part = b_z.at[:, :, zb]
        return part, part, bpeer(i)

    mine = pl.ds(pl.multiple_of(y * blk, blk), blk)

    def bias_y(c):
        heads = pl.ds(c * ny, ny)

        def b_y(i):
            part = bias_ref.at[heads, mine]
            return part, part, ypeer(i)[1]

        return Exchange(b_y, ny - 1, bias_ref.at[heads, pl.ds(0, (ny - 1) * blk)], by.at[c])

    def x_y(i):
        yp, peer = ypeer(i)
        return xg_s.at[:, yp], xg_y.at[:, y], peer

    def x_z(i):
        zp, peer = zpeer(i)
        return xg_zs.at[:, zp], xg_z.at[:, z], peer

    far = Exchange(b_far, qa - 1, b_z.at[:, pl.ds(0, qa - 1), 0], bf)
    near = Exchange(b_near, qb - 1, b_z.at[:, :, pl.ds(0, qb - 1)], bn)
    by_y = [bias_y(c) for c in range(plan.chunks)]
    rows_y = Exchange(x_y, ny - 1, xg_y.at[:, pl.ds(0, ny - 1)], xy)
    rows_z = Exchange(x_z, nz - 1, xg_z.at[:, pl.ds(0, nz - 1)], xz)

    far.start()
    rows_y.start()
    xg_y[:, y] = xg_s[:, y]
    rows_y.received()
    for t in range(2):
        rows = nn(to_z, xg_y[t].reshape(plan.tile, ch)).astype(BF)
        xg_zs[t] = rows.reshape(nz, msg, ch)
    early = EARLY * (nz - 1) // 15
    rows_z.start(0, early)
    far.received()
    near.start()
    rows_z.start(early)
    xg_z[:, z] = xg_zs[:, z]
    near.received()
    for c in range(plan.chunks):
        rows = nn(to_y, b_z[c].reshape(plan.tile, n)).astype(BF)
        bias_ref[pl.ds(c * ny, ny), mine] = rows.reshape(ny, blk, n)
        by_y[c].start()
    for c in local[3:]:
        c.wait()
    rows_z.received()

    size = ch // plan.heads
    mult = 1.0 / math.sqrt(size)
    extent = ext_ref[0]
    gain = gain_ref[...]
    value = nn(to_y, xg_z[0].reshape(plan.tile, ch))
    upstream = nn(to_y, xg_z[1].reshape(plan.tile, ch))
    centred = value - jnp.mean(value, axis=-1, keepdims=True)
    inv_std = lax.rsqrt(jnp.mean(centred * centred, axis=-1, keepdims=True) + EPSILON)
    normal = centred * inv_std
    normed = (normal * gain).astype(BF)
    q, k, v, gl = [nn(normed, win_ref[p]).astype(BF) for p in range(4)]
    gate = jax.nn.sigmoid(gl.astype(F32))
    row_valid = lax.broadcasted_iota(jnp.int32, (n, ch), 0) < extent
    mg = jnp.where(row_valid, upstream, 0.0).astype(BF)
    d_gated = nt(mg, wout_ref[...])
    da = (d_gated * gate).astype(BF)
    col_valid = lax.broadcasted_iota(jnp.int32, (n, n), 1) < extent
    head_of = lax.broadcasted_iota(jnp.int32, (1, ch), 1) // size
    att = dv = dq = dk = jnp.zeros((n, ch), F32)

    def scores_y(c):
        def ds_y_(i):
            yp, peer = ypeer(i)
            return ds_ref.at[pl.ds(c * ny, ny), yp], ds_y.at[c, i], peer

        return Exchange(ds_y_, ny - 1, ds_y.at[c], dy.at[c])

    ds_by_y = [scores_y(c) for c in range(plan.chunks)]
    for h in range(plan.heads):
        if h % ny == 0:
            by_y[h // ny].received()
        own = jnp.where(head_of == h, 1.0, 0.0).astype(BF)
        qh, kh, vh, dah = q * own, k * own, v * own, da * own
        scores = nt(qh, k) * mult + bias_ref[h].astype(F32)
        scores = jnp.where(col_valid, scores, MASKED)
        expo = jnp.exp(scores - jnp.max(scores, axis=-1, keepdims=True))
        probs = expo * (1.0 / jnp.sum(expo, axis=-1, keepdims=True))
        pb = probs.astype(BF)
        d_probs = nt(dah, v)
        total = jnp.sum(probs * d_probs, axis=-1, keepdims=True)
        dsb = (probs * (d_probs - total)).astype(BF)
        ds_ref[h] = dsb.reshape(ny, blk, n)
        att += nn(pb, vh)
        dv += tn(pb, dah)
        dq += nn(dsb, kh)
        dk += tn(dsb, qh)
        if h % ny == ny - 1 and h < plan.heads - 1:
            ds_by_y[h // ny].start()
    gated = (att * gate).astype(BF)
    grads = [
        (dq * mult).astype(BF),
        (dk * mult).astype(BF),
        dv.astype(BF),
        (d_gated * att * gate * (1.0 - gate)).astype(BF),
    ]
    d_normed = jnp.zeros((n, ch), F32)
    for p in range(4):
        d_normed += nt(grads[p], win_ref[p])
    terms = [tn(normed, grads[p]).astype(BF) for p in range(4)] + [tn(gated, mg).astype(BF)]

    def put(t, half, rows, s, at):
        wg[s // plane, s % plane, at] = terms[t][rows, half * LANES : (half + 1) * LANES]

    keep(plan, put)
    d_gain = jnp.sum(d_normed * normal, axis=0, keepdims=True)
    line = lax.broadcasted_iota(jnp.int32, (extra, LANES), 0)
    lo = jnp.broadcast_to(d_gain[:, :LANES], (extra, LANES))
    hi = jnp.broadcast_to(d_gain[:, LANES:], (extra, LANES))
    block = jnp.where(line == 0, lo, jnp.where(line == 1, hi, 0.0)).astype(BF)
    for core_of in range(2):
        wg[core_of, :, share:] = jnp.broadcast_to(block[None], (plane, extra, LANES))

    def w_c(i):
        return wg.at[1 - core], w_cin, other

    def w_plane(i):
        to, peer = ppeer(i)
        return w_p.at[to], w_pin.at[spot], peer

    def w_near(i):
        return w_a.at[zb], w_a.at[zb], bpeer(i)

    def w_far(i):
        return w_b.at[za], w_b.at[za], apeer(i)

    def g_plane(i):
        part = w_all.at[core, spot]
        return part, part, ppeer(i)[1]

    def g_core(i):
        return w_all.at[core], w_all.at[core], other

    by_core = Exchange(w_c, 1, w_cin, wc)
    by_plane = Exchange(w_plane, plane - 1, w_pin.at[pl.ds(0, plane - 1)], wp)
    by_near = Exchange(w_near, qb - 1, w_a.at[pl.ds(0, qb - 1)], wa)
    by_far = Exchange(w_far, qa - 1, w_b.at[pl.ds(0, qa - 1)], wb)
    to_plane = Exchange(g_plane, plane - 1, w_all.at[0, pl.ds(0, plane - 1)], gp)
    to_core = Exchange(g_core, 1, w_all.at[0], gc)

    def dr_y_(i):
        yp, peer = ypeer(i)
        return dr_s.at[yp], dr_y.at[y], peer

    def first_z(i):
        zp, peer = zpeer(i)
        return z_out.at[zp, pl.ds(0, half)], z_in.at[z, pl.ds(0, half)], peer

    def last_z(i):
        zp, peer = zpeer(i)
        part = pl.ds(half, plan.chunks + 1 - half)
        return z_out.at[zp, part], z_in.at[z, part], peer

    half = plan.chunks // 2
    others = pl.ds(0, nz - 1)
    dr_by_y = Exchange(dr_y_, ny - 1, dr_y.at[pl.ds(0, ny - 1)], ry)
    z_first = Exchange(first_z, nz - 1, z_in.at[others, pl.ds(0, half)], z1)
    z_last = Exchange(last_z, nz - 1, z_in.at[others, pl.ds(half, plan.chunks + 1 - half)], z2)

    def fold(c):
        ds_by_y[c].received()
        total = ds_ref[pl.ds(c * ny, ny), y].astype(F32)
        for i in range(ny - 1):
            total += ds_y[c, i].astype(F32)
        rows = nn(to_z, total.astype(BF).reshape(plan.tile, n)).astype(BF)
        z_out[:, c] = rows.reshape(nz, msg, n)

    by_core.start()
    ds_by_y[-1].start()
    scaled = d_normed * gain
    d_row = inv_std * (
        scaled
        - jnp.mean(scaled, axis=-1, keepdims=True)
        - normal * jnp.mean(scaled * normal, axis=-1, keepdims=True)
    )
    dr_s[...] = d_row.astype(BF).reshape(ny, blk, ch)
    dr_by_y.start()
    dr_y[y] = dr_s[y]

    by_core.received()
    w_p[...] = (wg[core].astype(F32) + w_cin[...].astype(F32)).astype(BF)
    by_plane.start()
    w_pin[spot] = w_p[spot]
    for c in range(half):
        fold(c)
    z_first.start()
    for c in range(half, plan.chunks):
        fold(c)
    dr_by_y.received()
    rows = nn(to_z, dr_y[...].reshape(plan.tile, ch)).astype(BF)
    z_out[:, plan.chunks] = rows.reshape(nz, msg, ch)
    z_last.start()
    z_in[z] = z_out[z]

    by_plane.received()
    w_a[zb] = summed(w_pin, plane).astype(BF)
    by_near.start()
    by_near.received()
    w_b[za] = summed(w_a, qb).astype(BF)
    by_far.start()
    by_far.received()
    scale = 1.0 / (plan.nc * plan.dap)
    total = summed(w_b, qa)
    w_all[core, spot] = total[:share].astype(BF)
    to_plane.start()
    gain_out[...] = total[share:] * scale
    z_first.received()
    z_last.received()
    for c in range(plan.chunks):
        total = z_in[0, c].astype(F32)
        for i in range(1, nz):
            total += z_in[i, c].astype(F32)
        db_out[c] = total
    rows = nn(to_y, z_in[:, plan.chunks].reshape(plan.tile, ch)).astype(BF)
    dr_out[...] = rows
    to_plane.received()
    to_core.start()

    exchanges = [far, near, *by_y, rows_y, rows_z, *ds_by_y, by_core, by_plane, by_near, by_far]
    for e in exchanges + [to_plane, dr_by_y, z_first, z_last]:
        e.sent()
    to_core.received()
    to_core.sent()


def unpack_kernel(
    plan, dr_ref, db_ref, w_all, gain_ref, dr_out, db_out, win_out, wout_out, gain_out
):
    scale = 1.0 / (plan.nc * plan.dap)
    dr_out[...] = dr_ref[...].reshape(dr_out.shape)
    db_out[...] = db_ref[...].reshape(db_out.shape)
    gain_out[:, :LANES] = gain_ref[0:1]
    gain_out[:, LANES:] = gain_ref[1:2]

    def take(t, half, rows, s, at):
        part = w_all[s // plan.plane, s % plan.plane, at].astype(F32) * scale
        cols = slice(half * LANES, (half + 1) * LANES)
        if t < 4:
            win_out[t, rows, cols] = part
        else:
            wout_out[rows, cols] = part

    keep(plan, take)


def dma(*shape):
    return pltpu.SemaphoreType.DMA(shape)


def on_device(plan, x, upstream, bias, extents, w_in, w_final, gain):
    ny, nz, n, ch = plan.ny, plan.nz, plan.n, plan.c
    msg, blk, chunks, heads = plan.msg, plan.blk, plan.chunks, plan.heads
    total, plane = plan.share + plan.extra, plan.plane

    def buf(*shape, kind=BF):
        return pltpu.VMEM(shape, kind)

    sums = pl.pallas_call(
        functools.partial(whole_kernel, plan),
        out_shape=(
            jax.ShapeDtypeStruct((n, ch), BF),
            jax.ShapeDtypeStruct((chunks, msg, n), F32),
            jax.ShapeDtypeStruct((2, plane, plan.share, LANES), BF),
            jax.ShapeDtypeStruct((plan.extra, LANES), F32),
        ),
        in_specs=[SMEM] + [ANY] * 6,
        out_specs=(VMEM,) * 4,
        scratch_shapes=[
            buf(plan.dap, plan.own, ch),
            buf(plan.dap, plan.own, ch),
            buf(heads, plan.own, n),
            buf(4, ch, ch),
            buf(ch, ch),
            buf(1, ch, kind=F32),
            buf(2, ny, blk, ch),
            buf(2, ny, blk, ch),
            buf(2, nz, msg, ch),
            buf(2, nz, msg, ch),
            buf(chunks, plan.qa, plan.qb, msg, n),
            buf(heads, n, n),
            buf(heads, ny, blk, n),
            buf(chunks, ny - 1, ny, blk, n),
            buf(nz, chunks + 1, msg, n),
            buf(nz, chunks + 1, msg, n),
            buf(ny, blk, ch),
            buf(ny, blk, ch),
            buf(2, plane, total, LANES),
            buf(plane, total, LANES),
            buf(plane, total, LANES),
            buf(plane, total, LANES),
            buf(plan.qb, total, LANES),
            buf(plan.qa, total, LANES),
            dma(6),
            dma(2),
            dma(2),
            dma(2),
            dma(2),
            dma(chunks, 2),
            dma(chunks, 2),
            *[dma(2)] * 9,
        ],
        compiler_params=pltpu.CompilerParams(
            collective_id=0, has_side_effects=True, vmem_limit_bytes=LIMIT
        ),
        name="row_attention_gradients",
    )(
        extents, x[0], upstream[0], bias[0], w_in, w_final, gain.reshape(1, ch)
    )
    d_rows, d_bias, d_in, d_out, d_gain = pl.pallas_call(
        functools.partial(unpack_kernel, plan),
        out_shape=(
            jax.ShapeDtypeStruct((plan.dap, plan.own, ch), BF),
            jax.ShapeDtypeStruct((heads, plan.own, n), F32),
            jax.ShapeDtypeStruct((4, ch, ch), F32),
            jax.ShapeDtypeStruct((ch, ch), F32),
            jax.ShapeDtypeStruct((1, ch), F32),
        ),
        in_specs=[VMEM] * 4,
        out_specs=(VMEM,) * 5,
        compiler_params=pltpu.CompilerParams(vmem_limit_bytes=LIMIT),
        name="unpack_gradients",
    )(*sums)
    return (d_rows[None], d_bias[None], d_in, d_out, d_gain.reshape(ch))


def solution(mesh):
    split = P("crop", None, "dap", None)

    def whole(*arrays):
        plan = Plan(mesh, arrays[0].shape[2], arrays[0].shape[3], arrays[2].shape[1])
        return jax.shard_map(
            functools.partial(on_device, plan),
            mesh=mesh,
            in_specs=(split, split, split, P("crop"), P(), P(), P()),
            out_specs=(split, split, P(), P(), P()),
            check_vma=False,
        )(*arrays)

    return whole
```

```python
import functools
import math

import jax
import jax.numpy as jnp
from jax import lax
from jax.experimental import pallas as pl
from jax.experimental.pallas import tpu as pltpu
from jax.sharding import PartitionSpec as P

EPSILON = 1e-05
MASKED = -1000000000.0
LANES = 128
BF = jnp.bfloat16
F32 = jnp.float32
ANY = pl.BlockSpec(memory_space=pl.ANY)
VMEM = pl.BlockSpec(memory_space=pltpu.VMEM)
SMEM = pl.BlockSpec(memory_space=pltpu.SMEM)
LIMIT = 60 * 1024 * 1024


class Plan:
    def __init__(self, mesh, residues, channels, heads):
        self.nc = mesh.shape["crop"]
        self.nx = self.nc // 2
        dap = mesh.shape["dap"]
        self.ny = 4 if dap >= 16 else 2
        self.nz = dap // self.ny
        self.qb = 4 if self.nz >= 16 else 2
        self.qa = self.nz // self.qb
        self.dap = dap
        self.n = residues
        self.c = channels
        self.heads = heads
        self.own = residues // dap
        self.msg = self.ny * self.own
        self.blk = self.nz * self.own
        self.chunks = heads // self.ny
        self.tile = self.ny * self.nz * self.own
        self.flat = 5 * channels * channels // LANES
        self.plane = self.nx * self.ny
        self.share = self.flat // (2 * self.plane)
        self.extra = 16


def nn(a, b):
    return lax.dot_general(a, b, (((1,), (0,)), ((), ())), preferred_element_type=F32)


def nt(a, b):
    return lax.dot_general(a, b, (((1,), (1,)), ((), ())), preferred_element_type=F32)


def tn(a, b):
    return lax.dot_general(a, b, (((0,), (0,)), ((), ())), preferred_element_type=F32)


def swap_matrix(plan, to_z):
    size = (plan.tile, plan.tile)
    row = lax.broadcasted_iota(jnp.int32, size, 0)
    col = lax.broadcasted_iota(jnp.int32, size, 1)
    za, az = (row, col) if to_z else (col, row)
    z, a, k = za // plan.msg, (za % plan.msg) // plan.own, za % plan.own
    return jnp.where(az == a * plan.blk + z * plan.own + k, 1.0, 0.0).astype(BF)


def place(plan):
    me = lax.axis_index("dap")
    return me // plan.nz, me % plan.nz


def signal(peer):
    pl.semaphore_signal(
        pltpu.get_barrier_semaphore(), inc=1, device_id=peer, device_id_type=pl.DeviceIdType.MESH
    )


def remote(src, dst, send, recv, peer):
    return pltpu.make_async_remote_copy(
        src_ref=src,
        dst_ref=dst,
        send_sem=send,
        recv_sem=recv,
        device_id=peer,
        device_id_type=pl.DeviceIdType.MESH,
    )


class Exchange:
    def __init__(self, make, count, like, sems):
        self.make, self.count, self.like, self.sems = make, count, like, sems

    def start(self, low=0, high=None):
        for i in range(low, self.count if high is None else high):
            src, dst, peer = self.make(i)
            remote(src, dst, self.sems.at[0], self.sems.at[1], peer).start()

    def received(self):
        pltpu.make_async_copy(self.like, self.like, self.sems.at[1]).wait()

    def sent(self):
        pltpu.make_async_copy(self.like, self.like, self.sems.at[0]).wait()


def keep(plan, put):
    for t in range(5):
        for half in range(2):
            start = (2 * t + half) * plan.c
            at = start
            while at < start + plan.c:
                s = at // plan.share
                end = min(start + plan.c, (s + 1) * plan.share)
                low = s * plan.share
                put(t, half, slice(at - start, end - start), s, slice(at - low, end - low))
                at = end


def summed(ref, count):
    out = ref[0].astype(F32)
    for i in range(1, count):
        out += ref[i].astype(F32)
    return out


def whole_kernel(
    plan, ext_ref, x_hbm, g_hbm, b_hbm, win_hbm, wout_hbm, gain_hbm,
    dr_out, db_out, w_all, gain_out,
    x_in, g_in, b_in, win_ref, wout_ref, gain_ref,
    xg_s, xg_y, xg_zs, xg_z, b_z, bias_ref, ds_ref, ds_y, z_out, z_in,
    dr_s, dr_y, wg, w_cin, w_p, w_pin, w_a, w_b,
    lsem, xy, xz, bf, bn, by, dy, z1, z2, ry, wc, wp, wa, wb, gp, gc,
):
    y, z = place(plan)
    crop = lax.axis_index("crop")
    cx, core = crop // 2, crop % 2
    ny, nz, nx, blk, qa, qb = plan.ny, plan.nz, plan.nx, plan.blk, plan.qa, plan.qb
    za, zb = z // qb, z % qb
    n, ch, msg = plan.n, plan.c, plan.msg
    share, extra, plane = plan.share, plan.extra, plan.plane
    spot = cx * ny + y

    def zpeer(i):
        step = (i + 1) // 2
        zp = lax.rem(z + nz // 2 + step * (1 - 2 * (i % 2)), nz)
        return zp, {"dap": y * nz + zp}

    def ypeer(i):
        yp = lax.rem(y + i + 1, ny)
        return yp, {"dap": yp * nz + z}

    def ppeer(i):
        to = lax.rem(spot + i + 1, plane)
        return to, {"crop": (to // ny) * 2 + core, "dap": (to % ny) * nz + z}

    def apeer(i):
        return {"dap": y * nz + lax.rem(za + i + 1, qa) * qb + zb}

    def bpeer(i):
        return {"dap": y * nz + za * qb + lax.rem(zb + i + 1, qb)}

    def xpeer(i):
        xp = lax.rem(cx + i // ny + 1, nx)
        return {"crop": xp * 2 + core, "dap": (i % ny) * nz + z}

    other = {"crop": cx * 2 + 1 - core}

    local = [
        pltpu.make_async_copy(s, d, lsem.at[i])
        for i, (s, d) in enumerate(
            [
                (b_hbm, b_in), (x_hbm, x_in), (g_hbm, g_in),
                (win_hbm, win_ref), (wout_hbm, wout_ref), (gain_hbm, gain_ref),
            ]
        )
    ]
    for c in local:
        c.start()
    for i in range(nz - 1):
        signal(zpeer(i)[1])
    for i in range(ny - 1):
        signal(ypeer(i)[1])
    for i in range(plane - ny):
        signal(xpeer(i))
    signal(other)
    for c in local[:3]:
        c.wait()
    b_z[:, za, zb] = b_in[...].reshape(plan.chunks, msg, n)
    xg_s[0] = x_in[...].reshape(ny, blk, ch)
    xg_s[1] = g_in[...].reshape(ny, blk, ch)
    to_y = swap_matrix(plan, False)
    to_z = swap_matrix(plan, True)
    pl.semaphore_wait(pltpu.get_barrier_semaphore(), nz + plane - 1)

    def b_far(i):
        part = b_z.at[:, za, zb]
        return part, part, apeer(i)

    def b_near(i):
        part = b_z.at[:, :, zb]
        return part, part, bpeer(i)

    mine = pl.ds(pl.multiple_of(y * blk, blk), blk)

    def bias_y(c):
        heads = pl.ds(c * ny, ny)

        def b_y(i):
            part = bias_ref.at[heads, mine]
            return part, part, ypeer(i)[1]

        return Exchange(b_y, ny - 1, bias_ref.at[heads, pl.ds(0, (ny - 1) * blk)], by.at[c])

    def x_y(i):
        yp, peer = ypeer(i)
        return xg_s.at[:, yp], xg_y.at[:, y], peer

    def x_z(i):
        zp, peer = zpeer(i)
        return xg_zs.at[:, zp], xg_z.at[:, z], peer

    far = Exchange(b_far, qa - 1, b_z.at[:, pl.ds(0, qa - 1), 0], bf)
    near = Exchange(b_near, qb - 1, b_z.at[:, :, pl.ds(0, qb - 1)], bn)
    by_y = [bias_y(c) for c in range(plan.chunks)]
    rows_y = Exchange(x_y, ny - 1, xg_y.at[:, pl.ds(0, ny - 1)], xy)
    rows_z = Exchange(x_z, nz - 1, xg_z.at[:, pl.ds(0, nz - 1)], xz)

    far.start()
    rows_y.start()
    xg_y[:, y] = xg_s[:, y]
    far.received()
    near.start()
    rows_y.received()
    for t in range(2):
        rows = nn(to_z, xg_y[t].reshape(plan.tile, ch)).astype(BF)
        xg_zs[t] = rows.reshape(nz, msg, ch)
    xg_z[:, z] = xg_zs[:, z]
    rows_z.start()
    near.received()
    for c in range(plan.chunks):
        rows = nn(to_y, b_z[c].reshape(plan.tile, n)).astype(BF)
        bias_ref[pl.ds(c * ny, ny), mine] = rows.reshape(ny, blk, n)
        by_y[c].start()
    for c in local[3:]:
        c.wait()
    rows_z.received()

    size = ch // plan.heads
    mult = 1.0 / math.sqrt(size)
    extent = ext_ref[0]
    gain = gain_ref[...]
    value = nn(to_y, xg_z[0].reshape(plan.tile, ch))
    upstream = nn(to_y, xg_z[1].reshape(plan.tile, ch))
    centred = value - jnp.mean(value, axis=-1, keepdims=True)
    inv_std = lax.rsqrt(jnp.mean(centred * centred, axis=-1, keepdims=True) + EPSILON)
    normal = centred * inv_std
    normed = (normal * gain).astype(BF)
    q, k, v, gl = [nn(normed, win_ref[p]).astype(BF) for p in range(4)]
    gate = jax.nn.sigmoid(gl.astype(F32))
    row_valid = lax.broadcasted_iota(jnp.int32, (n, ch), 0) < extent
    mg = jnp.where(row_valid, upstream, 0.0).astype(BF)
    d_gated = nt(mg, wout_ref[...])
    da = (d_gated * gate).astype(BF)
    col_valid = lax.broadcasted_iota(jnp.int32, (n, n), 1) < extent
    head_of = lax.broadcasted_iota(jnp.int32, (1, ch), 1) // size
    att = dv = dq = dk = jnp.zeros((n, ch), F32)

    def scores_y(c):
        def ds_y_(i):
            yp, peer = ypeer(i)
            return ds_ref.at[pl.ds(c * ny, ny), yp], ds_y.at[c, i], peer

        return Exchange(ds_y_, ny - 1, ds_y.at[c], dy.at[c])

    ds_by_y = [scores_y(c) for c in range(plan.chunks)]
    for h in range(plan.heads):
        if h % ny == 0:
            by_y[h // ny].received()
        own = jnp.where(head_of == h, 1.0, 0.0).astype(BF)
        qh, kh, vh, dah = q * own, k * own, v * own, da * own
        scores = nt(qh, k) * mult + bias_ref[h].astype(F32)
        scores = jnp.where(col_valid, scores, MASKED)
        expo = jnp.exp(scores - jnp.max(scores, axis=-1, keepdims=True))
        probs = expo * (1.0 / jnp.sum(expo, axis=-1, keepdims=True))
        pb = probs.astype(BF)
        d_probs = nt(dah, v)
        total = jnp.sum(probs * d_probs, axis=-1, keepdims=True)
        dsb = (probs * (d_probs - total)).astype(BF)
        ds_ref[h] = dsb.reshape(ny, blk, n)
        att += nn(pb, vh)
        dv += tn(pb, dah)
        dq += nn(dsb, kh)
        dk += tn(dsb, qh)
        if h % ny == ny - 1 and h < plan.heads - 1:
            ds_by_y[h // ny].start()
    gated = (att * gate).astype(BF)
    grads = [
        (dq * mult).astype(BF),
        (dk * mult).astype(BF),
        dv.astype(BF),
        (d_gated * att * gate * (1.0 - gate)).astype(BF),
    ]
    d_normed = jnp.zeros((n, ch), F32)
    for p in range(4):
        d_normed += nt(grads[p], win_ref[p])
    terms = [tn(normed, grads[p]).astype(BF) for p in range(4)] + [tn(gated, mg).astype(BF)]

    def put(t, half, rows, s, at):
        wg[s // plane, s % plane, at] = terms[t][rows, half * LANES : (half + 1) * LANES]

    keep(plan, put)
    d_gain = jnp.sum(d_normed * normal, axis=0, keepdims=True)
    line = lax.broadcasted_iota(jnp.int32, (extra, LANES), 0)
    lo = jnp.broadcast_to(d_gain[:, :LANES], (extra, LANES))
    hi = jnp.broadcast_to(d_gain[:, LANES:], (extra, LANES))
    block = jnp.where(line == 0, lo, jnp.where(line == 1, hi, 0.0)).astype(BF)
    for core_of in range(2):
        wg[core_of, :, share:] = jnp.broadcast_to(block[None], (plane, extra, LANES))

    def w_c(i):
        return wg.at[1 - core], w_cin, other

    def w_plane(i):
        to, peer = ppeer(i)
        return w_p.at[to], w_pin.at[spot], peer

    def w_near(i):
        return w_a.at[zb], w_a.at[zb], bpeer(i)

    def w_far(i):
        return w_b.at[za], w_b.at[za], apeer(i)

    def g_plane(i):
        part = w_all.at[core, spot]
        return part, part, ppeer(i)[1]

    def g_core(i):
        return w_all.at[core], w_all.at[core], other

    by_core = Exchange(w_c, 1, w_cin, wc)
    by_plane = Exchange(w_plane, plane - 1, w_pin.at[pl.ds(0, plane - 1)], wp)
    by_near = Exchange(w_near, qb - 1, w_a.at[pl.ds(0, qb - 1)], wa)
    by_far = Exchange(w_far, qa - 1, w_b.at[pl.ds(0, qa - 1)], wb)
    to_plane = Exchange(g_plane, plane - 1, w_all.at[0, pl.ds(0, plane - 1)], gp)
    to_core = Exchange(g_core, 1, w_all.at[0], gc)

    def dr_y_(i):
        yp, peer = ypeer(i)
        return dr_s.at[yp], dr_y.at[y], peer

    def first_z(i):
        zp, peer = zpeer(i)
        return z_out.at[zp, pl.ds(0, half)], z_in.at[z, pl.ds(0, half)], peer

    def last_z(i):
        zp, peer = zpeer(i)
        part = pl.ds(half, plan.chunks + 1 - half)
        return z_out.at[zp, part], z_in.at[z, part], peer

    half = plan.chunks // 2
    others = pl.ds(0, nz - 1)
    dr_by_y = Exchange(dr_y_, ny - 1, dr_y.at[pl.ds(0, ny - 1)], ry)
    z_first = Exchange(first_z, nz - 1, z_in.at[others, pl.ds(0, half)], z1)
    z_last = Exchange(last_z, nz - 1, z_in.at[others, pl.ds(half, plan.chunks + 1 - half)], z2)

    def fold(c):
        ds_by_y[c].received()
        total = ds_ref[pl.ds(c * ny, ny), y].astype(F32)
        for i in range(ny - 1):
            total += ds_y[c, i].astype(F32)
        rows = nn(to_z, total.astype(BF).reshape(plan.tile, n)).astype(BF)
        z_out[:, c] = rows.reshape(nz, msg, n)

    by_core.start()
    ds_by_y[-1].start()
    scaled = d_normed * gain
    d_row = inv_std * (
        scaled
        - jnp.mean(scaled, axis=-1, keepdims=True)
        - normal * jnp.mean(scaled * normal, axis=-1, keepdims=True)
    )
    dr_s[...] = d_row.astype(BF).reshape(ny, blk, ch)
    dr_by_y.start()
    dr_y[y] = dr_s[y]

    by_core.received()
    w_p[...] = (wg[core].astype(F32) + w_cin[...].astype(F32)).astype(BF)
    by_plane.start()
    w_pin[spot] = w_p[spot]
    for c in range(half):
        fold(c)
    z_first.start()
    for c in range(half, plan.chunks):
        fold(c)
    dr_by_y.received()
    rows = nn(to_z, dr_y[...].reshape(plan.tile, ch)).astype(BF)
    z_out[:, plan.chunks] = rows.reshape(nz, msg, ch)
    z_in[z] = z_out[z]

    by_plane.received()
    w_a[zb] = summed(w_pin, plane).astype(BF)
    by_near.start()
    by_near.received()
    w_b[za] = summed(w_a, qb).astype(BF)
    by_far.start()
    z_last.start()
    by_far.received()
    scale = 1.0 / (plan.nc * plan.dap)
    total = summed(w_b, qa)
    w_all[core, spot] = total[:share].astype(BF)
    to_plane.start()
    gain_out[...] = total[share:] * scale
    z_first.received()
    z_last.received()
    for c in range(plan.chunks):
        total = z_in[0, c].astype(F32)
        for i in range(1, nz):
            total += z_in[i, c].astype(F32)
        db_out[c] = total
    rows = nn(to_y, z_in[:, plan.chunks].reshape(plan.tile, ch)).astype(BF)
    dr_out[...] = rows
    to_plane.received()
    to_core.start()

    exchanges = [far, near, *by_y, rows_y, rows_z, *ds_by_y, by_core, by_plane, by_near, by_far]
    for e in exchanges + [to_plane, dr_by_y, z_first, z_last]:
        e.sent()
    to_core.received()
    to_core.sent()


def unpack_kernel(
    plan, dr_ref, db_ref, w_all, gain_ref, dr_out, db_out, win_out, wout_out, gain_out
):
    scale = 1.0 / (plan.nc * plan.dap)
    dr_out[...] = dr_ref[...].reshape(dr_out.shape)
    db_out[...] = db_ref[...].reshape(db_out.shape)
    gain_out[:, :LANES] = gain_ref[0:1]
    gain_out[:, LANES:] = gain_ref[1:2]

    def take(t, half, rows, s, at):
        part = w_all[s // plan.plane, s % plan.plane, at].astype(F32) * scale
        cols = slice(half * LANES, (half + 1) * LANES)
        if t < 4:
            win_out[t, rows, cols] = part
        else:
            wout_out[rows, cols] = part

    keep(plan, take)


def dma(*shape):
    return pltpu.SemaphoreType.DMA(shape)


def on_device(plan, x, upstream, bias, extents, w_in, w_final, gain):
    ny, nz, n, ch = plan.ny, plan.nz, plan.n, plan.c
    msg, blk, chunks, heads = plan.msg, plan.blk, plan.chunks, plan.heads
    total, plane = plan.share + plan.extra, plan.plane

    def buf(*shape, kind=BF):
        return pltpu.VMEM(shape, kind)

    sums = pl.pallas_call(
        functools.partial(whole_kernel, plan),
        out_shape=(
            jax.ShapeDtypeStruct((n, ch), BF),
            jax.ShapeDtypeStruct((chunks, msg, n), F32),
            jax.ShapeDtypeStruct((2, plane, plan.share, LANES), BF),
            jax.ShapeDtypeStruct((plan.extra, LANES), F32),
        ),
        in_specs=[SMEM] + [ANY] * 6,
        out_specs=(VMEM,) * 4,
        scratch_shapes=[
            buf(plan.dap, plan.own, ch),
            buf(plan.dap, plan.own, ch),
            buf(heads, plan.own, n),
            buf(4, ch, ch),
            buf(ch, ch),
            buf(1, ch, kind=F32),
            buf(2, ny, blk, ch),
            buf(2, ny, blk, ch),
            buf(2, nz, msg, ch),
            buf(2, nz, msg, ch),
            buf(chunks, plan.qa, plan.qb, msg, n),
            buf(heads, n, n),
            buf(heads, ny, blk, n),
            buf(chunks, ny - 1, ny, blk, n),
            buf(nz, chunks + 1, msg, n),
            buf(nz, chunks + 1, msg, n),
            buf(ny, blk, ch),
            buf(ny, blk, ch),
            buf(2, plane, total, LANES),
            buf(plane, total, LANES),
            buf(plane, total, LANES),
            buf(plane, total, LANES),
            buf(plan.qb, total, LANES),
            buf(plan.qa, total, LANES),
            dma(6),
            dma(2),
            dma(2),
            dma(2),
            dma(2),
            dma(chunks, 2),
            dma(chunks, 2),
            *[dma(2)] * 9,
        ],
        compiler_params=pltpu.CompilerParams(
            collective_id=0, has_side_effects=True, vmem_limit_bytes=LIMIT
        ),
        name="row_attention_gradients",
    )(
        extents, x[0], upstream[0], bias[0], w_in, w_final, gain.reshape(1, ch)
    )
    d_rows, d_bias, d_in, d_out, d_gain = pl.pallas_call(
        functools.partial(unpack_kernel, plan),
        out_shape=(
            jax.ShapeDtypeStruct((plan.dap, plan.own, ch), BF),
            jax.ShapeDtypeStruct((heads, plan.own, n), F32),
            jax.ShapeDtypeStruct((4, ch, ch), F32),
            jax.ShapeDtypeStruct((ch, ch), F32),
            jax.ShapeDtypeStruct((1, ch), F32),
        ),
        in_specs=[VMEM] * 4,
        out_specs=(VMEM,) * 5,
        compiler_params=pltpu.CompilerParams(vmem_limit_bytes=LIMIT),
        name="unpack_gradients",
    )(*sums)
    return (d_rows[None], d_bias[None], d_in, d_out, d_gain.reshape(ch))


def solution(mesh):
    split = P("crop", None, "dap", None)

    def whole(*arrays):
        plan = Plan(mesh, arrays[0].shape[2], arrays[0].shape[3], arrays[2].shape[1])
        return jax.shard_map(
            functools.partial(on_device, plan),
            mesh=mesh,
            in_specs=(split, split, split, P("crop"), P(), P(), P()),
            out_specs=(split, split, P(), P(), P()),
            check_vma=False,
        )(*arrays)

    return whole
```

```python
import functools
import math

import jax
import jax.numpy as jnp
from jax import lax
from jax.experimental import pallas as pl
from jax.experimental.pallas import tpu as pltpu
from jax.sharding import PartitionSpec as P

EPSILON = 1e-05
MASKED = -1000000000.0
LANES = 128
BF = jnp.bfloat16
F32 = jnp.float32
ANY = pl.BlockSpec(memory_space=pl.ANY)
VMEM = pl.BlockSpec(memory_space=pltpu.VMEM)
SMEM = pl.BlockSpec(memory_space=pltpu.SMEM)
LIMIT = 60 * 1024 * 1024


class Plan:
    def __init__(self, mesh, residues, channels, heads):
        self.nc = mesh.shape["crop"]
        self.nx = self.nc // 2
        dap = mesh.shape["dap"]
        self.ny = 4 if dap >= 16 else 2
        self.nz = dap // self.ny
        self.qb = 4 if self.nz >= 16 else 2
        self.qa = self.nz // self.qb
        self.dap = dap
        self.n = residues
        self.c = channels
        self.heads = heads
        self.own = residues // dap
        self.msg = self.ny * self.own
        self.blk = self.nz * self.own
        self.chunks = heads // self.ny
        self.tile = self.ny * self.nz * self.own
        self.cols = channels // self.ny
        self.flat = 10 * self.cols
        self.plane = self.nx * self.ny
        self.share = self.flat // (2 * self.nx)
        self.bits = 2 * self.chunks * self.own
        self.extra = 16


def nn(a, b):
    return lax.dot_general(a, b, (((1,), (0,)), ((), ())), preferred_element_type=F32)


def nt(a, b):
    return lax.dot_general(a, b, (((1,), (1,)), ((), ())), preferred_element_type=F32)


def tn(a, b):
    return lax.dot_general(a, b, (((0,), (0,)), ((), ())), preferred_element_type=F32)


def swap_matrix(plan, to_z):
    size = (plan.tile, plan.tile)
    row = lax.broadcasted_iota(jnp.int32, size, 0)
    col = lax.broadcasted_iota(jnp.int32, size, 1)
    za, az = (row, col) if to_z else (col, row)
    z, a, k = za // plan.msg, (za % plan.msg) // plan.own, za % plan.own
    return jnp.where(az == a * plan.blk + z * plan.own + k, 1.0, 0.0).astype(BF)


def place(plan):
    me = lax.axis_index("dap")
    return me // plan.nz, me % plan.nz


def signal(peer):
    pl.semaphore_signal(
        pltpu.get_barrier_semaphore(), inc=1, device_id=peer, device_id_type=pl.DeviceIdType.MESH
    )


def remote(src, dst, send, recv, peer):
    return pltpu.make_async_remote_copy(
        src_ref=src,
        dst_ref=dst,
        send_sem=send,
        recv_sem=recv,
        device_id=peer,
        device_id_type=pl.DeviceIdType.MESH,
    )


class Exchange:
    def __init__(self, make, count, like, sems):
        self.make, self.count, self.like, self.sems = make, count, like, sems

    def start(self, low=0, high=None):
        for i in range(low, self.count if high is None else high):
            src, dst, peer = self.make(i)
            remote(src, dst, self.sems.at[0], self.sems.at[1], peer).start()

    def received(self):
        pltpu.make_async_copy(self.like, self.like, self.sems.at[1]).wait()

    def sent(self):
        pltpu.make_async_copy(self.like, self.like, self.sems.at[0]).wait()


def keep(plan, start, count, put):
    at = start
    while at < start + count:
        s = at // plan.share
        end = min(start + count, (s + 1) * plan.share)
        low = s * plan.share
        put(slice(at - start, end - start), s, slice(at - low, end - low))
        at = end


def normalise(value):
    centred = value - jnp.mean(value, axis=-1, keepdims=True)
    inv_std = lax.rsqrt(jnp.mean(centred * centred, axis=-1, keepdims=True) + EPSILON)
    return centred * inv_std, inv_std


def summed(ref, count):
    out = ref[0].astype(F32)
    for i in range(1, count):
        out += ref[i].astype(F32)
    return out


def whole_kernel(
    plan, ext_ref, x_hbm, g_hbm, b_hbm, win_hbm, wout_hbm, gain_hbm,
    dr_out, db_out, w_all,
    x_in, g_in, b_in, win_ref, wout_ref, gain_ref,
    xg_s, xg_z, xg_ref, b_s, b_z, z_out, z_in, db_s, db_y,
    dn_s, dn_y, wg, w_cin, w_x, w_xin, w_a, w_b,
    lsem, xz, xy, by, bf, bn, z1, z2, dy, fy, wc, wx, wa, wb, gp, gc,
):
    y, z = place(plan)
    crop = lax.axis_index("crop")
    cx, core = crop // 2, crop % 2
    ny, nz, nx, blk, qa, qb = plan.ny, plan.nz, plan.nx, plan.blk, plan.qa, plan.qb
    za, zb = z // qb, z % qb
    n, ch, msg = plan.n, plan.c, plan.msg
    share, extra, plane = plan.share, plan.extra, plan.plane
    spot = cx * ny + y
    cols, chunks, heads = plan.cols, plan.chunks, plan.heads

    def zpeer(i):
        step = (i + 1) // 2
        zp = lax.rem(z + nz // 2 + step * (1 - 2 * (i % 2)), nz)
        return zp, {"dap": y * nz + zp}

    def ypeer(i):
        yp = lax.rem(y + i + 1, ny)
        return yp, {"dap": yp * nz + z}

    def ppeer(i):
        to = lax.rem(spot + i + 1, plane)
        return to, {"crop": (to // ny) * 2 + core, "dap": (to % ny) * nz + z}

    def apeer(i):
        return {"dap": y * nz + lax.rem(za + i + 1, qa) * qb + zb}

    def bpeer(i):
        return {"dap": y * nz + za * qb + lax.rem(zb + i + 1, qb)}

    def xpeer(i):
        xp = lax.rem(cx + i // ny + 1, nx)
        return {"crop": xp * 2 + core, "dap": (i % ny) * nz + z}

    def x_only(i):
        xp = lax.rem(cx + i + 1, nx)
        return xp, {"crop": xp * 2 + core}

    other = {"crop": cx * 2 + 1 - core}

    local = [
        pltpu.make_async_copy(s, d, lsem.at[i])
        for i, (s, d) in enumerate(
            [
                (b_hbm, b_in), (x_hbm, x_in), (g_hbm, g_in),
                (win_hbm, win_ref), (wout_hbm, wout_ref), (gain_hbm, gain_ref),
            ]
        )
    ]
    for c in local:
        c.start()
    for i in range(nz - 1):
        signal(zpeer(i)[1])
    for i in range(ny - 1):
        signal(ypeer(i)[1])
    for i in range(plane - ny):
        signal(xpeer(i))
    signal(other)
    for c in local[:3]:
        c.wait()
    xg_s[0] = x_in[...].reshape(nz, msg, ch)
    xg_s[1] = g_in[...].reshape(nz, msg, ch)
    lines = b_in[...].reshape(heads * plan.own, n)
    part = plan.chunks * plan.own
    for i in range(ny):
        for h in range(2):
            b_s[i, h * part : (h + 1) * part] = lines[
                i * part : (i + 1) * part, h * LANES : (h + 1) * LANES
            ]
    to_y = swap_matrix(plan, False)
    to_z = swap_matrix(plan, True)
    pl.semaphore_wait(pltpu.get_barrier_semaphore(), nz + plane - 1)

    def x_z(i):
        zp, peer = zpeer(i)
        return xg_s.at[:, zp], xg_z.at[:, z], peer

    def x_y(i):
        return xg_ref.at[:, mine], xg_ref.at[:, mine], ypeer(i)[1]

    def b_y(i):
        yp, peer = ypeer(i)
        return b_s.at[yp], b_z.at[za, zb, y], peer

    def b_far(i):
        return b_z.at[za, zb], b_z.at[za, zb], apeer(i)

    def b_near(i):
        return b_z.at[:, zb], b_z.at[:, zb], bpeer(i)

    mine = pl.ds(pl.multiple_of(y * blk, blk), blk)
    rows_z = Exchange(x_z, nz - 1, xg_z.at[:, pl.ds(0, nz - 1)], xz)
    rows_y = Exchange(x_y, ny - 1, xg_ref.at[:, pl.ds(0, (ny - 1) * blk)], xy)
    bias_y = Exchange(b_y, ny - 1, b_z.at[0, 0, pl.ds(0, ny - 1)], by)
    far = Exchange(b_far, qa - 1, b_z.at[pl.ds(0, qa - 1), 0], bf)
    near = Exchange(b_near, qb - 1, b_z.at[:, pl.ds(0, qb - 1)], bn)

    bias_y.start()
    rows_z.start()
    b_z[za, zb, y] = b_s[y]
    xg_z[:, z] = xg_s[:, z]
    for c in local[3:]:
        c.wait()
    source = lax.broadcasted_iota(jnp.int32, (ch, 4 * cols), 0) - y * cols
    target = lax.broadcasted_iota(jnp.int32, (ch, 4 * cols), 1)
    w_own = jnp.zeros((ch, 4 * cols), F32)
    for p in range(4):
        pick = jnp.logical_and(source == target - p * cols, target // cols == p)
        w_own += nn(win_ref[p], jnp.where(pick, 1.0, 0.0).astype(BF))
    w_own = w_own.astype(BF)
    w_last = wout_ref[pl.ds(pl.multiple_of(y * cols, cols), cols)]
    bias_y.received()
    far.start()
    rows_z.received()
    for t in range(2):
        rows = nn(to_y, xg_z[t].reshape(plan.tile, ch)).astype(BF)
        xg_ref[pl.ds(t * ny, ny), mine] = rows.reshape(ny, blk, ch)
    far.received()
    near.start()
    rows_y.start()
    near.received()
    pieces = b_z[...].reshape(plan.dap * plan.bits, LANES)
    size = (n, plan.dap * plan.bits)
    line = lax.broadcasted_iota(jnp.int32, size, 0)
    first = (line % blk) // plan.own * (ny * plan.bits) + line // blk * plan.bits
    off = lax.broadcasted_iota(jnp.int32, size, 1) - first - line % plan.own
    bias = []
    for h in range(chunks):
        sides = []
        for side in range(2):
            pick = jnp.where(off == (side * chunks + h) * plan.own, 1.0, 0.0).astype(BF)
            sides.append(nn(pick, pieces))
        bias.append(jnp.concatenate(sides, axis=1))
    rows_y.received()

    size = ch // heads
    mult = 1.0 / math.sqrt(size)
    extent = ext_ref[0]
    gain = gain_ref[...]
    row_valid = lax.broadcasted_iota(jnp.int32, (n, ch), 0) < extent
    normal, normed, mg, projected, d_gated = [], [], [], [], []
    for j in range(ny):
        normal.append(normalise(xg_ref[j].astype(F32))[0])
        normed.append((normal[j] * gain).astype(BF))
        projected.append(nn(normed[j], w_own))
        mg.append(jnp.where(row_valid, xg_ref[ny + j].astype(F32), 0.0).astype(BF))
        d_gated.append(nt(mg[j], w_last))

    def across(parts, p):
        return jnp.concatenate([a[:, p * cols : (p + 1) * cols] for a in parts], axis=1)

    q, k, v, gl = [across(projected, p).astype(BF) for p in range(4)]
    gate = jax.nn.sigmoid(gl.astype(F32))
    d_gated = across(d_gated, 0)
    da = (d_gated * gate).astype(BF)
    col_valid = lax.broadcasted_iota(jnp.int32, (n, n), 1) < extent
    group_of = lax.broadcasted_iota(jnp.int32, (1, ch), 1) // size
    att = dv = dq = dk = jnp.zeros((n, ch), F32)
    d_bias = [jnp.zeros((n, n), F32)] * chunks

    def first_z(i):
        zp, peer = zpeer(i)
        part = pl.ds(0, chunks)
        return z_out.at[zp, part], z_in.at[z, part], peer

    def last_z(i):
        zp, peer = zpeer(i)
        return z_out.at[zp, chunks], z_in.at[z, chunks], peer

    others = pl.ds(0, nz - 1)
    z_first = Exchange(first_z, nz - 1, z_in.at[others, pl.ds(0, chunks)], z1)
    z_last = Exchange(last_z, nz - 1, z_in.at[others, chunks], z2)

    for h in range(chunks):
        for j in range(ny):
            own = jnp.where(group_of == j * chunks + h, 1.0, 0.0).astype(BF)
            qh, kh, vh, dah = q * own, k * own, v * own, da * own
            scores = nt(qh, k) * mult + bias[h]
            scores = jnp.where(col_valid, scores, MASKED)
            expo = jnp.exp(scores - jnp.max(scores, axis=-1, keepdims=True))
            probs = expo * (1.0 / jnp.sum(expo, axis=-1, keepdims=True))
            pb = probs.astype(BF)
            d_probs = nt(dah, v)
            total = jnp.sum(probs * d_probs, axis=-1, keepdims=True)
            d_scores = probs * (d_probs - total)
            dsb = d_scores.astype(BF)
            d_bias[h] += d_scores
            att += nn(pb, vh)
            dv += tn(pb, dah)
            dq += nn(dsb, kh)
            dk += tn(dsb, qh)
        z_out[:, h] = nn(to_z, d_bias[h].astype(BF)).astype(BF).reshape(nz, msg, n)
    z_first.start()
    gated = (att * gate).astype(BF)
    grads = [dq * mult, dk * mult, dv, d_gated * att * gate * (1.0 - gate)]
    packed = [across(grads, j).astype(BF) for j in range(ny)]
    d_in = jnp.zeros((ch, 4 * cols), F32)
    d_last = jnp.zeros((cols, ch), F32)
    d_gain = jnp.zeros((1, ch), F32)
    for j in range(ny):
        d_in += tn(normed[j], packed[j])
        d_last += tn(gated[:, j * cols : (j + 1) * cols], mg[j])
        d_normed = nt(packed[j], w_own)
        d_gain += jnp.sum(d_normed * normal[j], axis=0, keepdims=True)
        dn_s[j] = d_normed.astype(BF).reshape(ny, blk, ch)

    at = 0
    for term, lanes in ((d_in, 4 * cols), (d_last, ch)):
        term = term.astype(BF)
        for side in range(lanes // LANES):
            piece = term[:, side * LANES : (side + 1) * LANES]

            def put(rows, s, to, piece=piece):
                wg[s // nx, s % nx, to] = piece[rows]

            keep(plan, at, piece.shape[0], put)
            at += piece.shape[0]
    line = lax.broadcasted_iota(jnp.int32, (extra, LANES), 0)
    lo = jnp.broadcast_to(d_gain[:, :LANES], (extra, LANES))
    hi = jnp.broadcast_to(d_gain[:, LANES:], (extra, LANES))
    block = jnp.where(line == 0, lo, jnp.where(line == 1, hi, 0.0)).astype(BF)
    for core_of in range(2):
        wg[core_of, :, share:] = jnp.broadcast_to(block[None], (nx, extra, LANES))

    def w_c(i):
        return wg.at[1 - core], w_cin, other

    def w_across(i):
        to, peer = x_only(i)
        return w_x.at[to], w_xin.at[cx], peer

    def w_near(i):
        return w_a.at[zb], w_a.at[zb], bpeer(i)

    def w_far(i):
        return w_b.at[za], w_b.at[za], apeer(i)

    def g_plane(i):
        part = w_all.at[core, spot]
        return part, part, ppeer(i)[1]

    def g_core(i):
        return w_all.at[core], w_all.at[core], other

    by_core = Exchange(w_c, 1, w_cin, wc)
    by_x = Exchange(w_across, nx - 1, w_xin.at[pl.ds(0, nx - 1)], wx)
    by_near = Exchange(w_near, qb - 1, w_a.at[pl.ds(0, qb - 1)], wa)
    by_far = Exchange(w_far, qa - 1, w_b.at[pl.ds(0, qa - 1)], wb)
    to_plane = Exchange(g_plane, plane - 1, w_all.at[0, pl.ds(0, plane - 1)], gp)
    to_core = Exchange(g_core, 1, w_all.at[0], gc)

    def dn_y_(i):
        yp, peer = ypeer(i)
        return dn_s.at[:, yp], dn_y.at[i], peer

    def db_y_(i):
        yp, peer = ypeer(i)
        return db_s.at[yp], db_y.at[y], peer

    dn_by_y = Exchange(dn_y_, ny - 1, dn_y, dy)
    db_by_y = Exchange(db_y_, ny - 1, db_y.at[pl.ds(0, ny - 1)], fy)

    by_core.start()
    dn_by_y.start()
    by_core.received()
    w_x[...] = (wg[core].astype(F32) + w_cin[...].astype(F32)).astype(BF)
    by_x.start()
    w_xin[cx] = w_x[cx]
    by_x.received()
    w_a[zb] = summed(w_xin, nx).astype(BF)
    by_near.start()

    dn_by_y.received()
    total = dn_s[:, y].astype(F32)
    for i in range(ny - 1):
        total += dn_y[i].astype(F32)
    total = total.reshape(plan.tile, ch)
    own_x, inv_std = normalise(xg_ref[pl.ds(0, ny), mine].astype(F32).reshape(plan.tile, ch))
    scaled = total * gain
    d_row = inv_std * (
        scaled
        - jnp.mean(scaled, axis=-1, keepdims=True)
        - own_x * jnp.mean(scaled * own_x, axis=-1, keepdims=True)
    )
    z_out[:, chunks] = nn(to_z, d_row.astype(BF)).astype(BF).reshape(nz, msg, ch)

    by_near.received()
    w_b[za] = summed(w_a, qb).astype(BF)
    by_far.start()
    z_last.start()
    z_in[z] = z_out[z]
    z_first.received()
    total = z_in[0, pl.ds(0, chunks)].astype(F32)
    for i in range(1, nz):
        total += z_in[i, pl.ds(0, chunks)].astype(F32)
    for i in range(ny):
        for h in range(chunks):
            to = slice(h * plan.own, (h + 1) * plan.own)
            db_s[i, to] = total[h, i * plan.own : (i + 1) * plan.own]
    db_by_y.start()
    db_y[y] = db_s[y]
    by_far.received()
    w_all[core, spot] = summed(w_b, qa).astype(BF)
    to_plane.start()
    db_by_y.received()
    db_out[...] = db_y[...]
    z_last.received()
    dr_out[...] = z_in[:, chunks].reshape(n, ch)
    to_plane.received()
    to_core.start()

    exchanges = [rows_z, rows_y, bias_y, far, near, by_core, by_x, by_near, by_far]
    for e in exchanges + [to_plane, dn_by_y, db_by_y, z_first, z_last]:
        e.sent()
    to_core.received()
    to_core.sent()


def unpack_kernel(plan, dr_ref, db_ref, w_all, dr_out, db_out, win_out, wout_out, gain_out):
    scale = 1.0 / (plan.nc * plan.dap)
    ch, cols, nx, ny, share = plan.c, plan.cols, plan.nx, plan.ny, plan.share
    dr_out[...] = dr_ref[...].reshape(dr_out.shape)
    db_out[...] = db_ref[...].reshape(db_out.shape)
    total = w_all[0, 0, share:].astype(F32)
    for y in range(1, ny):
        total += w_all[0, y, share:].astype(F32)
    gain_out[:, :LANES] = total[0:1] * scale
    gain_out[:, LANES:] = total[1:2] * scale

    def part(y, start, count):
        found = []

        def take(rows, s, at):
            found.append(w_all[s // nx, s % nx * ny + y, at].astype(F32) * scale)

        keep(plan, start, count, take)
        return jnp.concatenate(found, axis=0)

    sides = 4 * cols // LANES
    full = [
        jnp.concatenate([part(y, side * ch, ch) for side in range(sides)], axis=1)
        for y in range(ny)
    ]
    for p in range(4):
        own = slice(p * cols, (p + 1) * cols)
        win_out[p] = jnp.concatenate([a[:, own] for a in full], axis=1)
    for y in range(ny):
        low = [part(y, sides * ch + side * cols, cols) for side in range(2)]
        wout_out[y * cols : (y + 1) * cols] = jnp.concatenate(low, axis=1)


def dma(*shape):
    return pltpu.SemaphoreType.DMA(shape)


def on_device(plan, x, upstream, bias, extents, w_in, w_final, gain):
    ny, nz, n, ch = plan.ny, plan.nz, plan.n, plan.c
    msg, blk, chunks, heads = plan.msg, plan.blk, plan.chunks, plan.heads
    total, plane = plan.share + plan.extra, plan.plane

    def buf(*shape, kind=BF):
        return pltpu.VMEM(shape, kind)

    sums = pl.pallas_call(
        functools.partial(whole_kernel, plan),
        out_shape=(
            jax.ShapeDtypeStruct((n, ch), BF),
            jax.ShapeDtypeStruct((ny, chunks * plan.own, n), F32),
            jax.ShapeDtypeStruct((2, plane, total, LANES), BF),
        ),
        in_specs=[SMEM] + [ANY] * 6,
        out_specs=(VMEM,) * 3,
        scratch_shapes=[
            buf(plan.dap, plan.own, ch),
            buf(plan.dap, plan.own, ch),
            buf(heads, plan.own, n),
            buf(4, ch, ch),
            buf(ch, ch),
            buf(1, ch, kind=F32),
            buf(2, nz, msg, ch),
            buf(2, nz, msg, ch),
            buf(2 * ny, n, ch),
            buf(ny, plan.bits, LANES),
            buf(plan.qa, plan.qb, ny, plan.bits, LANES),
            buf(nz, chunks + 1, msg, n),
            buf(nz, chunks + 1, msg, n),
            buf(ny, chunks * plan.own, n, kind=F32),
            buf(ny, chunks * plan.own, n, kind=F32),
            buf(ny, ny, blk, ch),
            buf(ny - 1, ny, blk, ch),
            buf(2, plan.nx, total, LANES),
            buf(plan.nx, total, LANES),
            buf(plan.nx, total, LANES),
            buf(plan.nx, total, LANES),
            buf(plan.qb, total, LANES),
            buf(plan.qa, total, LANES),
            dma(6),
            *[dma(2)] * 15,
        ],
        compiler_params=pltpu.CompilerParams(
            collective_id=0, has_side_effects=True, vmem_limit_bytes=LIMIT
        ),
        name="row_attention_gradients",
    )(
        extents, x[0], upstream[0], bias[0], w_in, w_final, gain.reshape(1, ch)
    )
    d_rows, d_bias, d_in, d_out, d_gain = pl.pallas_call(
        functools.partial(unpack_kernel, plan),
        out_shape=(
            jax.ShapeDtypeStruct((plan.dap, plan.own, ch), BF),
            jax.ShapeDtypeStruct((heads, plan.own, n), F32),
            jax.ShapeDtypeStruct((4, ch, ch), F32),
            jax.ShapeDtypeStruct((ch, ch), F32),
            jax.ShapeDtypeStruct((1, ch), F32),
        ),
        in_specs=[VMEM] * 3,
        out_specs=(VMEM,) * 5,
        compiler_params=pltpu.CompilerParams(vmem_limit_bytes=LIMIT),
        name="unpack_gradients",
    )(*sums)
    return (d_rows[None], d_bias[None], d_in, d_out, d_gain.reshape(ch))


def solution(mesh):
    split = P("crop", None, "dap", None)

    def whole(*arrays):
        plan = Plan(mesh, arrays[0].shape[2], arrays[0].shape[3], arrays[2].shape[1])
        return jax.shard_map(
            functools.partial(on_device, plan),
            mesh=mesh,
            in_specs=(split, split, split, P("crop"), P(), P(), P()),
            out_specs=(split, split, P(), P(), P()),
            check_vma=False,
        )(*arrays)

    return whole
```

```python
import functools
import math

import jax
import jax.numpy as jnp
from jax import lax
from jax.experimental import pallas as pl
from jax.experimental.pallas import tpu as pltpu
from jax.sharding import PartitionSpec as P

EPSILON = 1e-05
MASKED = -1000000000.0
LANES = 128
BF = jnp.bfloat16
F32 = jnp.float32
ANY = pl.BlockSpec(memory_space=pl.ANY)
VMEM = pl.BlockSpec(memory_space=pltpu.VMEM)
SMEM = pl.BlockSpec(memory_space=pltpu.SMEM)
LIMIT = 60 * 1024 * 1024


class Plan:
    def __init__(self, mesh, residues, channels, heads):
        self.nc = mesh.shape["crop"]
        self.nx = self.nc // 2
        dap = mesh.shape["dap"]
        self.ny = 4 if dap >= 16 else 2
        self.nz = dap // self.ny
        self.qb = 4 if self.nz >= 16 else 2
        self.qa = self.nz // self.qb
        self.dap = dap
        self.n = residues
        self.c = channels
        self.heads = heads
        self.own = residues // dap
        self.msg = self.ny * self.own
        self.blk = self.nz * self.own
        self.chunks = heads // self.ny
        self.tile = self.ny * self.nz * self.own
        self.cols = channels // self.ny
        self.flat = 10 * self.cols
        self.plane = self.nx * self.ny
        self.share = self.flat // (2 * self.nx)
        self.bits = 2 * self.chunks * self.own
        self.extra = 16


def nn(a, b):
    return lax.dot_general(a, b, (((1,), (0,)), ((), ())), preferred_element_type=F32)


def nt(a, b):
    return lax.dot_general(a, b, (((1,), (1,)), ((), ())), preferred_element_type=F32)


def tn(a, b):
    return lax.dot_general(a, b, (((0,), (0,)), ((), ())), preferred_element_type=F32)


def swap_matrix(plan, to_z):
    size = (plan.tile, plan.tile)
    row = lax.broadcasted_iota(jnp.int32, size, 0)
    col = lax.broadcasted_iota(jnp.int32, size, 1)
    za, az = (row, col) if to_z else (col, row)
    z, a, k = za // plan.msg, (za % plan.msg) // plan.own, za % plan.own
    return jnp.where(az == a * plan.blk + z * plan.own + k, 1.0, 0.0).astype(BF)


def place(plan):
    me = lax.axis_index("dap")
    return me // plan.nz, me % plan.nz


def signal(peer):
    pl.semaphore_signal(
        pltpu.get_barrier_semaphore(), inc=1, device_id=peer, device_id_type=pl.DeviceIdType.MESH
    )


def remote(src, dst, send, recv, peer):
    return pltpu.make_async_remote_copy(
        src_ref=src,
        dst_ref=dst,
        send_sem=send,
        recv_sem=recv,
        device_id=peer,
        device_id_type=pl.DeviceIdType.MESH,
    )


class Exchange:
    def __init__(self, make, count, like, sems):
        self.make, self.count, self.like, self.sems = make, count, like, sems

    def start(self, low=0, high=None):
        for i in range(low, self.count if high is None else high):
            src, dst, peer = self.make(i)
            remote(src, dst, self.sems.at[0], self.sems.at[1], peer).start()

    def received(self):
        pltpu.make_async_copy(self.like, self.like, self.sems.at[1]).wait()

    def sent(self):
        pltpu.make_async_copy(self.like, self.like, self.sems.at[0]).wait()


def keep(plan, start, count, put):
    at = start
    while at < start + count:
        s = at // plan.share
        end = min(start + count, (s + 1) * plan.share)
        low = s * plan.share
        put(slice(at - start, end - start), s, slice(at - low, end - low))
        at = end


def normalise(value):
    centred = value - jnp.mean(value, axis=-1, keepdims=True)
    inv_std = lax.rsqrt(jnp.mean(centred * centred, axis=-1, keepdims=True) + EPSILON)
    return centred * inv_std, inv_std


def summed(ref, count):
    out = ref[0].astype(F32)
    for i in range(1, count):
        out += ref[i].astype(F32)
    return out


def whole_kernel(
    plan, ext_ref, x_hbm, g_hbm, b_hbm, win_hbm, wout_hbm, gain_hbm,
    dr_out, db_out, w_all,
    x_in, g_in, b_in, win_ref, wout_ref, gain_ref,
    xg_s, xg_z, xg_ref, b_s, b_z, z_out, z_in, db_s, db_y,
    dn_s, dn_y, wg, w_cin, w_x, w_xin, w_a, w_b,
    lsem, xz, xy, by, bf, bn, z1, z2, dy, fy, wc, wx, wa, wb, gp, gc,
):
    y, z = place(plan)
    crop = lax.axis_index("crop")
    cx, core = crop // 2, crop % 2
    ny, nz, nx, blk, qa, qb = plan.ny, plan.nz, plan.nx, plan.blk, plan.qa, plan.qb
    za, zb = z // qb, z % qb
    n, ch, msg = plan.n, plan.c, plan.msg
    share, extra, plane = plan.share, plan.extra, plan.plane
    spot = cx * ny + y
    cols, chunks, heads = plan.cols, plan.chunks, plan.heads

    def zpeer(i):
        step = (i + 1) // 2
        zp = lax.rem(z + nz // 2 + step * (1 - 2 * (i % 2)), nz)
        return zp, {"dap": y * nz + zp}

    def ypeer(i):
        yp = lax.rem(y + i + 1, ny)
        return yp, {"dap": yp * nz + z}

    def ppeer(i):
        to = lax.rem(spot + i + 1, plane)
        return to, {"crop": (to // ny) * 2 + core, "dap": (to % ny) * nz + z}

    def apeer(i):
        return {"dap": y * nz + lax.rem(za + i + 1, qa) * qb + zb}

    def bpeer(i):
        return {"dap": y * nz + za * qb + lax.rem(zb + i + 1, qb)}

    def xpeer(i):
        xp = lax.rem(cx + i // ny + 1, nx)
        return {"crop": xp * 2 + core, "dap": (i % ny) * nz + z}

    def x_only(i):
        xp = lax.rem(cx + i + 1, nx)
        return xp, {"crop": xp * 2 + core}

    other = {"crop": cx * 2 + 1 - core}

    local = [
        pltpu.make_async_copy(s, d, lsem.at[i])
        for i, (s, d) in enumerate(
            [
                (b_hbm, b_in), (x_hbm, x_in), (g_hbm, g_in),
                (win_hbm, win_ref), (wout_hbm, wout_ref), (gain_hbm, gain_ref),
            ]
        )
    ]
    for c in local:
        c.start()
    for i in range(nz - 1):
        signal(zpeer(i)[1])
    for i in range(ny - 1):
        signal(ypeer(i)[1])
    for i in range(plane - ny):
        signal(xpeer(i))
    signal(other)
    for c in local[:3]:
        c.wait()
    xg_s[0] = x_in[...].reshape(nz, msg, ch)
    xg_s[1] = g_in[...].reshape(nz, msg, ch)
    lines = b_in[...].reshape(heads * plan.own, n)
    part = plan.chunks * plan.own
    for i in range(ny):
        for h in range(2):
            b_s[i, h * part : (h + 1) * part] = lines[
                i * part : (i + 1) * part, h * LANES : (h + 1) * LANES
            ]
    to_y = swap_matrix(plan, False)
    to_z = swap_matrix(plan, True)
    pl.semaphore_wait(pltpu.get_barrier_semaphore(), nz + plane - 1)

    def over_z(t):
        def x_z(i):
            zp, peer = zpeer(i)
            return xg_s.at[t, zp], xg_z.at[t, z], peer

        return Exchange(x_z, nz - 1, xg_z.at[t, pl.ds(0, nz - 1)], xz.at[t])

    def over_y(t):
        def x_y(i):
            part = xg_ref.at[pl.ds(t * ny, ny), mine]
            return part, part, ypeer(i)[1]

        like = xg_ref.at[pl.ds(t * ny, ny), pl.ds(0, (ny - 1) * blk)]
        return Exchange(x_y, ny - 1, like, xy.at[t])

    def b_y(i):
        yp, peer = ypeer(i)
        return b_s.at[yp], b_z.at[za, zb, y], peer

    def b_far(i):
        return b_z.at[za, zb], b_z.at[za, zb], apeer(i)

    def b_near(i):
        return b_z.at[:, zb], b_z.at[:, zb], bpeer(i)

    mine = pl.ds(pl.multiple_of(y * blk, blk), blk)
    rows_z, rows_y = [over_z(t) for t in range(2)], [over_y(t) for t in range(2)]
    bias_y = Exchange(b_y, ny - 1, b_z.at[0, 0, pl.ds(0, ny - 1)], by)
    far = Exchange(b_far, qa - 1, b_z.at[pl.ds(0, qa - 1), 0], bf)
    near = Exchange(b_near, qb - 1, b_z.at[:, pl.ds(0, qb - 1)], bn)

    bias_y.start()
    rows_z[0].start()
    rows_z[1].start()
    b_z[za, zb, y] = b_s[y]
    xg_z[:, z] = xg_s[:, z]
    for c in local[3:]:
        c.wait()
    source = lax.broadcasted_iota(jnp.int32, (ch, 4 * cols), 0) - y * cols
    target = lax.broadcasted_iota(jnp.int32, (ch, 4 * cols), 1)
    w_own = jnp.zeros((ch, 4 * cols), F32)
    for p in range(4):
        pick = jnp.logical_and(source == target - p * cols, target // cols == p)
        w_own += nn(win_ref[p], jnp.where(pick, 1.0, 0.0).astype(BF))
    w_own = w_own.astype(BF)
    w_last = wout_ref[pl.ds(pl.multiple_of(y * cols, cols), cols)]
    bias_y.received()
    far.start()

    def regroup(t):
        rows_z[t].received()
        rows = nn(to_y, xg_z[t].reshape(plan.tile, ch)).astype(BF)
        xg_ref[pl.ds(t * ny, ny), mine] = rows.reshape(ny, blk, ch)

    regroup(0)
    far.received()
    near.start()
    rows_y[0].start()
    regroup(1)
    rows_y[1].start()
    near.received()
    pieces = b_z[...].reshape(plan.dap * plan.bits, LANES)
    size = (n, plan.dap * plan.bits)
    line = lax.broadcasted_iota(jnp.int32, size, 0)
    first = (line % blk) // plan.own * (ny * plan.bits) + line // blk * plan.bits
    off = lax.broadcasted_iota(jnp.int32, size, 1) - first - line % plan.own
    bias = []
    for h in range(chunks):
        sides = []
        for side in range(2):
            pick = jnp.where(off == (side * chunks + h) * plan.own, 1.0, 0.0).astype(BF)
            sides.append(nn(pick, pieces))
        bias.append(jnp.concatenate(sides, axis=1))
    rows_y[0].received()

    size = ch // heads
    mult = 1.0 / math.sqrt(size)
    extent = ext_ref[0]
    gain = gain_ref[...]
    row_valid = lax.broadcasted_iota(jnp.int32, (n, ch), 0) < extent
    normal, normed, mg, projected, d_gated = [], [], [], [], []
    for j in range(ny):
        normal.append(normalise(xg_ref[j].astype(F32))[0])
        normed.append((normal[j] * gain).astype(BF))
        projected.append(nn(normed[j], w_own))
    rows_y[1].received()
    for j in range(ny):
        mg.append(jnp.where(row_valid, xg_ref[ny + j].astype(F32), 0.0).astype(BF))
        d_gated.append(nt(mg[j], w_last))

    def across(parts, p):
        return jnp.concatenate([a[:, p * cols : (p + 1) * cols] for a in parts], axis=1)

    q, k, v, gl = [across(projected, p).astype(BF) for p in range(4)]
    gate = jax.nn.sigmoid(gl.astype(F32))
    d_gated = across(d_gated, 0)
    da = (d_gated * gate).astype(BF)
    col_valid = lax.broadcasted_iota(jnp.int32, (n, n), 1) < extent
    group_of = lax.broadcasted_iota(jnp.int32, (1, ch), 1) // size
    att = dv = dq = dk = jnp.zeros((n, ch), F32)
    d_bias = [jnp.zeros((n, n), F32)] * chunks

    def first_z(i):
        zp, peer = zpeer(i)
        part = pl.ds(0, chunks)
        return z_out.at[zp, part], z_in.at[z, part], peer

    def last_z(i):
        zp, peer = zpeer(i)
        return z_out.at[zp, chunks], z_in.at[z, chunks], peer

    others = pl.ds(0, nz - 1)
    z_first = Exchange(first_z, nz - 1, z_in.at[others, pl.ds(0, chunks)], z1)
    z_last = Exchange(last_z, nz - 1, z_in.at[others, chunks], z2)

    for h in range(chunks):
        for j in range(ny):
            own = jnp.where(group_of == j * chunks + h, 1.0, 0.0).astype(BF)
            qh, kh, vh, dah = q * own, k * own, v * own, da * own
            scores = nt(qh, k) * mult + bias[h]
            scores = jnp.where(col_valid, scores, MASKED)
            expo = jnp.exp(scores - jnp.max(scores, axis=-1, keepdims=True))
            probs = expo * (1.0 / jnp.sum(expo, axis=-1, keepdims=True))
            pb = probs.astype(BF)
            d_probs = nt(dah, v)
            total = jnp.sum(probs * d_probs, axis=-1, keepdims=True)
            d_scores = probs * (d_probs - total)
            dsb = d_scores.astype(BF)
            d_bias[h] += d_scores
            att += nn(pb, vh)
            dv += tn(pb, dah)
            dq += nn(dsb, kh)
            dk += tn(dsb, qh)
        z_out[:, h] = nn(to_z, d_bias[h].astype(BF)).astype(BF).reshape(nz, msg, n)
    z_first.start()
    gated = (att * gate).astype(BF)
    grads = [dq * mult, dk * mult, dv, d_gated * att * gate * (1.0 - gate)]
    packed = [across(grads, j).astype(BF) for j in range(ny)]
    d_in = jnp.zeros((ch, 4 * cols), F32)
    d_last = jnp.zeros((cols, ch), F32)
    d_gain = jnp.zeros((1, ch), F32)
    for j in range(ny):
        d_in += tn(normed[j], packed[j])
        d_last += tn(gated[:, j * cols : (j + 1) * cols], mg[j])
        d_normed = nt(packed[j], w_own)
        d_gain += jnp.sum(d_normed * normal[j], axis=0, keepdims=True)
        dn_s[j] = d_normed.astype(BF).reshape(ny, blk, ch)

    at = 0
    for term, lanes in ((d_in, 4 * cols), (d_last, ch)):
        term = term.astype(BF)
        for side in range(lanes // LANES):
            piece = term[:, side * LANES : (side + 1) * LANES]

            def put(rows, s, to, piece=piece):
                wg[s // nx, s % nx, to] = piece[rows]

            keep(plan, at, piece.shape[0], put)
            at += piece.shape[0]
    line = lax.broadcasted_iota(jnp.int32, (extra, LANES), 0)
    lo = jnp.broadcast_to(d_gain[:, :LANES], (extra, LANES))
    hi = jnp.broadcast_to(d_gain[:, LANES:], (extra, LANES))
    block = jnp.where(line == 0, lo, jnp.where(line == 1, hi, 0.0)).astype(BF)
    for core_of in range(2):
        wg[core_of, :, share:] = jnp.broadcast_to(block[None], (nx, extra, LANES))

    def w_c(i):
        return wg.at[1 - core], w_cin, other

    def w_across(i):
        to, peer = x_only(i)
        return w_x.at[to], w_xin.at[cx], peer

    def w_near(i):
        return w_a.at[zb], w_a.at[zb], bpeer(i)

    def w_far(i):
        return w_b.at[za], w_b.at[za], apeer(i)

    def g_plane(i):
        part = w_all.at[core, spot]
        return part, part, ppeer(i)[1]

    def g_core(i):
        return w_all.at[core], w_all.at[core], other

    by_core = Exchange(w_c, 1, w_cin, wc)
    by_x = Exchange(w_across, nx - 1, w_xin.at[pl.ds(0, nx - 1)], wx)
    by_near = Exchange(w_near, qb - 1, w_a.at[pl.ds(0, qb - 1)], wa)
    by_far = Exchange(w_far, qa - 1, w_b.at[pl.ds(0, qa - 1)], wb)
    to_plane = Exchange(g_plane, plane - 1, w_all.at[0, pl.ds(0, plane - 1)], gp)
    to_core = Exchange(g_core, 1, w_all.at[0], gc)

    def dn_y_(i):
        yp, peer = ypeer(i)
        return dn_s.at[:, yp], dn_y.at[i], peer

    def db_y_(i):
        yp, peer = ypeer(i)
        return db_s.at[yp], db_y.at[y], peer

    dn_by_y = Exchange(dn_y_, ny - 1, dn_y, dy)
    db_by_y = Exchange(db_y_, ny - 1, db_y.at[pl.ds(0, ny - 1)], fy)

    by_core.start()
    dn_by_y.start()
    by_core.received()
    w_x[...] = (wg[core].astype(F32) + w_cin[...].astype(F32)).astype(BF)
    by_x.start()
    w_xin[cx] = w_x[cx]
    by_x.received()
    w_a[zb] = summed(w_xin, nx).astype(BF)
    by_near.start()

    dn_by_y.received()
    total = dn_s[:, y].astype(F32)
    for i in range(ny - 1):
        total += dn_y[i].astype(F32)
    total = total.reshape(plan.tile, ch)
    own_x, inv_std = normalise(xg_ref[pl.ds(0, ny), mine].astype(F32).reshape(plan.tile, ch))
    scaled = total * gain
    d_row = inv_std * (
        scaled
        - jnp.mean(scaled, axis=-1, keepdims=True)
        - own_x * jnp.mean(scaled * own_x, axis=-1, keepdims=True)
    )
    z_out[:, chunks] = nn(to_z, d_row.astype(BF)).astype(BF).reshape(nz, msg, ch)

    by_near.received()
    w_b[za] = summed(w_a, qb).astype(BF)
    by_far.start()
    z_last.start()
    z_in[z] = z_out[z]
    z_first.received()
    total = z_in[0, pl.ds(0, chunks)].astype(F32)
    for i in range(1, nz):
        total += z_in[i, pl.ds(0, chunks)].astype(F32)
    for i in range(ny):
        for h in range(chunks):
            to = slice(h * plan.own, (h + 1) * plan.own)
            db_s[i, to] = total[h, i * plan.own : (i + 1) * plan.own]
    db_by_y.start()
    db_y[y] = db_s[y]
    by_far.received()
    w_all[core, spot] = summed(w_b, qa).astype(BF)
    to_plane.start()
    db_by_y.received()
    db_out[...] = db_y[...]
    z_last.received()
    dr_out[...] = z_in[:, chunks].reshape(n, ch)
    to_plane.received()
    to_core.start()

    exchanges = [*rows_z, *rows_y, bias_y, far, near, by_core, by_x, by_near, by_far]
    for e in exchanges + [to_plane, dn_by_y, db_by_y, z_first, z_last]:
        e.sent()
    to_core.received()
    to_core.sent()


def unpack_kernel(plan, dr_ref, db_ref, w_all, dr_out, db_out, win_out, wout_out, gain_out):
    scale = 1.0 / (plan.nc * plan.dap)
    ch, cols, nx, ny, share = plan.c, plan.cols, plan.nx, plan.ny, plan.share
    dr_out[...] = dr_ref[...].reshape(dr_out.shape)
    db_out[...] = db_ref[...].reshape(db_out.shape)
    total = w_all[0, 0, share:].astype(F32)
    for y in range(1, ny):
        total += w_all[0, y, share:].astype(F32)
    gain_out[:, :LANES] = total[0:1] * scale
    gain_out[:, LANES:] = total[1:2] * scale

    def part(y, start, count):
        found = []

        def take(rows, s, at):
            found.append(w_all[s // nx, s % nx * ny + y, at].astype(F32) * scale)

        keep(plan, start, count, take)
        return jnp.concatenate(found, axis=0)

    sides = 4 * cols // LANES
    full = [
        jnp.concatenate([part(y, side * ch, ch) for side in range(sides)], axis=1)
        for y in range(ny)
    ]
    for p in range(4):
        own = slice(p * cols, (p + 1) * cols)
        win_out[p] = jnp.concatenate([a[:, own] for a in full], axis=1)
    for y in range(ny):
        low = [part(y, sides * ch + side * cols, cols) for side in range(2)]
        wout_out[y * cols : (y + 1) * cols] = jnp.concatenate(low, axis=1)


def dma(*shape):
    return pltpu.SemaphoreType.DMA(shape)


def on_device(plan, x, upstream, bias, extents, w_in, w_final, gain):
    ny, nz, n, ch = plan.ny, plan.nz, plan.n, plan.c
    msg, blk, chunks, heads = plan.msg, plan.blk, plan.chunks, plan.heads
    total, plane = plan.share + plan.extra, plan.plane

    def buf(*shape, kind=BF):
        return pltpu.VMEM(shape, kind)

    sums = pl.pallas_call(
        functools.partial(whole_kernel, plan),
        out_shape=(
            jax.ShapeDtypeStruct((n, ch), BF),
            jax.ShapeDtypeStruct((ny, chunks * plan.own, n), F32),
            jax.ShapeDtypeStruct((2, plane, total, LANES), BF),
        ),
        in_specs=[SMEM] + [ANY] * 6,
        out_specs=(VMEM,) * 3,
        scratch_shapes=[
            buf(plan.dap, plan.own, ch),
            buf(plan.dap, plan.own, ch),
            buf(heads, plan.own, n),
            buf(4, ch, ch),
            buf(ch, ch),
            buf(1, ch, kind=F32),
            buf(2, nz, msg, ch),
            buf(2, nz, msg, ch),
            buf(2 * ny, n, ch),
            buf(ny, plan.bits, LANES),
            buf(plan.qa, plan.qb, ny, plan.bits, LANES),
            buf(nz, chunks + 1, msg, n),
            buf(nz, chunks + 1, msg, n),
            buf(ny, chunks * plan.own, n, kind=F32),
            buf(ny, chunks * plan.own, n, kind=F32),
            buf(ny, ny, blk, ch),
            buf(ny - 1, ny, blk, ch),
            buf(2, plan.nx, total, LANES),
            buf(plan.nx, total, LANES),
            buf(plan.nx, total, LANES),
            buf(plan.nx, total, LANES),
            buf(plan.qb, total, LANES),
            buf(plan.qa, total, LANES),
            dma(6),
            dma(2, 2),
            dma(2, 2),
            *[dma(2)] * 13,
        ],
        compiler_params=pltpu.CompilerParams(
            collective_id=0, has_side_effects=True, vmem_limit_bytes=LIMIT
        ),
        name="row_attention_gradients",
    )(
        extents, x[0], upstream[0], bias[0], w_in, w_final, gain.reshape(1, ch)
    )
    d_rows, d_bias, d_in, d_out, d_gain = pl.pallas_call(
        functools.partial(unpack_kernel, plan),
        out_shape=(
            jax.ShapeDtypeStruct((plan.dap, plan.own, ch), BF),
            jax.ShapeDtypeStruct((heads, plan.own, n), F32),
            jax.ShapeDtypeStruct((4, ch, ch), F32),
            jax.ShapeDtypeStruct((ch, ch), F32),
            jax.ShapeDtypeStruct((1, ch), F32),
        ),
        in_specs=[VMEM] * 3,
        out_specs=(VMEM,) * 5,
        compiler_params=pltpu.CompilerParams(vmem_limit_bytes=LIMIT),
        name="unpack_gradients",
    )(*sums)
    return (d_rows[None], d_bias[None], d_in, d_out, d_gain.reshape(ch))


def solution(mesh):
    split = P("crop", None, "dap", None)

    def whole(*arrays):
        plan = Plan(mesh, arrays[0].shape[2], arrays[0].shape[3], arrays[2].shape[1])
        return jax.shard_map(
            functools.partial(on_device, plan),
            mesh=mesh,
            in_specs=(split, split, split, P("crop"), P(), P(), P()),
            out_specs=(split, split, P(), P(), P()),
            check_vma=False,
        )(*arrays)

    return whole
```

```python
import functools
import math

import jax
import jax.numpy as jnp
from jax import lax
from jax.experimental import pallas as pl
from jax.experimental.pallas import tpu as pltpu
from jax.sharding import PartitionSpec as P

EPSILON = 1e-05
MASKED = -1000000000.0
LANES = 128
BF = jnp.bfloat16
F32 = jnp.float32
ANY = pl.BlockSpec(memory_space=pl.ANY)
VMEM = pl.BlockSpec(memory_space=pltpu.VMEM)
SMEM = pl.BlockSpec(memory_space=pltpu.SMEM)
LIMIT = 60 * 1024 * 1024


class Plan:
    def __init__(self, mesh, residues, channels, heads):
        self.nc = mesh.shape["crop"]
        self.nx = self.nc // 2
        dap = mesh.shape["dap"]
        self.ny = 4 if dap >= 16 else 2
        self.nz = dap // self.ny
        self.qb = 4 if self.nz >= 16 else 2
        self.qa = self.nz // self.qb
        self.dap = dap
        self.n = residues
        self.c = channels
        self.heads = heads
        self.own = residues // dap
        self.msg = self.ny * self.own
        self.blk = self.nz * self.own
        self.chunks = heads // self.ny
        self.tile = self.ny * self.nz * self.own
        self.cols = channels // self.ny
        self.flat = 10 * self.cols
        self.plane = self.nx * self.ny
        self.share = self.flat // (2 * self.nx)
        self.bits = 2 * self.chunks * self.own
        self.extra = 16


def nn(a, b):
    return lax.dot_general(a, b, (((1,), (0,)), ((), ())), preferred_element_type=F32)


def nt(a, b):
    return lax.dot_general(a, b, (((1,), (1,)), ((), ())), preferred_element_type=F32)


def tn(a, b):
    return lax.dot_general(a, b, (((0,), (0,)), ((), ())), preferred_element_type=F32)


def swap_matrix(plan, to_z):
    size = (plan.tile, plan.tile)
    row = lax.broadcasted_iota(jnp.int32, size, 0)
    col = lax.broadcasted_iota(jnp.int32, size, 1)
    za, az = (row, col) if to_z else (col, row)
    z, a, k = za // plan.msg, (za % plan.msg) // plan.own, za % plan.own
    return jnp.where(az == a * plan.blk + z * plan.own + k, 1.0, 0.0).astype(BF)


def place(plan):
    me = lax.axis_index("dap")
    return me // plan.nz, me % plan.nz


def signal(peer):
    pl.semaphore_signal(
        pltpu.get_barrier_semaphore(), inc=1, device_id=peer, device_id_type=pl.DeviceIdType.MESH
    )


def remote(src, dst, send, recv, peer):
    return pltpu.make_async_remote_copy(
        src_ref=src,
        dst_ref=dst,
        send_sem=send,
        recv_sem=recv,
        device_id=peer,
        device_id_type=pl.DeviceIdType.MESH,
    )


class Exchange:
    def __init__(self, make, count, like, sems):
        self.make, self.count, self.like, self.sems = make, count, like, sems

    def start(self, low=0, high=None):
        for i in range(low, self.count if high is None else high):
            src, dst, peer = self.make(i)
            remote(src, dst, self.sems.at[0], self.sems.at[1], peer).start()

    def received(self):
        pltpu.make_async_copy(self.like, self.like, self.sems.at[1]).wait()

    def sent(self):
        pltpu.make_async_copy(self.like, self.like, self.sems.at[0]).wait()


def keep(plan, start, count, put):
    at = start
    while at < start + count:
        s = at // plan.share
        end = min(start + count, (s + 1) * plan.share)
        low = s * plan.share
        put(slice(at - start, end - start), s, slice(at - low, end - low))
        at = end


def normalise(value):
    centred = value - jnp.mean(value, axis=-1, keepdims=True)
    inv_std = lax.rsqrt(jnp.mean(centred * centred, axis=-1, keepdims=True) + EPSILON)
    return centred * inv_std, inv_std


def summed(ref, count):
    out = ref[0].astype(F32)
    for i in range(1, count):
        out += ref[i].astype(F32)
    return out


def whole_kernel(
    plan, ext_ref, x_hbm, g_hbm, b_hbm, win_hbm, wout_hbm, gain_hbm,
    dr_out, db_out, w_all,
    x_in, g_in, b_in, win_ref, wout_ref, gain_ref,
    xg_s, xg_z, xg_ref, b_s, b_z, z_out, z_in, db_s, db_y,
    dn_s, dn_y, wg, w_in, w_a, w_b,
    lsem, xz, xy, by, bf, bn, z1, z2, dy, fy, wc, wa, wb, gp, gc,
):
    y, z = place(plan)
    crop = lax.axis_index("crop")
    cx, core = crop // 2, crop % 2
    ny, nz, nx, blk, qa, qb = plan.ny, plan.nz, plan.nx, plan.blk, plan.qa, plan.qb
    za, zb = z // qb, z % qb
    n, ch, msg = plan.n, plan.c, plan.msg
    share, extra, plane = plan.share, plan.extra, plan.plane
    spot = cx * ny + y
    cols, chunks, heads = plan.cols, plan.chunks, plan.heads

    def zpeer(i):
        step = (i + 1) // 2
        zp = lax.rem(z + nz // 2 + step * (1 - 2 * (i % 2)), nz)
        return zp, {"dap": y * nz + zp}

    def ypeer(i):
        yp = lax.rem(y + i + 1, ny)
        return yp, {"dap": yp * nz + z}

    def ppeer(i):
        to = lax.rem(spot + i + 1, plane)
        return to, {"crop": (to // ny) * 2 + core, "dap": (to % ny) * nz + z}

    def apeer(i):
        return {"dap": y * nz + lax.rem(za + i + 1, qa) * qb + zb}

    def bpeer(i):
        return {"dap": y * nz + za * qb + lax.rem(zb + i + 1, qb)}

    def xpeer(i):
        xp = lax.rem(cx + i // ny + 1, nx)
        return {"crop": xp * 2 + core, "dap": (i % ny) * nz + z}

    def cpeer(i):
        to = lax.rem(crop + i + 1, plan.nc)
        return to, {"crop": to}

    other = {"crop": cx * 2 + 1 - core}

    local = [
        pltpu.make_async_copy(s, d, lsem.at[i])
        for i, (s, d) in enumerate(
            [
                (b_hbm, b_in), (x_hbm, x_in), (g_hbm, g_in),
                (win_hbm, win_ref), (wout_hbm, wout_ref), (gain_hbm, gain_ref),
            ]
        )
    ]
    for c in local:
        c.start()
    for i in range(nz - 1):
        signal(zpeer(i)[1])
    for i in range(ny - 1):
        signal(ypeer(i)[1])
    for i in range(plane - ny):
        signal(xpeer(i))
    signal(other)
    for i in range(nx - 1):
        signal({"crop": lax.rem(cx + i + 1, nx) * 2 + 1 - core})
    for c in local[:3]:
        c.wait()
    xg_s[0] = x_in[...].reshape(nz, msg, ch)
    xg_s[1] = g_in[...].reshape(nz, msg, ch)
    lines = b_in[...].reshape(heads * plan.own, n)
    part = plan.chunks * plan.own
    for i in range(ny):
        for h in range(2):
            b_s[i, h * part : (h + 1) * part] = lines[
                i * part : (i + 1) * part, h * LANES : (h + 1) * LANES
            ]
    to_y = swap_matrix(plan, False)
    to_z = swap_matrix(plan, True)
    pl.semaphore_wait(pltpu.get_barrier_semaphore(), nz + plane + nx - 2)

    def over_z(t):
        def x_z(i):
            zp, peer = zpeer(i)
            return xg_s.at[t, zp], xg_z.at[t, z], peer

        return Exchange(x_z, nz - 1, xg_z.at[t, pl.ds(0, nz - 1)], xz.at[t])

    def over_y(t):
        def x_y(i):
            part = xg_ref.at[pl.ds(t * ny, ny), mine]
            return part, part, ypeer(i)[1]

        like = xg_ref.at[pl.ds(t * ny, ny), pl.ds(0, (ny - 1) * blk)]
        return Exchange(x_y, ny - 1, like, xy.at[t])

    def b_y(i):
        yp, peer = ypeer(i)
        return b_s.at[yp], b_z.at[za, zb, y], peer

    def b_far(i):
        return b_z.at[za, zb], b_z.at[za, zb], apeer(i)

    def b_near(i):
        return b_z.at[:, zb], b_z.at[:, zb], bpeer(i)

    mine = pl.ds(pl.multiple_of(y * blk, blk), blk)
    rows_z, rows_y = [over_z(t) for t in range(2)], [over_y(t) for t in range(2)]
    bias_y = Exchange(b_y, ny - 1, b_z.at[0, 0, pl.ds(0, ny - 1)], by)
    far = Exchange(b_far, qa - 1, b_z.at[pl.ds(0, qa - 1), 0], bf)
    near = Exchange(b_near, qb - 1, b_z.at[:, pl.ds(0, qb - 1)], bn)

    bias_y.start()
    rows_z[0].start()
    rows_z[1].start()
    b_z[za, zb, y] = b_s[y]
    xg_z[:, z] = xg_s[:, z]
    for c in local[3:]:
        c.wait()
    source = lax.broadcasted_iota(jnp.int32, (ch, 4 * cols), 0) - y * cols
    target = lax.broadcasted_iota(jnp.int32, (ch, 4 * cols), 1)
    w_own = jnp.zeros((ch, 4 * cols), F32)
    for p in range(4):
        pick = jnp.logical_and(source == target - p * cols, target // cols == p)
        w_own += nn(win_ref[p], jnp.where(pick, 1.0, 0.0).astype(BF))
    w_own = w_own.astype(BF)
    w_last = wout_ref[pl.ds(pl.multiple_of(y * cols, cols), cols)]
    bias_y.received()
    far.start()

    def regroup(t):
        rows_z[t].received()
        rows = nn(to_y, xg_z[t].reshape(plan.tile, ch)).astype(BF)
        xg_ref[pl.ds(t * ny, ny), mine] = rows.reshape(ny, blk, ch)

    regroup(0)
    far.received()
    near.start()
    rows_y[0].start()
    regroup(1)
    rows_y[1].start()
    near.received()
    pieces = b_z[...].reshape(plan.dap * plan.bits, LANES)
    size = (n, plan.dap * plan.bits)
    line = lax.broadcasted_iota(jnp.int32, size, 0)
    first = (line % blk) // plan.own * (ny * plan.bits) + line // blk * plan.bits
    off = lax.broadcasted_iota(jnp.int32, size, 1) - first - line % plan.own
    bias = []
    for h in range(chunks):
        sides = []
        for side in range(2):
            pick = jnp.where(off == (side * chunks + h) * plan.own, 1.0, 0.0).astype(BF)
            sides.append(nn(pick, pieces))
        bias.append(jnp.concatenate(sides, axis=1))
    rows_y[0].received()

    size = ch // heads
    mult = 1.0 / math.sqrt(size)
    extent = ext_ref[0]
    gain = gain_ref[...]
    row_valid = lax.broadcasted_iota(jnp.int32, (n, ch), 0) < extent
    normal, normed, mg, projected, d_gated = [], [], [], [], []
    for j in range(ny):
        normal.append(normalise(xg_ref[j].astype(F32))[0])
        normed.append((normal[j] * gain).astype(BF))
        projected.append(nn(normed[j], w_own))
    rows_y[1].received()
    for j in range(ny):
        mg.append(jnp.where(row_valid, xg_ref[ny + j].astype(F32), 0.0).astype(BF))
        d_gated.append(nt(mg[j], w_last))

    def across(parts, p):
        return jnp.concatenate([a[:, p * cols : (p + 1) * cols] for a in parts], axis=1)

    q, k, v, gl = [across(projected, p).astype(BF) for p in range(4)]
    gate = jax.nn.sigmoid(gl.astype(F32))
    d_gated = across(d_gated, 0)
    da = (d_gated * gate).astype(BF)
    col_valid = lax.broadcasted_iota(jnp.int32, (n, n), 1) < extent
    group_of = lax.broadcasted_iota(jnp.int32, (1, ch), 1) // size
    att = dv = dq = dk = jnp.zeros((n, ch), F32)
    d_bias = [jnp.zeros((n, n), F32)] * chunks

    def first_z(i):
        zp, peer = zpeer(i)
        part = pl.ds(0, chunks)
        return z_out.at[zp, part], z_in.at[z, part], peer

    def last_z(i):
        zp, peer = zpeer(i)
        return z_out.at[zp, chunks], z_in.at[z, chunks], peer

    others = pl.ds(0, nz - 1)
    z_first = Exchange(first_z, nz - 1, z_in.at[others, pl.ds(0, chunks)], z1)
    z_last = Exchange(last_z, nz - 1, z_in.at[others, chunks], z2)

    for h in range(chunks):
        for j in range(ny):
            own = jnp.where(group_of == j * chunks + h, 1.0, 0.0).astype(BF)
            qh, kh, vh, dah = q * own, k * own, v * own, da * own
            scores = nt(qh, k) * mult + bias[h]
            scores = jnp.where(col_valid, scores, MASKED)
            expo = jnp.exp(scores - jnp.max(scores, axis=-1, keepdims=True))
            probs = expo * (1.0 / jnp.sum(expo, axis=-1, keepdims=True))
            pb = probs.astype(BF)
            d_probs = nt(dah, v)
            total = jnp.sum(probs * d_probs, axis=-1, keepdims=True)
            d_scores = probs * (d_probs - total)
            dsb = d_scores.astype(BF)
            d_bias[h] += d_scores
            att += nn(pb, vh)
            dv += tn(pb, dah)
            dq += nn(dsb, kh)
            dk += tn(dsb, qh)
        z_out[:, h] = nn(to_z, d_bias[h].astype(BF)).astype(BF).reshape(nz, msg, n)
    z_first.start()
    gated = (att * gate).astype(BF)
    grads = [dq * mult, dk * mult, dv, d_gated * att * gate * (1.0 - gate)]
    packed = [across(grads, j).astype(BF) for j in range(ny)]
    d_in = jnp.zeros((ch, 4 * cols), F32)
    d_last = jnp.zeros((cols, ch), F32)
    d_gain = jnp.zeros((1, ch), F32)
    for j in range(ny):
        d_in += tn(normed[j], packed[j])
        d_last += tn(gated[:, j * cols : (j + 1) * cols], mg[j])
        d_normed = nt(packed[j], w_own)
        d_gain += jnp.sum(d_normed * normal[j], axis=0, keepdims=True)
        dn_s[j] = d_normed.astype(BF).reshape(ny, blk, ch)

    at = 0
    for term, lanes in ((d_in, 4 * cols), (d_last, ch)):
        term = term.astype(BF)
        for side in range(lanes // LANES):
            piece = term[:, side * LANES : (side + 1) * LANES]

            def put(rows, s, to, piece=piece):
                wg[s // nx, s % nx, to] = piece[rows]

            keep(plan, at, piece.shape[0], put)
            at += piece.shape[0]
    line = lax.broadcasted_iota(jnp.int32, (extra, LANES), 0)
    lo = jnp.broadcast_to(d_gain[:, :LANES], (extra, LANES))
    hi = jnp.broadcast_to(d_gain[:, LANES:], (extra, LANES))
    block = jnp.where(line == 0, lo, jnp.where(line == 1, hi, 0.0)).astype(BF)
    for core_of in range(2):
        wg[core_of, :, share:] = jnp.broadcast_to(block[None], (nx, extra, LANES))

    def w_crop(i):
        to, peer = cpeer(i)
        return wg.at[to % 2, to // 2], w_in.at[crop], peer

    def w_near(i):
        return w_a.at[zb], w_a.at[zb], bpeer(i)

    def w_far(i):
        return w_b.at[za], w_b.at[za], apeer(i)

    def g_plane(i):
        part = w_all.at[core, spot]
        return part, part, ppeer(i)[1]

    def g_core(i):
        return w_all.at[core], w_all.at[core], other

    by_crop = Exchange(w_crop, plan.nc - 1, w_in.at[pl.ds(0, plan.nc - 1)], wc)
    by_near = Exchange(w_near, qb - 1, w_a.at[pl.ds(0, qb - 1)], wa)
    by_far = Exchange(w_far, qa - 1, w_b.at[pl.ds(0, qa - 1)], wb)
    to_plane = Exchange(g_plane, plane - 1, w_all.at[0, pl.ds(0, plane - 1)], gp)
    to_core = Exchange(g_core, 1, w_all.at[0], gc)

    def dn_y_(i):
        yp, peer = ypeer(i)
        return dn_s.at[:, yp], dn_y.at[i], peer

    def db_y_(i):
        yp, peer = ypeer(i)
        return db_s.at[yp], db_y.at[y], peer

    dn_by_y = Exchange(dn_y_, ny - 1, dn_y, dy)
    db_by_y = Exchange(db_y_, ny - 1, db_y.at[pl.ds(0, ny - 1)], fy)

    by_crop.start()
    dn_by_y.start()
    w_in[crop] = wg[core, cx]
    by_crop.received()
    w_a[zb] = summed(w_in, plan.nc).astype(BF)
    by_near.start()

    dn_by_y.received()
    total = dn_s[:, y].astype(F32)
    for i in range(ny - 1):
        total += dn_y[i].astype(F32)
    total = total.reshape(plan.tile, ch)
    own_x, inv_std = normalise(xg_ref[pl.ds(0, ny), mine].astype(F32).reshape(plan.tile, ch))
    scaled = total * gain
    d_row = inv_std * (
        scaled
        - jnp.mean(scaled, axis=-1, keepdims=True)
        - own_x * jnp.mean(scaled * own_x, axis=-1, keepdims=True)
    )
    z_out[:, chunks] = nn(to_z, d_row.astype(BF)).astype(BF).reshape(nz, msg, ch)

    by_near.received()
    w_b[za] = summed(w_a, qb).astype(BF)
    by_far.start()
    z_last.start()
    z_in[z] = z_out[z]
    z_first.received()
    total = z_in[0, pl.ds(0, chunks)].astype(F32)
    for i in range(1, nz):
        total += z_in[i, pl.ds(0, chunks)].astype(F32)
    for i in range(ny):
        for h in range(chunks):
            to = slice(h * plan.own, (h + 1) * plan.own)
            db_s[i, to] = total[h, i * plan.own : (i + 1) * plan.own]
    db_by_y.start()
    db_y[y] = db_s[y]
    by_far.received()
    w_all[core, spot] = summed(w_b, qa).astype(BF)
    to_plane.start()
    db_by_y.received()
    db_out[...] = db_y[...]
    z_last.received()
    dr_out[...] = z_in[:, chunks].reshape(n, ch)
    to_plane.received()
    to_core.start()

    exchanges = [*rows_z, *rows_y, bias_y, far, near, by_crop, by_near, by_far]
    for e in exchanges + [to_plane, dn_by_y, db_by_y, z_first, z_last]:
        e.sent()
    to_core.received()
    to_core.sent()


def unpack_kernel(plan, dr_ref, db_ref, w_all, dr_out, db_out, win_out, wout_out, gain_out):
    scale = 1.0 / (plan.nc * plan.dap)
    ch, cols, nx, ny, share = plan.c, plan.cols, plan.nx, plan.ny, plan.share
    dr_out[...] = dr_ref[...].reshape(dr_out.shape)
    db_out[...] = db_ref[...].reshape(db_out.shape)
    total = w_all[0, 0, share:].astype(F32)
    for y in range(1, ny):
        total += w_all[0, y, share:].astype(F32)
    gain_out[:, :LANES] = total[0:1] * scale
    gain_out[:, LANES:] = total[1:2] * scale

    def part(y, start, count):
        found = []

        def take(rows, s, at):
            found.append(w_all[s // nx, s % nx * ny + y, at].astype(F32) * scale)

        keep(plan, start, count, take)
        return jnp.concatenate(found, axis=0)

    sides = 4 * cols // LANES
    full = [
        jnp.concatenate([part(y, side * ch, ch) for side in range(sides)], axis=1)
        for y in range(ny)
    ]
    for p in range(4):
        own = slice(p * cols, (p + 1) * cols)
        win_out[p] = jnp.concatenate([a[:, own] for a in full], axis=1)
    for y in range(ny):
        low = [part(y, sides * ch + side * cols, cols) for side in range(2)]
        wout_out[y * cols : (y + 1) * cols] = jnp.concatenate(low, axis=1)


def dma(*shape):
    return pltpu.SemaphoreType.DMA(shape)


def on_device(plan, x, upstream, bias, extents, w_in, w_final, gain):
    ny, nz, n, ch = plan.ny, plan.nz, plan.n, plan.c
    msg, blk, chunks, heads = plan.msg, plan.blk, plan.chunks, plan.heads
    total, plane = plan.share + plan.extra, plan.plane

    def buf(*shape, kind=BF):
        return pltpu.VMEM(shape, kind)

    sums = pl.pallas_call(
        functools.partial(whole_kernel, plan),
        out_shape=(
            jax.ShapeDtypeStruct((n, ch), BF),
            jax.ShapeDtypeStruct((ny, chunks * plan.own, n), F32),
            jax.ShapeDtypeStruct((2, plane, total, LANES), BF),
        ),
        in_specs=[SMEM] + [ANY] * 6,
        out_specs=(VMEM,) * 3,
        scratch_shapes=[
            buf(plan.dap, plan.own, ch),
            buf(plan.dap, plan.own, ch),
            buf(heads, plan.own, n),
            buf(4, ch, ch),
            buf(ch, ch),
            buf(1, ch, kind=F32),
            buf(2, nz, msg, ch),
            buf(2, nz, msg, ch),
            buf(2 * ny, n, ch),
            buf(ny, plan.bits, LANES),
            buf(plan.qa, plan.qb, ny, plan.bits, LANES),
            buf(nz, chunks + 1, msg, n),
            buf(nz, chunks + 1, msg, n),
            buf(ny, chunks * plan.own, n, kind=F32),
            buf(ny, chunks * plan.own, n, kind=F32),
            buf(ny, ny, blk, ch),
            buf(ny - 1, ny, blk, ch),
            buf(2, plan.nx, total, LANES),
            buf(plan.nc, total, LANES),
            buf(plan.qb, total, LANES),
            buf(plan.qa, total, LANES),
            dma(6),
            dma(2, 2),
            dma(2, 2),
            *[dma(2)] * 12,
        ],
        compiler_params=pltpu.CompilerParams(
            collective_id=0, has_side_effects=True, vmem_limit_bytes=LIMIT
        ),
        name="row_attention_gradients",
    )(
        extents, x[0], upstream[0], bias[0], w_in, w_final, gain.reshape(1, ch)
    )
    d_rows, d_bias, d_in, d_out, d_gain = pl.pallas_call(
        functools.partial(unpack_kernel, plan),
        out_shape=(
            jax.ShapeDtypeStruct((plan.dap, plan.own, ch), BF),
            jax.ShapeDtypeStruct((heads, plan.own, n), F32),
            jax.ShapeDtypeStruct((4, ch, ch), F32),
            jax.ShapeDtypeStruct((ch, ch), F32),
            jax.ShapeDtypeStruct((1, ch), F32),
        ),
        in_specs=[VMEM] * 3,
        out_specs=(VMEM,) * 5,
        compiler_params=pltpu.CompilerParams(vmem_limit_bytes=LIMIT),
        name="unpack_gradients",
    )(*sums)
    return (d_rows[None], d_bias[None], d_in, d_out, d_gain.reshape(ch))


def solution(mesh):
    split = P("crop", None, "dap", None)

    def whole(*arrays):
        plan = Plan(mesh, arrays[0].shape[2], arrays[0].shape[3], arrays[2].shape[1])
        return jax.shard_map(
            functools.partial(on_device, plan),
            mesh=mesh,
            in_specs=(split, split, split, P("crop"), P(), P(), P()),
            out_specs=(split, split, P(), P(), P()),
            check_vma=False,
        )(*arrays)

    return whole
```

```python
import functools
import math

import jax
import jax.numpy as jnp
from jax import lax
from jax.experimental import pallas as pl
from jax.experimental.pallas import tpu as pltpu
from jax.sharding import PartitionSpec as P

EPSILON = 1e-05
MASKED = -1000000000.0
LANES = 128
BF = jnp.bfloat16
F32 = jnp.float32
ANY = pl.BlockSpec(memory_space=pl.ANY)
VMEM = pl.BlockSpec(memory_space=pltpu.VMEM)
SMEM = pl.BlockSpec(memory_space=pltpu.SMEM)
LIMIT = 60 * 1024 * 1024


class Plan:
    def __init__(self, mesh, residues, channels, heads):
        self.nc = mesh.shape["crop"]
        self.nx = self.nc // 2
        dap = mesh.shape["dap"]
        self.ny = 4 if dap >= 16 else 2
        self.nz = dap // self.ny
        self.qb = 4 if self.nz >= 16 else 2
        self.qa = self.nz // self.qb
        self.dap = dap
        self.n = residues
        self.c = channels
        self.heads = heads
        self.own = residues // dap
        self.msg = self.ny * self.own
        self.blk = self.nz * self.own
        self.chunks = heads // self.ny
        self.tile = self.ny * self.nz * self.own
        self.cols = channels // self.ny
        self.flat = 10 * self.cols
        self.plane = self.nx * self.ny
        self.share = self.flat // (2 * self.nx)
        self.bits = 2 * self.chunks * self.own
        self.extra = 16


def nn(a, b):
    return lax.dot_general(a, b, (((1,), (0,)), ((), ())), preferred_element_type=F32)


def nt(a, b):
    return lax.dot_general(a, b, (((1,), (1,)), ((), ())), preferred_element_type=F32)


def tn(a, b):
    return lax.dot_general(a, b, (((0,), (0,)), ((), ())), preferred_element_type=F32)


def swap_matrix(plan, to_z):
    size = (plan.tile, plan.tile)
    row = lax.broadcasted_iota(jnp.int32, size, 0)
    col = lax.broadcasted_iota(jnp.int32, size, 1)
    za, az = (row, col) if to_z else (col, row)
    z, a, k = za // plan.msg, (za % plan.msg) // plan.own, za % plan.own
    return jnp.where(az == a * plan.blk + z * plan.own + k, 1.0, 0.0).astype(BF)


def place(plan):
    me = lax.axis_index("dap")
    return me // plan.nz, me % plan.nz


def signal(peer):
    pl.semaphore_signal(
        pltpu.get_barrier_semaphore(), inc=1, device_id=peer, device_id_type=pl.DeviceIdType.MESH
    )


def remote(src, dst, send, recv, peer):
    return pltpu.make_async_remote_copy(
        src_ref=src,
        dst_ref=dst,
        send_sem=send,
        recv_sem=recv,
        device_id=peer,
        device_id_type=pl.DeviceIdType.MESH,
    )


class Exchange:
    def __init__(self, make, count, like, sems):
        self.make, self.count, self.like, self.sems = make, count, like, sems

    def start(self, low=0, high=None):
        for i in range(low, self.count if high is None else high):
            src, dst, peer = self.make(i)
            remote(src, dst, self.sems.at[0], self.sems.at[1], peer).start()

    def received(self):
        pltpu.make_async_copy(self.like, self.like, self.sems.at[1]).wait()

    def sent(self):
        pltpu.make_async_copy(self.like, self.like, self.sems.at[0]).wait()


def keep(plan, start, count, put):
    at = start
    while at < start + count:
        s = at // plan.share
        end = min(start + count, (s + 1) * plan.share)
        low = s * plan.share
        put(slice(at - start, end - start), s, slice(at - low, end - low))
        at = end


def normalise(value):
    centred = value - jnp.mean(value, axis=-1, keepdims=True)
    inv_std = lax.rsqrt(jnp.mean(centred * centred, axis=-1, keepdims=True) + EPSILON)
    return centred * inv_std, inv_std


def summed(ref, count):
    out = ref[0].astype(F32)
    for i in range(1, count):
        out += ref[i].astype(F32)
    return out


def whole_kernel(
    plan, ext_ref, x_hbm, g_hbm, b_hbm, win_hbm, wout_hbm, gain_hbm,
    dr_out, db_out, w_all,
    x_in, g_in, b_in, win_ref, wout_ref, gain_ref,
    xg_s, xg_z, xg_ref, b_s, b_z, z_out, z_in, db_s, db_y,
    dn_s, dn_y, wg, w_in, w_a, w_b,
    lsem, xz, xy, by, bf, bn, z1, z2, dy, fy, wc, wa, wb, gp, gc,
):
    y, z = place(plan)
    crop = lax.axis_index("crop")
    cx, core = crop // 2, crop % 2
    ny, nz, nx, blk, qa, qb = plan.ny, plan.nz, plan.nx, plan.blk, plan.qa, plan.qb
    za, zb = z // qb, z % qb
    n, ch, msg = plan.n, plan.c, plan.msg
    share, extra, plane = plan.share, plan.extra, plan.plane
    spot = cx * ny + y
    cols, chunks, heads = plan.cols, plan.chunks, plan.heads

    def zpeer(i):
        step = (i + 1) // 2
        zp = lax.rem(z + nz // 2 + step * (1 - 2 * (i % 2)), nz)
        return zp, {"dap": y * nz + zp}

    def ypeer(i):
        yp = lax.rem(y + i + 1, ny)
        return yp, {"dap": yp * nz + z}

    def ppeer(i):
        to = lax.rem(spot + i + 1, plane)
        return to, {"crop": (to // ny) * 2 + core, "dap": (to % ny) * nz + z}

    def apeer(i):
        return {"dap": y * nz + lax.rem(za + i + 1, qa) * qb + zb}

    def bpeer(i):
        return {"dap": y * nz + za * qb + lax.rem(zb + i + 1, qb)}

    def xpeer(i):
        xp = lax.rem(cx + i // ny + 1, nx)
        return {"crop": xp * 2 + core, "dap": (i % ny) * nz + z}

    def cpeer(i):
        to = lax.rem(crop + i + 1, plan.nc)
        return to, {"crop": to}

    other = {"crop": cx * 2 + 1 - core}

    local = [
        pltpu.make_async_copy(s, d, lsem.at[i])
        for i, (s, d) in enumerate(
            [
                (b_hbm, b_in), (x_hbm, x_in), (g_hbm, g_in),
                (win_hbm, win_ref), (wout_hbm, wout_ref), (gain_hbm, gain_ref),
            ]
        )
    ]
    for c in local:
        c.start()
    for i in range(nz - 1):
        signal(zpeer(i)[1])
    for i in range(ny - 1):
        signal(ypeer(i)[1])
    for i in range(plane - ny):
        signal(xpeer(i))
    signal(other)
    for i in range(nx - 1):
        signal({"crop": lax.rem(cx + i + 1, nx) * 2 + 1 - core})
    for c in local[:3]:
        c.wait()
    xg_s[0] = x_in[...].reshape(nz, msg, ch)
    xg_s[1] = g_in[...].reshape(nz, msg, ch)
    lines = b_in[...].reshape(heads * plan.own, n)
    part = plan.chunks * plan.own
    for i in range(ny):
        for h in range(2):
            b_s[i, h * part : (h + 1) * part] = lines[
                i * part : (i + 1) * part, h * LANES : (h + 1) * LANES
            ]
    to_y = swap_matrix(plan, False)
    to_z = swap_matrix(plan, True)
    pl.semaphore_wait(pltpu.get_barrier_semaphore(), nz + plane + nx - 2)

    def over_z(t):
        def x_z(i):
            zp, peer = zpeer(i)
            return xg_s.at[t, zp], xg_z.at[t, z], peer

        return Exchange(x_z, nz - 1, xg_z.at[t, pl.ds(0, nz - 1)], xz.at[t])

    def over_y(t):
        def x_y(i):
            part = xg_ref.at[pl.ds(t * ny, ny), mine]
            return part, part, ypeer(i)[1]

        like = xg_ref.at[pl.ds(t * ny, ny), pl.ds(0, (ny - 1) * blk)]
        return Exchange(x_y, ny - 1, like, xy.at[t])

    def b_y(i):
        yp, peer = ypeer(i)
        return b_s.at[yp], b_z.at[za, zb, y], peer

    def b_far(i):
        return b_z.at[za, zb], b_z.at[za, zb], apeer(i)

    def b_near(i):
        return b_z.at[:, zb], b_z.at[:, zb], bpeer(i)

    mine = pl.ds(pl.multiple_of(y * blk, blk), blk)
    rows_z, rows_y = [over_z(t) for t in range(2)], [over_y(t) for t in range(2)]
    bias_y = Exchange(b_y, ny - 1, b_z.at[0, 0, pl.ds(0, ny - 1)], by)
    far = Exchange(b_far, qa - 1, b_z.at[pl.ds(0, qa - 1), 0], bf)
    near = Exchange(b_near, qb - 1, b_z.at[:, pl.ds(0, qb - 1)], bn)

    bias_y.start()
    rows_z[0].start()
    rows_z[1].start()
    b_z[za, zb, y] = b_s[y]
    xg_z[:, z] = xg_s[:, z]
    for c in local[3:]:
        c.wait()
    source = lax.broadcasted_iota(jnp.int32, (ch, 4 * cols), 0) - y * cols
    target = lax.broadcasted_iota(jnp.int32, (ch, 4 * cols), 1)
    w_own = jnp.zeros((ch, 4 * cols), F32)
    for p in range(4):
        pick = jnp.logical_and(source == target - p * cols, target // cols == p)
        w_own += nn(win_ref[p], jnp.where(pick, 1.0, 0.0).astype(BF))
    w_own = w_own.astype(BF)
    w_last = wout_ref[pl.ds(pl.multiple_of(y * cols, cols), cols)]
    bias_y.received()
    far.start()

    def regroup(t):
        rows_z[t].received()
        rows = nn(to_y, xg_z[t].reshape(plan.tile, ch)).astype(BF)
        xg_ref[pl.ds(t * ny, ny), mine] = rows.reshape(ny, blk, ch)

    regroup(0)
    far.received()
    near.start()
    rows_y[0].start()
    regroup(1)
    rows_y[1].start()
    near.received()
    pieces = b_z[...].reshape(plan.dap * plan.bits, LANES)
    size = (n, plan.dap * plan.bits)
    line = lax.broadcasted_iota(jnp.int32, size, 0)
    first = (line % blk) // plan.own * (ny * plan.bits) + line // blk * plan.bits
    off = lax.broadcasted_iota(jnp.int32, size, 1) - first - line % plan.own
    bias = []
    for h in range(chunks):
        sides = []
        for side in range(2):
            pick = jnp.where(off == (side * chunks + h) * plan.own, 1.0, 0.0).astype(BF)
            sides.append(nn(pick, pieces))
        bias.append(jnp.concatenate(sides, axis=1))
    rows_y[0].received()

    size = ch // heads
    mult = 1.0 / math.sqrt(size)
    extent = ext_ref[0]
    gain = gain_ref[...]
    row_valid = lax.broadcasted_iota(jnp.int32, (n, ch), 0) < extent
    normal, normed, mg, projected, d_gated = [], [], [], [], []
    for j in range(ny):
        normal.append(normalise(xg_ref[j].astype(F32))[0])
        normed.append((normal[j] * gain).astype(BF))
        projected.append(nn(normed[j], w_own))
    rows_y[1].received()
    for j in range(ny):
        mg.append(jnp.where(row_valid, xg_ref[ny + j].astype(F32), 0.0).astype(BF))
        d_gated.append(nt(mg[j], w_last))

    def across(parts, p):
        return jnp.concatenate([a[:, p * cols : (p + 1) * cols] for a in parts], axis=1)

    q, k, v, gl = [across(projected, p).astype(BF) for p in range(4)]
    gate = jax.nn.sigmoid(gl.astype(F32))
    d_gated = across(d_gated, 0)
    da = (d_gated * gate).astype(BF)
    col_valid = lax.broadcasted_iota(jnp.int32, (n, n), 1) < extent
    group_of = lax.broadcasted_iota(jnp.int32, (1, ch), 1) // size
    att = dv = dq = dk = jnp.zeros((n, ch), F32)
    d_bias = [jnp.zeros((n, n), F32)] * chunks

    def first_z(i):
        zp, peer = zpeer(i)
        part = pl.ds(0, chunks)
        return z_out.at[zp, part], z_in.at[z, part], peer

    def last_z(i):
        zp, peer = zpeer(i)
        return z_out.at[zp, chunks], z_in.at[z, chunks], peer

    others = pl.ds(0, nz - 1)
    z_first = Exchange(first_z, nz - 1, z_in.at[others, pl.ds(0, chunks)], z1)
    z_last = Exchange(last_z, nz - 1, z_in.at[others, chunks], z2)

    for h in range(chunks):
        for j in range(ny):
            own = jnp.where(group_of == j * chunks + h, 1.0, 0.0).astype(BF)
            qh, kh, vh, dah = q * own, k * own, v * own, da * own
            scores = nt(qh, k) * mult + bias[h]
            scores = jnp.where(col_valid, scores, MASKED)
            expo = jnp.exp(scores - jnp.max(scores, axis=-1, keepdims=True))
            probs = expo * (1.0 / jnp.sum(expo, axis=-1, keepdims=True))
            pb = probs.astype(BF)
            d_probs = nt(dah, v)
            total = jnp.sum(probs * d_probs, axis=-1, keepdims=True)
            d_scores = probs * (d_probs - total)
            dsb = d_scores.astype(BF)
            d_bias[h] += d_scores
            att += nn(pb, vh)
            dv += tn(pb, dah)
            dq += nn(dsb, kh)
            dk += tn(dsb, qh)
        z_out[:, h] = nn(to_z, d_bias[h].astype(BF)).astype(BF).reshape(nz, msg, n)
    z_first.start()
    gated = (att * gate).astype(BF)
    grads = [dq * mult, dk * mult, dv, d_gated * att * gate * (1.0 - gate)]
    packed = [across(grads, j).astype(BF) for j in range(ny)]
    d_in = jnp.zeros((ch, 4 * cols), F32)
    d_last = jnp.zeros((cols, ch), F32)
    d_gain = jnp.zeros((1, ch), F32)
    for j in range(ny):
        d_in += tn(normed[j], packed[j])
        d_last += tn(gated[:, j * cols : (j + 1) * cols], mg[j])
        d_normed = nt(packed[j], w_own)
        d_gain += jnp.sum(d_normed * normal[j], axis=0, keepdims=True)
        dn_s[j] = d_normed.astype(BF).reshape(ny, blk, ch)

    at = 0
    for term, lanes in ((d_in, 4 * cols), (d_last, ch)):
        term = term.astype(BF)
        for side in range(lanes // LANES):
            piece = term[:, side * LANES : (side + 1) * LANES]

            def put(rows, s, to, piece=piece):
                wg[s // nx, s % nx, to] = piece[rows]

            keep(plan, at, piece.shape[0], put)
            at += piece.shape[0]
    line = lax.broadcasted_iota(jnp.int32, (extra, LANES), 0)
    lo = jnp.broadcast_to(d_gain[:, :LANES], (extra, LANES))
    hi = jnp.broadcast_to(d_gain[:, LANES:], (extra, LANES))
    block = jnp.where(line == 0, lo, jnp.where(line == 1, hi, 0.0)).astype(BF)
    for core_of in range(2):
        wg[core_of, :, share:] = jnp.broadcast_to(block[None], (nx, extra, LANES))

    def w_crop(i):
        to, peer = cpeer(i)
        return wg.at[to % 2, to // 2], w_in.at[crop], peer

    def w_near(i):
        return w_a.at[zb], w_a.at[zb], bpeer(i)

    def w_far(i):
        return w_b.at[za], w_b.at[za], apeer(i)

    def g_plane(i):
        part = w_all.at[core, spot]
        return part, part, ppeer(i)[1]

    def g_core(i):
        return w_all.at[core], w_all.at[core], other

    by_crop = Exchange(w_crop, plan.nc - 1, w_in.at[pl.ds(0, plan.nc - 1)], wc)
    by_near = Exchange(w_near, qb - 1, w_a.at[pl.ds(0, qb - 1)], wa)
    by_far = Exchange(w_far, qa - 1, w_b.at[pl.ds(0, qa - 1)], wb)
    to_plane = Exchange(g_plane, plane - 1, w_all.at[0, pl.ds(0, plane - 1)], gp)
    to_core = Exchange(g_core, 1, w_all.at[0], gc)

    def dn_y_(i):
        yp, peer = ypeer(i)
        return dn_s.at[:, yp], dn_y.at[i], peer

    def db_y_(i):
        yp, peer = ypeer(i)
        return db_s.at[yp], db_y.at[y], peer

    dn_by_y = Exchange(dn_y_, ny - 1, dn_y, dy)
    db_by_y = Exchange(db_y_, ny - 1, db_y.at[pl.ds(0, ny - 1)], fy)

    by_crop.start()
    dn_by_y.start()
    w_in[crop] = wg[core, cx]
    by_crop.received()
    w_a[zb] = summed(w_in, plan.nc).astype(BF)
    by_near.start()

    dn_by_y.received()
    total = dn_s[:, y].astype(F32)
    for i in range(ny - 1):
        total += dn_y[i].astype(F32)
    total = total.reshape(plan.tile, ch)
    own_x, inv_std = normalise(xg_ref[pl.ds(0, ny), mine].astype(F32).reshape(plan.tile, ch))
    scaled = total * gain
    d_row = inv_std * (
        scaled
        - jnp.mean(scaled, axis=-1, keepdims=True)
        - own_x * jnp.mean(scaled * own_x, axis=-1, keepdims=True)
    )
    z_out[:, chunks] = nn(to_z, d_row.astype(BF)).astype(BF).reshape(nz, msg, ch)

    by_near.received()
    w_b[za] = summed(w_a, qb).astype(BF)
    by_far.start()
    z_last.start()
    z_in[z] = z_out[z]
    z_first.received()
    total = z_in[0, pl.ds(0, chunks)].astype(F32)
    for i in range(1, nz):
        total += z_in[i, pl.ds(0, chunks)].astype(F32)
    for i in range(ny):
        for h in range(chunks):
            to = slice(h * plan.own, (h + 1) * plan.own)
            db_s[i, to] = total[h, i * plan.own : (i + 1) * plan.own]
    db_by_y.start()
    db_y[y] = db_s[y]
    by_far.received()
    w_all[core, spot] = summed(w_b, qa).astype(BF)
    to_plane.start()
    to_plane.received()
    to_core.start()
    db_by_y.received()
    db_out[...] = db_y[...]
    z_last.received()
    dr_out[...] = z_in[:, chunks].reshape(n, ch)

    exchanges = [*rows_z, *rows_y, bias_y, far, near, by_crop, by_near, by_far]
    for e in exchanges + [to_plane, dn_by_y, db_by_y, z_first, z_last]:
        e.sent()
    to_core.received()
    to_core.sent()


def unpack_kernel(plan, dr_ref, db_ref, w_all, dr_out, db_out, win_out, wout_out, gain_out):
    scale = 1.0 / (plan.nc * plan.dap)
    ch, cols, nx, ny, share = plan.c, plan.cols, plan.nx, plan.ny, plan.share
    dr_out[...] = dr_ref[...].reshape(dr_out.shape)
    db_out[...] = db_ref[...].reshape(db_out.shape)
    total = w_all[0, 0, share:].astype(F32)
    for y in range(1, ny):
        total += w_all[0, y, share:].astype(F32)
    gain_out[:, :LANES] = total[0:1] * scale
    gain_out[:, LANES:] = total[1:2] * scale

    def part(y, start, count):
        found = []

        def take(rows, s, at):
            found.append(w_all[s // nx, s % nx * ny + y, at].astype(F32) * scale)

        keep(plan, start, count, take)
        return jnp.concatenate(found, axis=0)

    sides = 4 * cols // LANES
    full = [
        jnp.concatenate([part(y, side * ch, ch) for side in range(sides)], axis=1)
        for y in range(ny)
    ]
    for p in range(4):
        own = slice(p * cols, (p + 1) * cols)
        win_out[p] = jnp.concatenate([a[:, own] for a in full], axis=1)
    for y in range(ny):
        low = [part(y, sides * ch + side * cols, cols) for side in range(2)]
        wout_out[y * cols : (y + 1) * cols] = jnp.concatenate(low, axis=1)


def dma(*shape):
    return pltpu.SemaphoreType.DMA(shape)


def on_device(plan, x, upstream, bias, extents, w_in, w_final, gain):
    ny, nz, n, ch = plan.ny, plan.nz, plan.n, plan.c
    msg, blk, chunks, heads = plan.msg, plan.blk, plan.chunks, plan.heads
    total, plane = plan.share + plan.extra, plan.plane

    def buf(*shape, kind=BF):
        return pltpu.VMEM(shape, kind)

    sums = pl.pallas_call(
        functools.partial(whole_kernel, plan),
        out_shape=(
            jax.ShapeDtypeStruct((n, ch), BF),
            jax.ShapeDtypeStruct((ny, chunks * plan.own, n), F32),
            jax.ShapeDtypeStruct((2, plane, total, LANES), BF),
        ),
        in_specs=[SMEM] + [ANY] * 6,
        out_specs=(VMEM,) * 3,
        scratch_shapes=[
            buf(plan.dap, plan.own, ch),
            buf(plan.dap, plan.own, ch),
            buf(heads, plan.own, n),
            buf(4, ch, ch),
            buf(ch, ch),
            buf(1, ch, kind=F32),
            buf(2, nz, msg, ch),
            buf(2, nz, msg, ch),
            buf(2 * ny, n, ch),
            buf(ny, plan.bits, LANES),
            buf(plan.qa, plan.qb, ny, plan.bits, LANES),
            buf(nz, chunks + 1, msg, n),
            buf(nz, chunks + 1, msg, n),
            buf(ny, chunks * plan.own, n, kind=F32),
            buf(ny, chunks * plan.own, n, kind=F32),
            buf(ny, ny, blk, ch),
            buf(ny - 1, ny, blk, ch),
            buf(2, plan.nx, total, LANES),
            buf(plan.nc, total, LANES),
            buf(plan.qb, total, LANES),
            buf(plan.qa, total, LANES),
            dma(6),
            dma(2, 2),
            dma(2, 2),
            *[dma(2)] * 12,
        ],
        compiler_params=pltpu.CompilerParams(
            collective_id=0, has_side_effects=True, vmem_limit_bytes=LIMIT
        ),
        name="row_attention_gradients",
    )(
        extents, x[0], upstream[0], bias[0], w_in, w_final, gain.reshape(1, ch)
    )
    d_rows, d_bias, d_in, d_out, d_gain = pl.pallas_call(
        functools.partial(unpack_kernel, plan),
        out_shape=(
            jax.ShapeDtypeStruct((plan.dap, plan.own, ch), BF),
            jax.ShapeDtypeStruct((heads, plan.own, n), F32),
            jax.ShapeDtypeStruct((4, ch, ch), F32),
            jax.ShapeDtypeStruct((ch, ch), F32),
            jax.ShapeDtypeStruct((1, ch), F32),
        ),
        in_specs=[VMEM] * 3,
        out_specs=(VMEM,) * 5,
        compiler_params=pltpu.CompilerParams(vmem_limit_bytes=LIMIT),
        name="unpack_gradients",
    )(*sums)
    return (d_rows[None], d_bias[None], d_in, d_out, d_gain.reshape(ch))


def solution(mesh):
    split = P("crop", None, "dap", None)

    def whole(*arrays):
        plan = Plan(mesh, arrays[0].shape[2], arrays[0].shape[3], arrays[2].shape[1])
        return jax.shard_map(
            functools.partial(on_device, plan),
            mesh=mesh,
            in_specs=(split, split, split, P("crop"), P(), P(), P()),
            out_specs=(split, split, P(), P(), P()),
            check_vma=False,
        )(*arrays)

    return whole
```
